256 devices in a mesh: date: 4 (over x_lo, core), az: 16 (over z, x_hi), rg: 4 (over y).
Axes of the slice: x: 4 (x_hi: 2, x_lo: 2; x = x_hi * 2 + x_lo), y: 4, z: 8, core: 2. Of those that a mesh axis runs over, the one named last changes fastest.
Arguments:
- reference_slab: bfloat16 [2, 1024, 4, 512], P(None, 'az', 'rg', 'date'), may hold values from -6 to 6
- secondary: bfloat16 [4, 2, 1024, 2048], P('date', None, 'az', 'rg'), may hold values from -6 to 6
- az_shift: int32 [4, 1024], P('date', 'az'), may hold values from -12 to 12
- az_fraction: float32 [4, 1024], P('date', 'az'), as said below
- rg_shift: int32 [4, 2048], P('date', 'rg'), may hold values from -12 to 12
- rg_fraction: float32 [4, 2048], P('date', 'rg'), as said below
Outputs:
- filtered: float32 [4, 2, 1024, 2048], P('date', None, 'az', 'rg')
The draws below stay inside these ranges and needn't reach their ends.
Inputs may be any that keep to these rules, and one draw needn't show every extreme that they name: `az_fraction`: whole multiples of 1/64, below 1. `rg_fraction`: whole multiples of 1/64, below 1.
All inputs are finite; a program needn't handle non-finite values.
Results may differ from the reference program's by a relative error of at most 0.0031.
The reference program's roundings to bfloat16 on the way count: a program that leaves them out, or rounds other values in their place, can miss the bound.
Values may be sent and summed in bfloat16 or wider, within the bound.
No kernel may reach another device: no remote copies, remote signals or barrier semaphores. Data moves between devices by JAX's collectives and lax.ppermute only.
A program may use at most 64 MiB of HBM per device.

```python
import jax
import jax.numpy as jnp
from jax import lax

COLS_DEV = 512
PATCH = 64
TAPS = 8
MAXOFF = 12
DATES = 4
LINES = 1024
SAMPLES = 2048
RG_TILES = 4


def draw_az_fraction(key, part):
    key = jax.random.fold_in(key, 11)
    return jax.random.randint(key, (DATES, LINES), 0, 64).astype(jnp.float32) / 64.0


def draw_rg_fraction(key, part):
    key = jax.random.fold_in(key, 23)
    return jax.random.randint(key, (DATES, SAMPLES), 0, 64).astype(jnp.float32) / 64.0


def touch_ends(array, stream_key, low, high):
    spot = [jax.random.randint(jax.random.fold_in(stream_key, axis), (), 0, length) for axis, length in enumerate(array.shape)]
    main_axis = array.shape.index(max(array.shape))
    beside = spot[:main_axis] + [(spot[main_axis] + 1) % array.shape[main_axis]] + spot[main_axis + 1:]
    return array.at[tuple(spot)].set(low).at[tuple(beside)].set(high)


def level_of(key, shape, pieces, low, largest):
    level, own = 1.0, jax.random.fold_in(key, 6)
    for axis_at, parts in pieces:
        heights = jnp.exp(jax.random.uniform(jax.random.fold_in(own, axis_at), (parts,), jnp.float32, low / len(pieces), largest / len(pieces)))
        level = level * jnp.repeat(heights, shape[axis_at] // parts).reshape([-1 if axis == axis_at else 1 for axis in range(len(shape))])
    return level


def scatter_about(stream_key, shape, spread, most, cuts=(), kind=jnp.bfloat16):
    entries = spread * jax.random.normal(stream_key, shape, jnp.float32)
    if cuts:
        entries = entries * level_of(stream_key, shape, cuts, -0.22, 0.18)
    return jnp.clip(entries, -most, most).astype(kind)


def setup_inputs(seed: int = 0) -> dict:
    key_list = jax.random.split(jax.random.key(seed), 7)
    return {
        "reference_slab": scatter_about(key_list[0], (2, LINES, RG_TILES, COLS_DEV), 1.0, 6.0, ((1, 16), (2, 4), (3, 4))),
        "secondary": scatter_about(key_list[1], (DATES, 2, LINES, SAMPLES), 1.0, 6.0, ((0, 4), (2, 16), (3, 4))),
        "az_shift": touch_ends(jax.random.randint(key_list[2], (DATES, LINES), 0 - MAXOFF, MAXOFF + 1), jax.random.fold_in(key_list[2], 1), 0 - MAXOFF, MAXOFF).astype(jnp.int32),
        "az_fraction": draw_az_fraction(jax.random.fold_in(key_list[6], 71), 0),
        "rg_shift": touch_ends(jax.random.randint(key_list[4], (DATES, SAMPLES), 0 - MAXOFF, MAXOFF + 1), jax.random.fold_in(key_list[4], 1), 0 - MAXOFF, MAXOFF).astype(jnp.int32),
        "rg_fraction": draw_rg_fraction(jax.random.fold_in(key_list[6], 71), 0),
    }


def sinc_weights(fraction):
    tap_offset = (jnp.arange(TAPS) - (TAPS // 2 - 1)).astype(fraction.dtype)
    distance = fraction[..., None] - tap_offset
    taper = 0.5 + 0.5 * jnp.cos(jnp.pi * distance / (TAPS // 2))
    return (jnp.sinc(distance) * taper).astype(jnp.bfloat16)

def shift_along(source, shifts, weights, axis, length):
    weight_values = weights.astype(jnp.float32)
    total = jnp.zeros(source.shape, jnp.float32)
    for tap_step in range(TAPS):
        anchor = jnp.arange(length, dtype=jnp.int32) + shifts + (tap_step - (TAPS // 2 - 1))
        inside = (anchor >= 0) & (anchor < length)
        picked = jnp.take(source, jnp.clip(anchor, 0, length - 1), axis=axis).astype(jnp.float32)
        factor = jnp.where(inside, weight_values[:, tap_step], 0.0)
        if axis == 1:
            factor = factor[None, :, None]
        else:
            factor = factor[None, None, :]
        total = total + picked * factor
    return total

def taper_table(length, float_type):
    position = jnp.arange(length).astype(float_type)
    return jnp.minimum(position + 0.5, length - 0.5 - position) / (length // 2)

def filter_band(padded, band_start):
    half_size = PATCH // 2
    strip = lax.dynamic_slice_in_dim(padded, band_start, PATCH, 0)
    blocks = strip.reshape(PATCH, SAMPLES // half_size + 2, half_size)
    patches = jnp.concatenate([blocks[:, :-1], blocks[:, 1:]], axis=2)
    patches = jnp.transpose(patches, (1, 0, 2))
    spectrum = jnp.fft.fft2(patches, axes=(1, 2))
    magnitude = jnp.abs(spectrum)
    smooth = jnp.zeros_like(magnitude)
    for row_step in (-1, 0, 1):
        for col_step in (-1, 0, 1):
            smooth = smooth + jnp.roll(magnitude, (row_step, col_step), axis=(1, 2))
    response = jnp.sqrt(smooth / 9.0)
    gain = response / (lax.optimization_barrier(jnp.mean(response, axis=(1, 2), keepdims=True)) + 1e-06)
    result = jnp.fft.ifft2(spectrum * gain, axes=(1, 2))
    taper = taper_table(PATCH, magnitude.dtype)
    result = result * (taper[:, None] * taper[None, :])
    joined = result[1:, :, :half_size] + result[:-1, :, half_size:]
    joined = jnp.transpose(joined, (1, 0, 2)).reshape(PATCH, SAMPLES)
    return jnp.stack([jnp.real(joined), jnp.imag(joined)]).astype(jnp.float32)

def goldstein(interferogram):
    half_size = PATCH // 2
    field = interferogram[0] + 1j * interferogram[1]
    padded = jnp.pad(field, half_size)
    band_starts = jnp.arange(LINES // half_size + 1, dtype=jnp.int32) * half_size
    bands = lax.map(lambda band_start: filter_band(padded, band_start), band_starts)
    joined = bands[1:, :, :half_size] + bands[:-1, :, half_size:]
    return jnp.transpose(joined, (1, 0, 2, 3)).reshape(2, LINES, SAMPLES)

def reference(reference_slab, secondary, az_shift, az_fraction, rg_shift, rg_fraction):
    master = reference_slab.reshape(2, LINES, SAMPLES).astype(jnp.float32)

    def one_date(date_items):
        date_slab, line_shift, line_fraction, sample_shift, sample_fraction = date_items
        az_rows = shift_along(date_slab, line_shift, sinc_weights(line_fraction), 1, LINES).astype(jnp.bfloat16)
        az_rows = lax.optimization_barrier(az_rows)
        resampled = shift_along(az_rows, sample_shift, sinc_weights(sample_fraction), 2, SAMPLES)
        real_part = master[0] * resampled[0] + master[1] * resampled[1]
        imag_part = master[1] * resampled[0] - master[0] * resampled[1]
        return goldstein(jnp.stack([real_part, imag_part]))
    return lax.map(one_date, (secondary, az_shift, az_fraction, rg_shift, rg_fraction))
```

```python
import functools

import jax
import jax.numpy as jnp
import ml_dtypes
import numpy as np
from jax import lax
from jax.experimental import pallas as pl
from jax.experimental.pallas import tpu as pltpu
from jax.sharding import PartitionSpec as P

PATCH = 64
HALF = 32
TAPS = 8
MARGIN = 48
LINES_DEV = 64
SAMPLES_DEV = 512
BF = jnp.bfloat16
F32 = jnp.float32
VMEM_LIMIT = 32 * 1024 * 1024


def split_table(table):
    high = table.astype(ml_dtypes.bfloat16)
    low = (table - high.astype(np.float64)).astype(ml_dtypes.bfloat16)
    return high, low


def hann(position):
    return np.minimum(position + 0.5, PATCH - 0.5 - position) / HALF


def sample_forward():
    table = np.zeros((2, 128, 2, 64, 2))
    v = np.arange(64)
    for p in range(2):
        for m in range(64):
            angle = 2 * np.pi * ((v * m) % 64) / 64
            n = m + 32 * p
            table[0, n, 0, :, p] = np.cos(angle)
            table[1, n, 0, :, p] = np.sin(angle)
            table[0, n, 1, :, p] = -np.sin(angle)
            table[1, n, 1, :, p] = np.cos(angle)
    return table.reshape(256, 256)


def line_forward():
    table = np.zeros((3, 2, 64, 2, 128))
    u = np.arange(64)
    for band in range(3):
        for m in range(64):
            angle = 2 * np.pi * ((u * m) % 64) / 64
            i = m + 32 * band
            table[band, 0, :, 0, i] = np.cos(angle)
            table[band, 0, :, 1, i] = np.sin(angle)
            table[band, 1, :, 0, i] = -np.sin(angle)
            table[band, 1, :, 1, i] = np.cos(angle)
    return table.reshape(384, 256)


def line_inverse():
    table = np.zeros((2, 64, 3, 2, 64))
    u = np.arange(64)
    for band in range(3):
        for y in range(64):
            m = y + 32 - 32 * band
            if 0 <= m < 64:
                angle = 2 * np.pi * ((u * m) % 64) / 64
                weight = hann(m) / 64
                table[0, y, band, 0, :] = weight * np.cos(angle)
                table[0, y, band, 1, :] = -weight * np.sin(angle)
                table[1, y, band, 0, :] = weight * np.sin(angle)
                table[1, y, band, 1, :] = weight * np.cos(angle)
    return table.reshape(128, 384)


def sample_inverse(start):
    table = np.zeros((2, 64, 2, 2, 128))
    v = np.arange(64)
    for p in range(2):
        for y in range(128):
            n = 32 + y - start - 32 * p
            if 0 <= n < 64:
                angle = 2 * np.pi * ((v * n) % 64) / 64
                weight = hann(n) / 64
                table[0, :, p, 0, y] = weight * np.cos(angle)
                table[1, :, p, 0, y] = -weight * np.sin(angle)
                table[0, :, p, 1, y] = weight * np.sin(angle)
                table[1, :, p, 1, y] = weight * np.cos(angle)
    return table.reshape(256, 256)


def filter_tables():
    inverse = np.stack([sample_inverse(start) for start in (0, 64, 128, 96)])
    tables = []
    for table in (sample_forward(), line_forward(), line_inverse(), inverse):
        tables.extend(split_table(table))
    return tables


def sinc_rows(fraction):
    tap = lax.broadcasted_iota(jnp.int32, (TAPS, fraction.shape[1]), 0)
    distance = fraction - (tap - (TAPS // 2 - 1)).astype(F32)
    centre = distance == 0.0
    sign = jnp.where(tap % 2 == 1, 1.0, -1.0)
    wave = sign * jnp.sin(np.float32(np.pi) * fraction)
    sinc = wave / jnp.where(centre, 1.0, np.float32(np.pi) * distance)
    sinc = jnp.where(centre, 1.0, sinc)
    taper = 0.5 + 0.5 * jnp.cos(np.float32(np.pi) * distance / (TAPS // 2))
    return (sinc * taper).astype(BF).astype(F32)


def kernel_rows(shift, fraction):
    weights = sinc_rows(fraction)
    row = lax.broadcasted_iota(jnp.int32, weights.shape, 0)
    shifts = jnp.where(row == 0, shift.astype(F32), 0.0)
    return jnp.concatenate([weights, shifts], axis=0)


def band_matrix(rows, depth):
    width = rows.shape[1]
    shift = rows[TAPS : TAPS + 1].astype(jnp.int32)
    source = lax.broadcasted_iota(jnp.int32, (depth, width), 0)
    target = lax.broadcasted_iota(jnp.int32, (depth, width), 1)
    step = source - (target + 13 + shift)
    matrix = jnp.zeros((depth, width), F32)
    for k in range(TAPS):
        matrix = jnp.where(step == k, rows[k : k + 1], matrix)
    return matrix


def split(values):
    high = values.astype(BF)
    return high, (values - high.astype(F32)).astype(BF)


def dot(left, right):
    return jnp.dot(left, right, preferred_element_type=F32)


def dot_table(values, high, low):
    values_high, values_low = split(values)
    return dot(values_high, high) + dot(values_low, high) + dot(values_high, low)


def table_dot(high, low, values):
    values_high, values_low = split(values)
    return dot(high, values_high) + dot(high, values_low) + dot(low, values_high)


def pack_body(secondary, own, peer1, peer2, peer3, shift, fraction, first, second, reference, line_rows):
    date = lax.axis_index("date")
    odd = lax.axis_index("az") % 2 == 1
    pieces = (own, peer1, peer2, peer3)
    for value in range(4):

        @pl.when(date == value)
        def _():
            for offset in range(4):
                place = value ^ offset
                reference[:, :, place * 128 : place * 128 + 128] = pieces[offset][...]

    row_shift = jnp.concatenate([shift[...], shift[...]], axis=1)
    row_fraction = jnp.concatenate([fraction[...], fraction[...]], axis=1)
    rows = kernel_rows(pltpu.roll(row_shift, 32, 1), pltpu.roll(row_fraction, 32, 1))
    line_rows[...] = rows
    rows = rows.astype(BF)

    def fill(message, sec_start, ref_start):
        for part in range(2):
            message[part * 48 : part * 48 + 48] = secondary[0, part, sec_start : sec_start + 48]
            message[96 + part * 32 : 128 + part * 32] = reference[part, ref_start : ref_start + 32]
        message[160:176, 0:128] = rows
        message[160:176, 128:512] = jnp.zeros((16, 384), BF)

    @pl.when(odd)
    def _():
        fill(first, 0, 0)
        fill(second, 16, 32)

    @pl.when(jnp.logical_not(odd))
    def _():
        fill(first, 16, 32)
        fill(second, 0, 0)


def lines_body(secondary, reference, line_rows, first, second, shift, fraction,
               rows_out, master, sample_rows, send_first, send_second, extended, halo_rows):
    az = lax.axis_index("az")
    odd = az % 2 == 1
    has_top = az > 0
    has_bottom = az < lax.axis_size("az") - 1

    def place(top, bottom):
        for part in range(2):
            extended[part, 0:48] = top[part * 48 : part * 48 + 48]
            extended[part, 112:160] = bottom[part * 48 : part * 48 + 48]
            master[part * 128 : part * 128 + 32] = top[96 + part * 32 : 128 + part * 32]
            master[part * 128 + 96 : part * 128 + 128] = bottom[96 + part * 32 : 128 + part * 32]
        halo_rows[0] = top[160:176, 0:128].astype(F32)
        halo_rows[1] = bottom[160:176, 0:128].astype(F32)

    @pl.when(odd)
    def _():
        place(first, second)

    @pl.when(jnp.logical_not(odd))
    def _():
        place(second, first)

    for part in range(2):
        extended[part, 48:112] = secondary[0, part]
        master[part * 128 + 32 : part * 128 + 96] = reference[part]

    @pl.when(jnp.logical_not(has_top))
    def _():
        for part in range(2):
            master[part * 128 : part * 128 + 32] = jnp.zeros((32, 512), BF)
            extended[part, 0:48] = jnp.zeros((48, 512), BF)

    @pl.when(jnp.logical_not(has_bottom))
    def _():
        for part in range(2):
            master[part * 128 + 96 : part * 128 + 128] = jnp.zeros((32, 512), BF)
            extended[part, 112:160] = jnp.zeros((48, 512), BF)

    lane = lax.broadcasted_iota(jnp.int32, (16, 128), 1)
    rows = jnp.where(
        lane < 32,
        pltpu.roll(halo_rows[0], 64, 1),
        jnp.where(lane < 96, line_rows[...], pltpu.roll(halo_rows[1], 64, 1)),
    )
    matrix = band_matrix(rows, 160).astype(BF)
    for part in range(2):
        values = lax.dot_general(
            matrix, extended[part], (((0,), (0,)), ((), ())), preferred_element_type=F32
        )
        rows_out[part * 128 : part * 128 + 128] = values.astype(BF)

    samples = kernel_rows(shift[...], fraction[...])
    sample_rows[...] = samples
    lane = lax.broadcasted_iota(jnp.int32, (256, 128), 1)
    to_right = jnp.where(
        lane < 48,
        pltpu.roll(rows_out[:, 384:512].astype(F32), 48, 1),
        master[:, 384:512].astype(F32),
    ).astype(BF)
    to_left = jnp.where(
        lane >= 80,
        pltpu.roll(rows_out[:, 0:128].astype(F32), 80, 1),
        master[:, 0:128].astype(F32),
    ).astype(BF)
    right_rows = samples[:, 384:512].astype(BF)
    left_rows = samples[:, 0:128].astype(BF)
    rg_odd = lax.axis_index("rg") % 2 == 1

    @pl.when(rg_odd)
    def _():
        send_first[0:256] = to_left
        send_first[256:272] = left_rows
        send_second[0:256] = to_right
        send_second[256:272] = right_rows

    @pl.when(jnp.logical_not(rg_odd))
    def _():
        send_first[0:256] = to_right
        send_first[256:272] = right_rows
        send_second[0:256] = to_left
        send_second[256:272] = left_rows


def shifted(tiles, start):
    index, offset = start // 128, start % 128
    here = pltpu.roll(tiles[index], 128 - offset, 1)
    after = pltpu.roll(tiles[min(index + 1, 3)], 128 - offset, 1)
    lane = lax.broadcasted_iota(jnp.int32, here.shape, 1)
    return jnp.where(lane < 128 - offset, here, after)


def lane_sum(values):
    for step in (2, 4, 8, 16, 32, 64):
        values = values + pltpu.roll(values, step, 1)
    return values


def block_spectrum(window, master, rows, forward):
    matrix = band_matrix(rows, 128).astype(BF)
    resampled = dot(window.astype(BF), matrix)
    real, imag = resampled[:128], resampled[128:]
    product = jnp.concatenate(
        [master[:128] * real + master[128:] * imag, master[128:] * real - master[:128] * imag],
        axis=1,
    )
    columns = dot_table(product, forward[0][...], forward[1][...])
    return jnp.concatenate([columns[:, :128], columns[:, 128:]], axis=0)


def filter_spectrum(spectrum, single):
    parts = []
    for band in range(3):
        real = spectrum[band * 128 : band * 128 + 64]
        imag = spectrum[band * 128 + 64 : band * 128 + 128]
        smooth = jnp.sqrt(real * real + imag * imag)
        smooth = smooth + pltpu.roll(smooth, 2, 1) + pltpu.roll(smooth, 126, 1)
        smooth = smooth + pltpu.roll(smooth, 1, 0) + pltpu.roll(smooth, 63, 0)
        response = jnp.sqrt(smooth * np.float32(1 / 9))
        mean = lane_sum(jnp.sum(response, axis=0, keepdims=True)) * np.float32(1 / 4096)
        scale = 1.0 / (mean + 1e-06)
        if single:
            lane = lax.broadcasted_iota(jnp.int32, scale.shape, 1)
            scale = jnp.where(lane % 2 == 0, scale, 0.0)
        gain = response * scale
        parts.extend([real * gain, imag * gain])
    return jnp.concatenate(parts, axis=0)


def filter_blocks(columns, singles, lines, inverse):
    spectrum = table_dot(lines[0][...], lines[1][...], jnp.concatenate(columns, axis=1))
    gained = jnp.concatenate(
        [
            filter_spectrum(spectrum[:, at * 128 : at * 128 + 128], single)
            for at, single in enumerate(singles)
        ],
        axis=1,
    )
    back = table_dot(inverse[0][...], inverse[1][...], gained)
    result = []
    for at in range(len(singles)):
        tile = back[:, at * 128 : at * 128 + 128]
        result.append(jnp.concatenate([tile[:64], tile[64:]], axis=1))
    return result


def filter_body(rows_in, master, sample_rows, first, second, *refs):
    forward, lines, inverse, samples = refs[0:2], refs[2:4], refs[4:6], refs[6:8]
    out = refs[8]
    rg = lax.axis_index("rg")
    odd = rg % 2 == 1
    left_scale = jnp.where(rg > 0, 1.0, 0.0).astype(F32)
    right_scale = jnp.where(rg < lax.axis_size("rg") - 1, 1.0, 0.0).astype(F32)

    row_tiles = [rows_in[:, t * 128 : t * 128 + 128].astype(F32) for t in range(4)]
    master_tiles = [master[:, t * 128 : t * 128 + 128].astype(F32) for t in range(4)]
    sample_tiles = [sample_rows[:, t * 128 : t * 128 + 128] for t in range(4)]

    def interior(j):
        return block_spectrum(
            shifted(row_tiles, 64 * j - 48),
            shifted(master_tiles, 64 * j - 32),
            shifted(sample_tiles, 64 * j - 32),
            forward,
        )

    def contribute(values, block, which):
        return dot_table(values, samples[0][which], samples[1][which])

    totals = [None] * 4

    def add(block, which, values):
        part = contribute(values, block, which)
        totals[block] = part if totals[block] is None else totals[block] + part

    for group in ((1, 2), (3, 4), (5, 6), (7,)):
        columns = [interior(j) for j in group]
        results = filter_blocks(columns, [j == 7 for j in group], lines, inverse)
        for j, values in zip(group, results):
            if j % 2 == 1:
                add(j // 2, 1, values)
            else:
                add(j // 2, 0, values)
                add(j // 2 - 1, 2, values)

    first_f = first[...].astype(F32)
    second_f = second[...].astype(F32)
    from_left = jnp.where(odd, first_f, second_f)
    from_right = jnp.where(odd, second_f, first_f)

    def mixed(lane_count, halo, own, reverse):
        lane = lax.broadcasted_iota(jnp.int32, own.shape, 1)
        return jnp.where(lane >= lane_count if reverse else lane < lane_count, halo, own)

    left = block_spectrum(
        mixed(48, from_left[:256] * left_scale, pltpu.roll(row_tiles[0], 48, 1), False),
        mixed(32, pltpu.roll(from_left[:256], 32, 1) * left_scale, pltpu.roll(master_tiles[0], 32, 1), False),
        mixed(32, pltpu.roll(from_left[256:], 32, 1), pltpu.roll(sample_tiles[0], 32, 1), False),
        forward,
    )
    right = block_spectrum(
        mixed(80, from_right[:256] * right_scale, pltpu.roll(row_tiles[3], 80, 1), True),
        mixed(64, pltpu.roll(from_right[:256], 64, 1) * right_scale, pltpu.roll(master_tiles[3], 64, 1), True),
        mixed(64, pltpu.roll(from_right[256:], 64, 1), pltpu.roll(sample_tiles[3], 64, 1), True),
        forward,
    )
    results = filter_blocks([left, right], [False, False], lines, inverse)
    add(0, 0, results[0])
    add(3, 3, results[1])
    for block in range(4):
        out[0, 0, :, block * 128 : block * 128 + 128] = totals[block][:, :128]
        out[0, 1, :, block * 128 : block * 128 + 128] = totals[block][:, 128:]


def call(body, outputs, scratch=()):
    vmem = pl.BlockSpec(memory_space=pltpu.VMEM)
    return lambda *args: pl.pallas_call(
        body,
        out_shape=[jax.ShapeDtypeStruct(shape, kind) for shape, kind in outputs],
        in_specs=[vmem] * len(args),
        out_specs=[vmem] * len(outputs),
        scratch_shapes=list(scratch),
        compiler_params=pltpu.CompilerParams(vmem_limit_bytes=VMEM_LIMIT),
    )(*args)


def swaps(size):
    first = [(i, i ^ 1) for i in range(size)]
    second = [(i, (i + 1) % size if i % 2 == 1 else (i - 1) % size) for i in range(size)]
    return first, second


def exchange(first, second, axis):
    pairs = swaps(lax.axis_size(axis))
    received_second = lax.ppermute(second, axis, pairs[1])
    received_first = lax.ppermute(first, axis, pairs[0])
    return received_first, received_second


def on_device(reference_slab, secondary, az_shift, az_fraction, rg_shift, rg_fraction):
    own = reference_slab.reshape(2, LINES_DEV, 128)
    peers = [lax.ppermute(own, "date", [(i, i ^ k) for i in range(4)]) for k in (1, 2, 3)]
    first, second, reference, line_rows = call(
        pack_body,
        [((176, 512), BF), ((176, 512), BF), ((2, LINES_DEV, 512), BF), ((16, 128), F32)],
    )(secondary, own, *peers, az_shift, az_fraction)
    first, second = exchange(first, second, "az")
    rows, master, sample_rows, first, second = call(
        lines_body,
        [((256, 512), BF), ((256, 512), BF), ((16, 512), F32), ((272, 128), BF), ((272, 128), BF)],
        [pltpu.VMEM((2, 160, 512), BF), pltpu.VMEM((2, 16, 128), F32)],
    )(secondary, reference, line_rows, first, second, rg_shift, rg_fraction)
    first, second = exchange(first, second, "rg")
    tables = [jnp.asarray(table) for table in filter_tables()]
    return call(filter_body, [((1, 2, LINES_DEV, SAMPLES_DEV), F32)])(
        rows, master, sample_rows, first, second, *tables
    )[0]


def solution(mesh):
    in_specs = (
        P(None, "az", "rg", "date"),
        P("date", None, "az", "rg"),
        P("date", "az"),
        P("date", "az"),
        P("date", "rg"),
        P("date", "rg"),
    )
    out_specs = P("date", None, "az", "rg")
    return jax.shard_map(
        on_device, mesh=mesh, in_specs=in_specs, out_specs=out_specs, check_vma=False
    )
```

```python
import functools

import jax
import jax.numpy as jnp
import ml_dtypes
import numpy as np
from jax import lax
from jax.experimental import pallas as pl
from jax.experimental.pallas import tpu as pltpu
from jax.sharding import PartitionSpec as P

PATCH = 64
HALF = 32
TAPS = 8
MARGIN = 48
LINES_DEV = 64
SAMPLES_DEV = 512
BF = jnp.bfloat16
F32 = jnp.float32
VMEM_LIMIT = 32 * 1024 * 1024


def split_table(table):
    high = table.astype(ml_dtypes.bfloat16)
    low = (table - high.astype(np.float64)).astype(ml_dtypes.bfloat16)
    return high, low


def hann(position):
    return np.minimum(position + 0.5, PATCH - 0.5 - position) / HALF


def sample_forward():
    table = np.zeros((2, 128, 2, 64, 2))
    v = np.arange(64)
    for p in range(2):
        for m in range(64):
            angle = 2 * np.pi * ((v * m) % 64) / 64
            n = m + 32 * p
            table[0, n, 0, :, p] = np.cos(angle)
            table[1, n, 0, :, p] = np.sin(angle)
            table[0, n, 1, :, p] = -np.sin(angle)
            table[1, n, 1, :, p] = np.cos(angle)
    return table.reshape(256, 256)


def line_forward():
    table = np.zeros((3, 2, 64, 2, 128))
    u = np.arange(64)
    for band in range(3):
        for m in range(64):
            angle = 2 * np.pi * ((u * m) % 64) / 64
            i = m + 32 * band
            table[band, 0, :, 0, i] = np.cos(angle)
            table[band, 0, :, 1, i] = np.sin(angle)
            table[band, 1, :, 0, i] = -np.sin(angle)
            table[band, 1, :, 1, i] = np.cos(angle)
    return table.reshape(384, 256)


def line_inverse():
    table = np.zeros((2, 64, 3, 2, 64))
    u = np.arange(64)
    for band in range(3):
        for y in range(64):
            m = y + 32 - 32 * band
            if 0 <= m < 64:
                angle = 2 * np.pi * ((u * m) % 64) / 64
                weight = hann(m) / 64
                table[0, y, band, 0, :] = weight * np.cos(angle)
                table[0, y, band, 1, :] = -weight * np.sin(angle)
                table[1, y, band, 0, :] = weight * np.sin(angle)
                table[1, y, band, 1, :] = weight * np.cos(angle)
    return table.reshape(128, 384)


def sample_inverse(start):
    table = np.zeros((2, 64, 2, 2, 128))
    v = np.arange(64)
    for p in range(2):
        for y in range(128):
            n = 32 + y - start - 32 * p
            if 0 <= n < 64:
                angle = 2 * np.pi * ((v * n) % 64) / 64
                weight = hann(n) / 64
                table[0, :, p, 0, y] = weight * np.cos(angle)
                table[1, :, p, 0, y] = -weight * np.sin(angle)
                table[0, :, p, 1, y] = weight * np.sin(angle)
                table[1, :, p, 1, y] = weight * np.cos(angle)
    return table.reshape(256, 256)


def triple(table, axis):
    high, low = split_table(table)
    return np.concatenate([high, high, low], axis=axis)


def filter_tables():
    inverse = [sample_inverse(start) for start in (0, 64, 128, 96)]
    return [
        triple(sample_forward(), 0),
        triple(line_forward(), 1),
        triple(line_inverse(), 1),
        np.concatenate([triple(table, 0) for table in inverse], axis=0),
    ]


def sinc_rows(fraction):
    tap = lax.broadcasted_iota(jnp.int32, (TAPS, fraction.shape[1]), 0)
    distance = fraction - (tap - (TAPS // 2 - 1)).astype(F32)
    centre = distance == 0.0
    sign = jnp.where(tap % 2 == 1, 1.0, -1.0)
    wave = sign * jnp.sin(np.float32(np.pi) * fraction)
    sinc = wave / jnp.where(centre, 1.0, np.float32(np.pi) * distance)
    sinc = jnp.where(centre, 1.0, sinc)
    taper = 0.5 + 0.5 * jnp.cos(np.float32(np.pi) * distance / (TAPS // 2))
    return (sinc * taper).astype(BF).astype(F32)


def kernel_rows(shift, fraction):
    weights = sinc_rows(fraction)
    row = lax.broadcasted_iota(jnp.int32, weights.shape, 0)
    shifts = jnp.where(row == 0, shift.astype(F32), 0.0)
    return jnp.concatenate([weights, shifts], axis=0)


def band_matrix(rows, depth):
    width = rows.shape[1]
    shift = rows[TAPS : TAPS + 1].astype(jnp.int32)
    source = lax.broadcasted_iota(jnp.int32, (depth, width), 0)
    target = lax.broadcasted_iota(jnp.int32, (depth, width), 1)
    step = source - (target + 13 + shift)
    matrix = jnp.zeros((depth, width), F32)
    for k in range(TAPS):
        matrix = jnp.where(step == k, rows[k : k + 1], matrix)
    return matrix


def split(values):
    high = values.astype(BF)
    return high, (values - high.astype(F32)).astype(BF)


def dot(left, right):
    return jnp.dot(left, right, preferred_element_type=F32)


def columns_triple(values):
    high, low = split(values)
    return jnp.concatenate([high, low, high], axis=1)


def rows_triple(values):
    high, low = split(values)
    return jnp.concatenate([high, low, high], axis=0)


def shifted(tiles, start):
    index, offset = start // 128, start % 128
    here = pltpu.roll(tiles[index], 128 - offset, 1)
    after = pltpu.roll(tiles[min(index + 1, 3)], 128 - offset, 1)
    lane = lax.broadcasted_iota(jnp.int32, here.shape, 1)
    return jnp.where(lane < 128 - offset, here, after)


def tiles_of(values):
    return [values[:, t * 128 : t * 128 + 128].astype(F32) for t in range(4)]


def pack_body(secondary, own, shift, fraction, first, second, line_rows, shift_v, fraction_v, sems):
    odd = lax.axis_index("az") % 2 == 1
    small = [
        pltpu.make_async_copy(shift, shift_v, sems.at[20]),
        pltpu.make_async_copy(fraction, fraction_v, sems.at[21]),
    ]
    for copy in small:
        copy.start()
    copies = []
    for message, upper in ((first, odd), (second, jnp.logical_not(odd))):
        line = pl.multiple_of(jnp.where(upper, 0, 16), 16)
        half = pl.multiple_of(jnp.where(upper, 0, 32), 16)
        for part in range(2):
            for tile in range(4):
                copies.append(
                    pltpu.make_async_copy(
                        secondary.at[0, part, pl.ds(line, 48), pl.ds(tile * 128, 128)],
                        message.at[pl.ds((2 * tile + part) * 48, 48)],
                        sems.at[len(copies)],
                    )
                )
            copies.append(
                pltpu.make_async_copy(
                    own.at[part, pl.ds(half, 32)],
                    message.at[pl.ds(384 + part * 32, 32)],
                    sems.at[len(copies)],
                )
            )
    for copy in copies:
        copy.start()
    for copy in small:
        copy.wait()
    row_shift = jnp.concatenate([shift_v[...], shift_v[...]], axis=1)
    row_fraction = jnp.concatenate([fraction_v[...], fraction_v[...]], axis=1)
    rows = kernel_rows(pltpu.roll(row_shift, 32, 1), pltpu.roll(row_fraction, 32, 1))
    line_rows[...] = rows
    first[448:464] = rows.astype(BF)
    second[448:464] = rows.astype(BF)
    for copy in copies:
        copy.wait()


def prepare_body(secondary, own, shift, fraction, *refs):
    tables, outs = refs[0:4], refs[4:13]
    secondary_v, own_v, sample_rows, bands = outs[0:4]
    tables_v = outs[4:8]
    shift_v, fraction_v, sems = outs[8], refs[13], refs[14]
    pairs = [(shift, shift_v), (fraction, fraction_v), (own, own_v), (secondary, secondary_v)]
    pairs.extend(zip(tables, tables_v))
    copies = [
        pltpu.make_async_copy(source, target, sems.at[at]) for at, (source, target) in enumerate(pairs)
    ]
    for copy in copies:
        copy.start()
    for copy in copies[:2]:
        copy.wait()
    samples = kernel_rows(shift_v[...], fraction_v[...])
    sample_rows[...] = samples
    tiles = tiles_of(samples)
    for j in range(1, 8):
        bands[j - 1] = band_matrix(shifted(tiles, 64 * j - 32), 128).astype(BF)
    for copy in copies[2:]:
        copy.wait()


def lines_body(secondary, line_rows, first, second, bands, edges, resampled, extended, halo_rows):
    odd = lax.axis_index("az") % 2 == 1
    has_top = lax.axis_index("az") > 0
    has_bottom = lax.axis_index("az") < lax.axis_size("az") - 1

    def place(top, bottom):
        for part in range(2):
            for tile in range(4):
                rows = slice((2 * tile + part) * 48, (2 * tile + part) * 48 + 48)
                lanes = slice(tile * 128, tile * 128 + 128)
                extended[part, 0:48, lanes] = top[rows]
                extended[part, 112:160, lanes] = bottom[rows]
        halo_rows[0] = top[448:464].astype(F32)
        halo_rows[1] = bottom[448:464].astype(F32)

    @pl.when(odd)
    def _():
        place(first, second)

    @pl.when(jnp.logical_not(odd))
    def _():
        place(second, first)

    for part in range(2):
        extended[part, 48:112] = secondary[0, part]

    lane = lax.broadcasted_iota(jnp.int32, (16, 128), 1)
    rows = jnp.where(
        lane < 32,
        pltpu.roll(halo_rows[0], 64, 1),
        jnp.where(lane < 96, line_rows[...], pltpu.roll(halo_rows[1], 64, 1)),
    )
    matrix = band_matrix(rows, 160)
    line = lax.broadcasted_iota(jnp.int32, matrix.shape, 0)
    low = jnp.where(has_top, 0, 48)
    high = jnp.where(has_bottom, 160, 112)
    matrix = jnp.where((line >= low) & (line < high), matrix, 0.0).astype(BF)
    values = [
        lax.dot_general(
            matrix, extended[part], (((0,), (0,)), ((), ())), preferred_element_type=F32
        )
        for part in range(2)
    ]
    values = jnp.concatenate(values, axis=0).astype(BF)
    edges[:, 0:128] = values[:, 0:128]
    edges[:, 128:256] = values[:, 384:512]
    tiles = tiles_of(values)
    for j in range(1, 8):
        resampled[j - 1] = dot(shifted(tiles, 64 * j - 48).astype(BF), bands[j - 1])


def reference_body(own, peer1, peer2, peer3, halo, halo1, halo2, halo3, edges, sample_rows,
                   master, send_first, send_second):
    date = lax.axis_index("date")
    az = lax.axis_index("az")
    odd = az % 2 == 1
    has_top = az > 0
    has_bottom = az < lax.axis_size("az") - 1
    pieces = (own, peer1, peer2, peer3)
    halos = (halo, halo1, halo2, halo3)
    for value in range(4):

        @pl.when(date == value)
        def _():
            for offset in range(4):
                lanes = slice((value ^ offset) * 128, (value ^ offset) * 128 + 128)
                piece, around = pieces[offset], halos[offset]
                for part in range(2):
                    base = part * 128
                    master[base + 32 : base + 96, lanes] = piece[part]

                    @pl.when(odd)
                    def _():
                        master[base : base + 32, lanes] = around[part * 32 : part * 32 + 32]
                        master[base + 96 : base + 128, lanes] = around[64 + part * 32 : 96 + part * 32]

                    @pl.when(jnp.logical_not(odd))
                    def _():
                        master[base : base + 32, lanes] = around[64 + part * 32 : 96 + part * 32]
                        master[base + 96 : base + 128, lanes] = around[part * 32 : part * 32 + 32]

    @pl.when(jnp.logical_not(has_top))
    def _():
        for part in range(2):
            master[part * 128 : part * 128 + 32] = jnp.zeros((32, 512), BF)

    @pl.when(jnp.logical_not(has_bottom))
    def _():
        for part in range(2):
            master[part * 128 + 96 : part * 128 + 128] = jnp.zeros((32, 512), BF)

    lane = lax.broadcasted_iota(jnp.int32, (256, 128), 1)
    to_right = jnp.where(
        lane < 48,
        pltpu.roll(edges[:, 128:256].astype(F32), 48, 1),
        master[:, 384:512].astype(F32),
    ).astype(BF)
    to_left = jnp.where(
        lane >= 80,
        pltpu.roll(edges[:, 0:128].astype(F32), 80, 1),
        master[:, 0:128].astype(F32),
    ).astype(BF)
    right_rows = sample_rows[:, 384:512].astype(BF)
    left_rows = sample_rows[:, 0:128].astype(BF)
    rg_odd = lax.axis_index("rg") % 2 == 1

    @pl.when(rg_odd)
    def _():
        send_first[0:256] = to_left
        send_first[256:272] = left_rows
        send_second[0:256] = to_right
        send_second[256:272] = right_rows

    @pl.when(jnp.logical_not(rg_odd))
    def _():
        send_first[0:256] = to_right
        send_first[256:272] = right_rows
        send_second[0:256] = to_left
        send_second[256:272] = left_rows


def lane_sum(values):
    for step in (2, 4, 8, 16, 32, 64):
        values = values + pltpu.roll(values, step, 1)
    return values


def root(values):
    return values * lax.rsqrt(jnp.maximum(values, np.float32(1e-36)))


def block_columns(resampled, master, forward):
    real, imag = resampled[:128], resampled[128:]
    product = jnp.concatenate(
        [master[:128] * real + master[128:] * imag, master[128:] * real - master[:128] * imag],
        axis=1,
    )
    columns = dot(columns_triple(product), forward)
    return jnp.concatenate([columns[:, :128], columns[:, 128:]], axis=0)


def responses(spectrum):
    result = []
    for band in range(3):
        real = spectrum[band * 128 : band * 128 + 64]
        imag = spectrum[band * 128 + 64 : band * 128 + 128]
        smooth = root(real * real + imag * imag)
        smooth = smooth + pltpu.roll(smooth, 2, 1) + pltpu.roll(smooth, 126, 1)
        smooth = smooth + pltpu.roll(smooth, 1, 0) + pltpu.roll(smooth, 63, 0)
        result.append(root(smooth))
    return result


def gained(spectrum, response, scale):
    parts = []
    for band in range(3):
        gain = response[band] * scale[band : band + 1]
        parts.append(spectrum[band * 128 : band * 128 + 64] * gain)
        parts.append(spectrum[band * 128 + 64 : band * 128 + 128] * gain)
    return jnp.concatenate(parts, axis=0)


def filter_blocks(columns, singles, lines, inverse):
    count = len(columns)
    spectrum = dot(lines, jnp.concatenate([rows_triple(column) for column in columns], axis=1))
    spectra = [spectrum[:, at * 128 : at * 128 + 128] for at in range(count)]
    response = [responses(values) for values in spectra]
    sums = jnp.concatenate(
        [jnp.sum(values, axis=0, keepdims=True) for block in response for values in block], axis=0
    )
    scale = 1.0 / (lane_sum(sums) * np.float32(1 / 4096) + np.float32(3e-06))
    lane = lax.broadcasted_iota(jnp.int32, (3, 128), 1)
    filtered = []
    for at in range(count):
        factor = scale[3 * at : 3 * at + 3]
        if singles[at]:
            factor = jnp.where(lane % 2 == 0, factor, 0.0)
        filtered.append(rows_triple(gained(spectra[at], response[at], factor)))
    back = dot(inverse, jnp.concatenate(filtered, axis=1))
    result = []
    for at in range(count):
        tile = back[:, at * 128 : at * 128 + 128]
        result.append(columns_triple(jnp.concatenate([tile[:64], tile[64:]], axis=1)))
    return result


def interior_body(resampled, master, forward, lines, inverse, samples, out):
    tiles = tiles_of(master[...])
    columns = [
        block_columns(resampled[j - 1], shifted(tiles, 64 * j - 32), forward[...])
        for j in range(1, 8)
    ]
    parts = filter_blocks(columns, [j == 7 for j in range(1, 8)], lines[...], inverse[...])
    for block in range(4):
        used = [j for j in (2 * block, 2 * block + 1, 2 * block + 2) if 1 <= j <= 7]
        start = (used[0] - 2 * block) * 768
        values = dot(
            jnp.concatenate([parts[j - 1] for j in used], axis=1),
            samples[start : start + 768 * len(used)],
        )
        out[0, 0, :, block * 128 : block * 128 + 128] = values[:, :128]
        out[0, 1, :, block * 128 : block * 128 + 128] = values[:, 128:]


def edge_body(part, edges, master, sample_rows, first, second, forward, lines, inverse, samples, out):
    rg = lax.axis_index("rg")
    odd = rg % 2 == 1
    left_scale = jnp.where(rg > 0, 1.0, 0.0).astype(F32)
    right_scale = jnp.where(rg < lax.axis_size("rg") - 1, 1.0, 0.0).astype(F32)
    first_f = first[...].astype(F32)
    second_f = second[...].astype(F32)
    from_left = jnp.where(odd, first_f, second_f)
    from_right = jnp.where(odd, second_f, first_f)

    def mixed(lane_count, halo, own, reverse):
        lane = lax.broadcasted_iota(jnp.int32, own.shape, 1)
        return jnp.where(lane >= lane_count if reverse else lane < lane_count, halo, own)

    def edge(window, around, rows):
        matrix = band_matrix(rows, 128).astype(BF)
        return block_columns(dot(window.astype(BF), matrix), around, forward[...])

    left = edge(
        mixed(48, from_left[:256] * left_scale,
              pltpu.roll(edges[:, 0:128].astype(F32), 48, 1), False),
        mixed(32, pltpu.roll(from_left[:256], 32, 1) * left_scale,
              pltpu.roll(master[:, 0:128].astype(F32), 32, 1), False),
        mixed(32, pltpu.roll(from_left[256:], 32, 1),
              pltpu.roll(sample_rows[:, 0:128], 32, 1), False),
    )
    right = edge(
        mixed(80, from_right[:256] * right_scale,
              pltpu.roll(edges[:, 128:256].astype(F32), 80, 1), True),
        mixed(64, pltpu.roll(from_right[:256], 64, 1) * right_scale,
              pltpu.roll(master[:, 384:512].astype(F32), 64, 1), True),
        mixed(64, pltpu.roll(from_right[256:], 64, 1),
              pltpu.roll(sample_rows[:, 384:512], 64, 1), True),
    )
    parts = filter_blocks([left, right], [False, False], lines[...], inverse[...])
    for at, block in ((0, 0), (1, 3)):
        values = dot(parts[at], samples[block * 768 : block * 768 + 768])
        lanes = slice(block * 128, block * 128 + 128)
        out[0, 0, :, lanes] = part[0, 0, :, lanes] + values[:, :128]
        out[0, 1, :, lanes] = part[0, 1, :, lanes] + values[:, 128:]
    out[0, :, :, 128:384] = part[0, :, :, 128:384]


def call(name, body, outputs, scratch=(), hbm=0, cost=0):
    vmem = pl.BlockSpec(memory_space=pltpu.VMEM)
    far = pl.BlockSpec(memory_space=pltpu.HBM)
    return lambda *args: pl.pallas_call(
        body,
        name=name,
        out_shape=[jax.ShapeDtypeStruct(shape, kind) for shape, kind in outputs],
        in_specs=[far] * hbm + [vmem] * (len(args) - hbm),
        out_specs=[vmem] * len(outputs),
        scratch_shapes=list(scratch),
        compiler_params=pltpu.CompilerParams(vmem_limit_bytes=VMEM_LIMIT),
        cost_estimate=pl.CostEstimate(flops=cost, bytes_accessed=cost // 100, transcendentals=0),
    )(*args)


def swaps(size):
    first = [(i, i ^ 1) for i in range(size)]
    second = [(i, (i + 1) % size if i % 2 == 1 else (i - 1) % size) for i in range(size)]
    return first, second


def exchange(first, second, axis):
    pairs = swaps(lax.axis_size(axis))
    received_first = lax.ppermute(first, axis, pairs[0])
    received_second = lax.ppermute(second, axis, pairs[1])
    return received_first, received_second


def date_swaps(values):
    return [lax.ppermute(values, "date", [(i, i ^ k) for i in range(4)]) for k in (1, 2, 3)]


def on_device(reference_slab, secondary, az_shift, az_fraction, rg_shift, rg_fraction):
    own = reference_slab.reshape(2, LINES_DEV, 128)
    message = ((464, 128), BF)
    first, second, line_rows = call(
        "pack", pack_body, [message, message, ((16, 128), F32)],
        [pltpu.VMEM((1, 64), jnp.int32), pltpu.VMEM((1, 64), F32), pltpu.SemaphoreType.DMA((22,))],
        hbm=4, cost=10**9,
    )(secondary, own, az_shift, az_fraction)
    tables = [jnp.asarray(table) for table in filter_tables()]
    prepared = call(
        "prepare", prepare_body,
        [((1, 2, LINES_DEV, 512), BF), ((2, LINES_DEV, 128), BF), ((16, 512), F32), ((7, 128, 128), BF)]
        + [(table.shape, BF) for table in tables],
        [pltpu.VMEM((1, 512), jnp.int32), pltpu.VMEM((1, 512), F32), pltpu.SemaphoreType.DMA((8,))],
        hbm=8, cost=2 * 10**9,
    )(secondary, own, rg_shift, rg_fraction, *tables)
    secondary_v, own_v, sample_rows, bands = prepared[:4]
    tables_v = prepared[4:]
    first, second = exchange(first, second, "az")
    peers = date_swaps(own_v)
    halo = jnp.concatenate([first[384:448], second[384:448]], axis=0)
    halos = date_swaps(halo)
    edges, resampled = call(
        "lines", lines_body, [((256, 256), BF), ((7, 256, 128), F32)],
        [pltpu.VMEM((2, 160, 512), BF), pltpu.VMEM((2, 16, 128), F32)],
        cost=10**9,
    )(secondary_v, line_rows, first, second, bands)
    master, first, second = call(
        "reference", reference_body, [((256, 512), BF), ((272, 128), BF), ((272, 128), BF)],
        cost=10**8,
    )(own_v, *peers, halo, *halos, edges, sample_rows)
    first, second = exchange(first, second, "rg")
    whole = ((1, 2, LINES_DEV, SAMPLES_DEV), F32)
    part = call("interior", interior_body, [whole], cost=4 * 10**9)(resampled, master, *tables_v)[0]
    return call("edge", edge_body, [whole], cost=10**9)(
        part, edges, master, sample_rows, first, second, *tables_v
    )[0]


def solution(mesh):
    in_specs = (
        P(None, "az", "rg", "date"),
        P("date", None, "az", "rg"),
        P("date", "az"),
        P("date", "az"),
        P("date", "rg"),
        P("date", "rg"),
    )
    out_specs = P("date", None, "az", "rg")
    return jax.shard_map(
        on_device, mesh=mesh, in_specs=in_specs, out_specs=out_specs, check_vma=False
    )
```

```python
import functools

import jax
import jax.numpy as jnp
import ml_dtypes
import numpy as np
from jax import lax
from jax.experimental import pallas as pl
from jax.experimental.pallas import tpu as pltpu
from jax.sharding import PartitionSpec as P

PATCH = 64
HALF = 32
TAPS = 8
MARGIN = 48
LINES_DEV = 64
SAMPLES_DEV = 512
BF = jnp.bfloat16
F32 = jnp.float32
VMEM_LIMIT = 32 * 1024 * 1024


def split_table(table):
    high = table.astype(ml_dtypes.bfloat16)
    low = (table - high.astype(np.float64)).astype(ml_dtypes.bfloat16)
    return high, low


def hann(position):
    return np.minimum(position + 0.5, PATCH - 0.5 - position) / HALF


def sample_forward():
    table = np.zeros((2, 128, 2, 64, 2))
    v = np.arange(64)
    for p in range(2):
        for m in range(64):
            angle = 2 * np.pi * ((v * m) % 64) / 64
            n = m + 32 * p
            table[0, n, 0, :, p] = np.cos(angle)
            table[1, n, 0, :, p] = np.sin(angle)
            table[0, n, 1, :, p] = -np.sin(angle)
            table[1, n, 1, :, p] = np.cos(angle)
    return table.reshape(256, 256)


def line_forward():
    table = np.zeros((3, 2, 64, 2, 128))
    u = np.arange(64)
    for band in range(3):
        for m in range(64):
            angle = 2 * np.pi * ((u * m) % 64) / 64
            i = m + 32 * band
            table[band, 0, :, 0, i] = np.cos(angle)
            table[band, 0, :, 1, i] = np.sin(angle)
            table[band, 1, :, 0, i] = -np.sin(angle)
            table[band, 1, :, 1, i] = np.cos(angle)
    return table.reshape(384, 256)


def line_inverse():
    table = np.zeros((2, 64, 3, 2, 64))
    u = np.arange(64)
    for band in range(3):
        for y in range(64):
            m = y + 32 - 32 * band
            if 0 <= m < 64:
                angle = 2 * np.pi * ((u * m) % 64) / 64
                weight = hann(m) / 64
                table[0, y, band, 0, :] = weight * np.cos(angle)
                table[0, y, band, 1, :] = -weight * np.sin(angle)
                table[1, y, band, 0, :] = weight * np.sin(angle)
                table[1, y, band, 1, :] = weight * np.cos(angle)
    return table.reshape(128, 384)


def sample_inverse(start):
    table = np.zeros((2, 64, 2, 2, 128))
    v = np.arange(64)
    for p in range(2):
        for y in range(128):
            n = 32 + y - start - 32 * p
            if 0 <= n < 64:
                angle = 2 * np.pi * ((v * n) % 64) / 64
                weight = hann(n) / 64
                table[0, :, p, 0, y] = weight * np.cos(angle)
                table[1, :, p, 0, y] = -weight * np.sin(angle)
                table[0, :, p, 1, y] = weight * np.sin(angle)
                table[1, :, p, 1, y] = weight * np.cos(angle)
    return table.reshape(256, 256)


def triple(table, axis):
    high, low = split_table(table)
    return np.concatenate([high, high, low], axis=axis)


def filter_tables():
    inverse = [sample_inverse(start) for start in (0, 64, 128, 96)]
    return [
        triple(sample_forward(), 0),
        triple(line_forward(), 1),
        triple(line_inverse(), 1),
        np.concatenate([triple(table, 0) for table in inverse], axis=0),
    ]


def sinc_rows(fraction):
    tap = lax.broadcasted_iota(jnp.int32, (TAPS, fraction.shape[1]), 0)
    distance = fraction - (tap - (TAPS // 2 - 1)).astype(F32)
    centre = distance == 0.0
    sign = jnp.where(tap % 2 == 1, 1.0, -1.0)
    wave = sign * jnp.sin(np.float32(np.pi) * fraction)
    sinc = wave / jnp.where(centre, 1.0, np.float32(np.pi) * distance)
    sinc = jnp.where(centre, 1.0, sinc)
    taper = 0.5 + 0.5 * jnp.cos(np.float32(np.pi) * distance / (TAPS // 2))
    return (sinc * taper).astype(BF).astype(F32)


def kernel_rows(shift, fraction):
    weights = sinc_rows(fraction)
    row = lax.broadcasted_iota(jnp.int32, weights.shape, 0)
    shifts = jnp.where(row == 0, shift.astype(F32), 0.0)
    return jnp.concatenate([weights, shifts], axis=0)


def band_matrix(rows, depth):
    width = rows.shape[1]
    shift = rows[TAPS : TAPS + 1].astype(jnp.int32)
    source = lax.broadcasted_iota(jnp.int32, (depth, width), 0)
    target = lax.broadcasted_iota(jnp.int32, (depth, width), 1)
    step = source - (target + 13 + shift)
    matrix = jnp.zeros((depth, width), F32)
    for k in range(TAPS):
        matrix = jnp.where(step == k, rows[k : k + 1], matrix)
    return matrix


def split(values):
    high = values.astype(BF)
    return high, (values - high.astype(F32)).astype(BF)


def dot(left, right):
    return jnp.dot(left, right, preferred_element_type=F32)


def columns_triple(values):
    high, low = split(values)
    return jnp.concatenate([high, low, high], axis=1)


def rows_triple(values):
    high, low = split(values)
    return jnp.concatenate([high, low, high], axis=0)


def shifted(tiles, start):
    index, offset = start // 128, start % 128
    here = pltpu.roll(tiles[index], 128 - offset, 1)
    after = pltpu.roll(tiles[min(index + 1, 3)], 128 - offset, 1)
    lane = lax.broadcasted_iota(jnp.int32, here.shape, 1)
    return jnp.where(lane < 128 - offset, here, after)


def tiles_of(values):
    return [values[:, t * 128 : t * 128 + 128].astype(F32) for t in range(4)]


def lead_body(out):
    out[...] = jnp.zeros_like(out)


def pack_body(secondary, own, shift, fraction, lead, first, second, line_rows):
    odd = lax.axis_index("az") % 2 == 1

    def fill(message, line, half):
        for part in range(2):
            for tile in range(4):
                rows = slice((2 * tile + part) * 48, (2 * tile + part) * 48 + 48)
                message[rows] = secondary[0, part, line : line + 48, tile * 128 : tile * 128 + 128]
            message[384 + part * 32 : 416 + part * 32] = own[part, half : half + 32]

    @pl.when(odd)
    def _():
        fill(first, 0, 0)
        fill(second, 16, 32)

    @pl.when(jnp.logical_not(odd))
    def _():
        fill(first, 16, 32)
        fill(second, 0, 0)

    row_shift = jnp.concatenate([shift[...], shift[...]], axis=1)
    row_fraction = jnp.concatenate([fraction[...], fraction[...]], axis=1)
    rows = kernel_rows(pltpu.roll(row_shift, 32, 1), pltpu.roll(row_fraction, 32, 1)) + lead[...]
    line_rows[...] = rows
    first[448:464] = rows.astype(BF)
    second[448:464] = rows.astype(BF)


def prepare_body(secondary, own, shift, fraction, *refs):
    tables, outs = refs[0:4], refs[4:13]
    secondary_v, own_v, sample_rows, bands = outs[0:4]
    tables_v = outs[4:8]
    shift_v, fraction_v, sems = outs[8], refs[13], refs[14]
    pairs = [(shift, shift_v), (fraction, fraction_v), (own, own_v), (secondary, secondary_v)]
    pairs.extend(zip(tables, tables_v))
    copies = [
        pltpu.make_async_copy(source, target, sems.at[at]) for at, (source, target) in enumerate(pairs)
    ]
    for copy in copies:
        copy.start()
    for copy in copies[:2]:
        copy.wait()
    samples = kernel_rows(shift_v[...], fraction_v[...])
    sample_rows[...] = samples
    tiles = tiles_of(samples)
    for j in range(1, 8):
        bands[j - 1] = band_matrix(shifted(tiles, 64 * j - 32), 128).astype(BF)
    for copy in copies[2:]:
        copy.wait()


def lines_body(secondary, line_rows, first, second, bands, edges, resampled, extended, halo_rows):
    odd = lax.axis_index("az") % 2 == 1
    has_top = lax.axis_index("az") > 0
    has_bottom = lax.axis_index("az") < lax.axis_size("az") - 1

    def place(top, bottom):
        for part in range(2):
            for tile in range(4):
                rows = slice((2 * tile + part) * 48, (2 * tile + part) * 48 + 48)
                lanes = slice(tile * 128, tile * 128 + 128)
                extended[part, 0:48, lanes] = top[rows]
                extended[part, 112:160, lanes] = bottom[rows]
        halo_rows[0] = top[448:464].astype(F32)
        halo_rows[1] = bottom[448:464].astype(F32)

    @pl.when(odd)
    def _():
        place(first, second)

    @pl.when(jnp.logical_not(odd))
    def _():
        place(second, first)

    for part in range(2):
        extended[part, 48:112] = secondary[0, part]

    lane = lax.broadcasted_iota(jnp.int32, (16, 128), 1)
    rows = jnp.where(
        lane < 32,
        pltpu.roll(halo_rows[0], 64, 1),
        jnp.where(lane < 96, line_rows[...], pltpu.roll(halo_rows[1], 64, 1)),
    )
    matrix = band_matrix(rows, 160)
    line = lax.broadcasted_iota(jnp.int32, matrix.shape, 0)
    low = jnp.where(has_top, 0, 48)
    high = jnp.where(has_bottom, 160, 112)
    matrix = jnp.where((line >= low) & (line < high), matrix, 0.0).astype(BF)
    values = [
        lax.dot_general(
            matrix, extended[part], (((0,), (0,)), ((), ())), preferred_element_type=F32
        )
        for part in range(2)
    ]
    values = jnp.concatenate(values, axis=0).astype(BF)
    edges[:, 0:128] = values[:, 0:128]
    edges[:, 128:256] = values[:, 384:512]
    tiles = tiles_of(values)
    for j in range(1, 8):
        resampled[j - 1] = dot(shifted(tiles, 64 * j - 48).astype(BF), bands[j - 1])


def reference_body(own, peer1, peer2, peer3, halo, halo1, halo2, halo3, edges, sample_rows,
                   master, send_first, send_second):
    date = lax.axis_index("date")
    az = lax.axis_index("az")
    odd = az % 2 == 1
    has_top = az > 0
    has_bottom = az < lax.axis_size("az") - 1
    pieces = (own, peer1, peer2, peer3)
    halos = (halo, halo1, halo2, halo3)
    for value in range(4):

        @pl.when(date == value)
        def _():
            for offset in range(4):
                lanes = slice((value ^ offset) * 128, (value ^ offset) * 128 + 128)
                piece, around = pieces[offset], halos[offset]
                for part in range(2):
                    base = part * 128
                    master[base + 32 : base + 96, lanes] = piece[part]

                    @pl.when(odd)
                    def _():
                        master[base : base + 32, lanes] = around[part * 32 : part * 32 + 32]
                        master[base + 96 : base + 128, lanes] = around[64 + part * 32 : 96 + part * 32]

                    @pl.when(jnp.logical_not(odd))
                    def _():
                        master[base : base + 32, lanes] = around[64 + part * 32 : 96 + part * 32]
                        master[base + 96 : base + 128, lanes] = around[part * 32 : part * 32 + 32]

    @pl.when(jnp.logical_not(has_top))
    def _():
        for part in range(2):
            master[part * 128 : part * 128 + 32] = jnp.zeros((32, 512), BF)

    @pl.when(jnp.logical_not(has_bottom))
    def _():
        for part in range(2):
            master[part * 128 + 96 : part * 128 + 128] = jnp.zeros((32, 512), BF)

    lane = lax.broadcasted_iota(jnp.int32, (256, 128), 1)
    to_right = jnp.where(
        lane < 48,
        pltpu.roll(edges[:, 128:256].astype(F32), 48, 1),
        master[:, 384:512].astype(F32),
    ).astype(BF)
    to_left = jnp.where(
        lane >= 80,
        pltpu.roll(edges[:, 0:128].astype(F32), 80, 1),
        master[:, 0:128].astype(F32),
    ).astype(BF)
    right_rows = sample_rows[:, 384:512].astype(BF)
    left_rows = sample_rows[:, 0:128].astype(BF)
    rg_odd = lax.axis_index("rg") % 2 == 1

    @pl.when(rg_odd)
    def _():
        send_first[0:256] = to_left
        send_first[256:272] = left_rows
        send_second[0:256] = to_right
        send_second[256:272] = right_rows

    @pl.when(jnp.logical_not(rg_odd))
    def _():
        send_first[0:256] = to_right
        send_first[256:272] = right_rows
        send_second[0:256] = to_left
        send_second[256:272] = left_rows


def lane_sum(values):
    for step in (2, 4, 8, 16, 32, 64):
        values = values + pltpu.roll(values, step, 1)
    return values


def root(values):
    return values * lax.rsqrt(jnp.maximum(values, np.float32(1e-36)))


def block_columns(resampled, master, forward):
    real, imag = resampled[:128], resampled[128:]
    product = jnp.concatenate(
        [master[:128] * real + master[128:] * imag, master[128:] * real - master[:128] * imag],
        axis=1,
    )
    columns = dot(columns_triple(product), forward)
    return jnp.concatenate([columns[:, :128], columns[:, 128:]], axis=0)


def responses(spectrum):
    result = []
    for band in range(3):
        real = spectrum[band * 128 : band * 128 + 64]
        imag = spectrum[band * 128 + 64 : band * 128 + 128]
        smooth = root(real * real + imag * imag)
        smooth = smooth + pltpu.roll(smooth, 2, 1) + pltpu.roll(smooth, 126, 1)
        smooth = smooth + pltpu.roll(smooth, 1, 0) + pltpu.roll(smooth, 63, 0)
        result.append(root(smooth))
    return result


def gained(spectrum, response, scale):
    parts = []
    for band in range(3):
        gain = response[band] * scale[band : band + 1]
        parts.append(spectrum[band * 128 : band * 128 + 64] * gain)
        parts.append(spectrum[band * 128 + 64 : band * 128 + 128] * gain)
    return jnp.concatenate(parts, axis=0)


def filter_blocks(columns, singles, lines, inverse):
    count = len(columns)
    spectrum = dot(lines, jnp.concatenate([rows_triple(column) for column in columns], axis=1))
    spectra = [spectrum[:, at * 128 : at * 128 + 128] for at in range(count)]
    response = [responses(values) for values in spectra]
    sums = jnp.concatenate(
        [jnp.sum(values, axis=0, keepdims=True) for block in response for values in block], axis=0
    )
    scale = 1.0 / (lane_sum(sums) * np.float32(1 / 4096) + np.float32(3e-06))
    lane = lax.broadcasted_iota(jnp.int32, (3, 128), 1)
    filtered = []
    for at in range(count):
        factor = scale[3 * at : 3 * at + 3]
        if singles[at]:
            factor = jnp.where(lane % 2 == 0, factor, 0.0)
        filtered.append(rows_triple(gained(spectra[at], response[at], factor)))
    back = dot(inverse, jnp.concatenate(filtered, axis=1))
    result = []
    for at in range(count):
        tile = back[:, at * 128 : at * 128 + 128]
        result.append(columns_triple(jnp.concatenate([tile[:64], tile[64:]], axis=1)))
    return result


def interior_body(resampled, master, forward, lines, inverse, samples, out):
    tiles = tiles_of(master[...])
    columns = [
        block_columns(resampled[j - 1], shifted(tiles, 64 * j - 32), forward[...])
        for j in range(1, 8)
    ]
    parts = filter_blocks(columns, [j == 7 for j in range(1, 8)], lines[...], inverse[...])
    for block in range(4):
        used = [j for j in (2 * block, 2 * block + 1, 2 * block + 2) if 1 <= j <= 7]
        start = (used[0] - 2 * block) * 768
        values = dot(
            jnp.concatenate([parts[j - 1] for j in used], axis=1),
            samples[start : start + 768 * len(used)],
        )
        out[0, 0, :, block * 128 : block * 128 + 128] = values[:, :128]
        out[0, 1, :, block * 128 : block * 128 + 128] = values[:, 128:]


def edge_body(part, edges, master, sample_rows, first, second, forward, lines, inverse, samples, out):
    rg = lax.axis_index("rg")
    odd = rg % 2 == 1
    left_scale = jnp.where(rg > 0, 1.0, 0.0).astype(F32)
    right_scale = jnp.where(rg < lax.axis_size("rg") - 1, 1.0, 0.0).astype(F32)
    first_f = first[...].astype(F32)
    second_f = second[...].astype(F32)
    from_left = jnp.where(odd, first_f, second_f)
    from_right = jnp.where(odd, second_f, first_f)

    def mixed(lane_count, halo, own, reverse):
        lane = lax.broadcasted_iota(jnp.int32, own.shape, 1)
        return jnp.where(lane >= lane_count if reverse else lane < lane_count, halo, own)

    def edge(window, around, rows):
        matrix = band_matrix(rows, 128).astype(BF)
        return block_columns(dot(window.astype(BF), matrix), around, forward[...])

    left = edge(
        mixed(48, from_left[:256] * left_scale,
              pltpu.roll(edges[:, 0:128].astype(F32), 48, 1), False),
        mixed(32, pltpu.roll(from_left[:256], 32, 1) * left_scale,
              pltpu.roll(master[:, 0:128].astype(F32), 32, 1), False),
        mixed(32, pltpu.roll(from_left[256:], 32, 1),
              pltpu.roll(sample_rows[:, 0:128], 32, 1), False),
    )
    right = edge(
        mixed(80, from_right[:256] * right_scale,
              pltpu.roll(edges[:, 128:256].astype(F32), 80, 1), True),
        mixed(64, pltpu.roll(from_right[:256], 64, 1) * right_scale,
              pltpu.roll(master[:, 384:512].astype(F32), 64, 1), True),
        mixed(64, pltpu.roll(from_right[256:], 64, 1),
              pltpu.roll(sample_rows[:, 384:512], 64, 1), True),
    )
    parts = filter_blocks([left, right], [False, False], lines[...], inverse[...])
    for at, block in ((0, 0), (1, 3)):
        values = dot(parts[at], samples[block * 768 : block * 768 + 768])
        lanes = slice(block * 128, block * 128 + 128)
        out[0, 0, :, lanes] = part[0, 0, :, lanes] + values[:, :128]
        out[0, 1, :, lanes] = part[0, 1, :, lanes] + values[:, 128:]
    out[0, :, :, 128:384] = part[0, :, :, 128:384]


def call(name, body, outputs, scratch=(), hbm=0, cost=0):
    vmem = pl.BlockSpec(memory_space=pltpu.VMEM)
    far = pl.BlockSpec(memory_space=pltpu.HBM)
    return lambda *args: pl.pallas_call(
        body,
        name=name,
        out_shape=[jax.ShapeDtypeStruct(shape, kind) for shape, kind in outputs],
        in_specs=[far] * hbm + [vmem] * (len(args) - hbm),
        out_specs=[vmem] * len(outputs),
        scratch_shapes=list(scratch),
        compiler_params=pltpu.CompilerParams(vmem_limit_bytes=VMEM_LIMIT),
        cost_estimate=pl.CostEstimate(flops=cost, bytes_accessed=cost // 100, transcendentals=0),
    )(*args)


def exchange(first, second, axis):
    size = lax.axis_size(axis)
    dates = lax.axis_size("date")
    pairs = []
    for date in range(dates):
        for i in range(size):
            partner = (date, i + 1 if i % 2 == 1 else i - 1)
            if i in (0, size - 1):
                partner = (date ^ 1, i)
            pairs.append((date * size + i, partner[0] * size + partner[1]))
    received_first = lax.ppermute(first, axis, [(i, i ^ 1) for i in range(size)])
    received_second = lax.ppermute(second, ("date", axis), pairs)
    return received_first, received_second


def date_swaps(values):
    return [lax.ppermute(values, "date", [(i, i ^ k) for i in range(4)]) for k in (1, 2, 3)]


def on_device(reference_slab, secondary, az_shift, az_fraction, rg_shift, rg_fraction):
    own = reference_slab.reshape(2, LINES_DEV, 128)
    message = ((464, 128), BF)
    lead = call("lead", lead_body, [((16, 128), F32)], cost=2 * 10**9)()[0]
    first, second, line_rows = call(
        "pack", pack_body, [message, message, ((16, 128), F32)],
        cost=10**9,
    )(secondary, own, az_shift, az_fraction, lead)
    tables = [jnp.asarray(table) for table in filter_tables()]
    prepared = call(
        "prepare", prepare_body,
        [((1, 2, LINES_DEV, 512), BF), ((2, LINES_DEV, 128), BF), ((16, 512), F32), ((7, 128, 128), BF)]
        + [(table.shape, BF) for table in tables],
        [pltpu.VMEM((1, 512), jnp.int32), pltpu.VMEM((1, 512), F32), pltpu.SemaphoreType.DMA((8,))],
        hbm=8, cost=2 * 10**9,
    )(secondary, own, rg_shift, rg_fraction, *tables)
    secondary_v, own_v, sample_rows, bands = prepared[:4]
    tables_v = prepared[4:]
    first, second = exchange(first, second, "az")
    peers = date_swaps(own_v)
    halo = jnp.concatenate([first[384:448], second[384:448]], axis=0)
    halos = date_swaps(halo)
    edges, resampled = call(
        "lines", lines_body, [((256, 256), BF), ((7, 256, 128), F32)],
        [pltpu.VMEM((2, 160, 512), BF), pltpu.VMEM((2, 16, 128), F32)],
        cost=10**9,
    )(secondary_v, line_rows, first, second, bands)
    master, first, second = call(
        "reference", reference_body, [((256, 512), BF), ((272, 128), BF), ((272, 128), BF)],
        cost=10**8,
    )(own_v, *peers, halo, *halos, edges, sample_rows)
    first, second = exchange(first, second, "rg")
    whole = ((1, 2, LINES_DEV, SAMPLES_DEV), F32)
    part = call("interior", interior_body, [whole], cost=4 * 10**9)(resampled, master, *tables_v)[0]
    return call("edge", edge_body, [whole], cost=10**9)(
        part, edges, master, sample_rows, first, second, *tables_v
    )[0]


def solution(mesh):
    in_specs = (
        P(None, "az", "rg", "date"),
        P("date", None, "az", "rg"),
        P("date", "az"),
        P("date", "az"),
        P("date", "rg"),
        P("date", "rg"),
    )
    out_specs = P("date", None, "az", "rg")
    return jax.shard_map(
        on_device, mesh=mesh, in_specs=in_specs, out_specs=out_specs, check_vma=False
    )
```

```python
import functools

import jax
import jax.numpy as jnp
import ml_dtypes
import numpy as np
from jax import lax
from jax.experimental import pallas as pl
from jax.experimental.pallas import tpu as pltpu
from jax.sharding import PartitionSpec as P

PATCH = 64
HALF = 32
TAPS = 8
MARGIN = 48
LINES_DEV = 64
SAMPLES_DEV = 512
BF = jnp.bfloat16
F32 = jnp.float32
VMEM_LIMIT = 32 * 1024 * 1024


def split_table(table):
    high = table.astype(ml_dtypes.bfloat16)
    low = (table - high.astype(np.float64)).astype(ml_dtypes.bfloat16)
    return high, low


def hann(position):
    return np.minimum(position + 0.5, PATCH - 0.5 - position) / HALF


def sample_forward():
    table = np.zeros((2, 128, 2, 64, 2))
    v = np.arange(64)
    for p in range(2):
        for m in range(64):
            angle = 2 * np.pi * ((v * m) % 64) / 64
            n = m + 32 * p
            table[0, n, 0, :, p] = np.cos(angle)
            table[1, n, 0, :, p] = np.sin(angle)
            table[0, n, 1, :, p] = -np.sin(angle)
            table[1, n, 1, :, p] = np.cos(angle)
    return table.reshape(256, 256)


def line_forward():
    table = np.zeros((2, 64, 2, 64))
    u = np.arange(64)
    for m in range(64):
        angle = 2 * np.pi * ((u * m) % 64) / 64
        table[0, :, 0, m] = np.cos(angle)
        table[0, :, 1, m] = np.sin(angle)
        table[1, :, 0, m] = -np.sin(angle)
        table[1, :, 1, m] = np.cos(angle)
    return table.reshape(128, 128)


def line_inverse():
    table = np.zeros((2, 2, 32, 2, 64))
    u = np.arange(64)
    for m in range(64):
        angle = 2 * np.pi * ((u * m) % 64) / 64
        weight = hann(m) / 64
        table[m // 32, 0, m % 32, 0, :] = weight * np.cos(angle)
        table[m // 32, 0, m % 32, 1, :] = -weight * np.sin(angle)
        table[m // 32, 1, m % 32, 0, :] = weight * np.sin(angle)
        table[m // 32, 1, m % 32, 1, :] = weight * np.cos(angle)
    return table.reshape(128, 128)


def sample_inverse(start):
    table = np.zeros((2, 64, 2, 2, 128))
    v = np.arange(64)
    for p in range(2):
        for y in range(128):
            n = 32 + y - start - 32 * p
            if 0 <= n < 64:
                angle = 2 * np.pi * ((v * n) % 64) / 64
                weight = hann(n) / 64
                table[0, :, p, 0, y] = weight * np.cos(angle)
                table[1, :, p, 0, y] = -weight * np.sin(angle)
                table[0, :, p, 1, y] = weight * np.sin(angle)
                table[1, :, p, 1, y] = weight * np.cos(angle)
    return table.reshape(256, 256)


def triple(table, axis):
    high, low = split_table(table)
    return np.concatenate([high, high, low], axis=axis)


def filter_tables():
    inverse = [sample_inverse(start) for start in (0, 64, 128, 96)]
    return [
        triple(sample_forward(), 0),
        triple(line_forward(), 1),
        triple(line_inverse(), 1),
        np.concatenate([triple(table, 0) for table in inverse], axis=0),
    ]


def sinc_rows(fraction):
    tap = lax.broadcasted_iota(jnp.int32, (TAPS, fraction.shape[1]), 0)
    distance = fraction - (tap - (TAPS // 2 - 1)).astype(F32)
    centre = distance == 0.0
    sign = jnp.where(tap % 2 == 1, 1.0, -1.0)
    wave = sign * jnp.sin(np.float32(np.pi) * fraction)
    sinc = wave / jnp.where(centre, 1.0, np.float32(np.pi) * distance)
    sinc = jnp.where(centre, 1.0, sinc)
    taper = 0.5 + 0.5 * jnp.cos(np.float32(np.pi) * distance / (TAPS // 2))
    return (sinc * taper).astype(BF).astype(F32)


def kernel_rows(shift, fraction):
    weights = sinc_rows(fraction)
    row = lax.broadcasted_iota(jnp.int32, weights.shape, 0)
    shifts = jnp.where(row == 0, shift.astype(F32), 0.0)
    return jnp.concatenate([weights, shifts], axis=0)


def band_matrix(rows, depth):
    width = rows.shape[1]
    shift = rows[TAPS : TAPS + 1].astype(jnp.int32)
    source = lax.broadcasted_iota(jnp.int32, (depth, width), 0)
    target = lax.broadcasted_iota(jnp.int32, (depth, width), 1)
    step = source - (target + 13 + shift)
    matrix = jnp.zeros((depth, width), F32)
    for k in range(TAPS):
        matrix = jnp.where(step == k, rows[k : k + 1], matrix)
    return matrix


def split(values):
    high = values.astype(BF)
    return high, (values - high.astype(F32)).astype(BF)


def dot(left, right):
    return jnp.dot(left, right, preferred_element_type=F32)


def columns_triple(values):
    high, low = split(values)
    return jnp.concatenate([high, low, high], axis=1)


def rows_triple(values):
    high, low = split(values)
    return jnp.concatenate([high, low, high], axis=0)


def shifted(tiles, start):
    index, offset = start // 128, start % 128
    here = pltpu.roll(tiles[index], 128 - offset, 1)
    after = pltpu.roll(tiles[min(index + 1, 3)], 128 - offset, 1)
    lane = lax.broadcasted_iota(jnp.int32, here.shape, 1)
    return jnp.where(lane < 128 - offset, here, after)


def tiles_of(values):
    return [values[:, t * 128 : t * 128 + 128].astype(F32) for t in range(4)]


def lead_body(out):
    out[...] = jnp.zeros_like(out)


def pack_body(secondary, own, shift, fraction, lead, first, second, line_rows):
    odd = lax.axis_index("az") % 2 == 1

    def fill(message, line, half):
        for part in range(2):
            for tile in range(4):
                rows = slice((2 * tile + part) * 48, (2 * tile + part) * 48 + 48)
                message[rows] = secondary[0, part, line : line + 48, tile * 128 : tile * 128 + 128]
            message[384 + part * 32 : 416 + part * 32] = own[part, half : half + 32]

    @pl.when(odd)
    def _():
        fill(first, 0, 0)
        fill(second, 16, 32)

    @pl.when(jnp.logical_not(odd))
    def _():
        fill(first, 16, 32)
        fill(second, 0, 0)

    row_shift = jnp.concatenate([shift[...], shift[...]], axis=1)
    row_fraction = jnp.concatenate([fraction[...], fraction[...]], axis=1)
    rows = kernel_rows(pltpu.roll(row_shift, 32, 1), pltpu.roll(row_fraction, 32, 1)) + lead[...]
    line_rows[...] = rows
    first[448:464] = rows.astype(BF)
    second[448:464] = rows.astype(BF)


def prepare_body(secondary, own, shift, fraction, *refs):
    tables, outs = refs[0:4], refs[4:13]
    secondary_v, own_v, sample_rows, bands = outs[0:4]
    tables_v = outs[4:8]
    shift_v, fraction_v, sems = outs[8], refs[13], refs[14]
    pairs = [(shift, shift_v), (fraction, fraction_v), (own, own_v), (secondary, secondary_v)]
    pairs.extend(zip(tables, tables_v))
    copies = [
        pltpu.make_async_copy(source, target, sems.at[at]) for at, (source, target) in enumerate(pairs)
    ]
    for copy in copies:
        copy.start()
    for copy in copies[:2]:
        copy.wait()
    samples = kernel_rows(shift_v[...], fraction_v[...])
    sample_rows[...] = samples
    tiles = tiles_of(samples)
    for j in range(1, 8):
        bands[j - 1] = band_matrix(shifted(tiles, 64 * j - 32), 128).astype(BF)
    for copy in copies[2:]:
        copy.wait()


def lines_body(secondary, line_rows, first, second, bands, edges, resampled, late, extended, halo_rows):
    odd = lax.axis_index("az") % 2 == 1
    has_top = lax.axis_index("az") > 0
    has_bottom = lax.axis_index("az") < lax.axis_size("az") - 1

    def place(top, bottom):
        for part in range(2):
            for tile in range(4):
                rows = slice((2 * tile + part) * 48, (2 * tile + part) * 48 + 48)
                lanes = slice(tile * 128, tile * 128 + 128)
                extended[part, 0:48, lanes] = top[rows]
                extended[part, 112:160, lanes] = bottom[rows]
        halo_rows[0] = top[448:464].astype(F32)
        halo_rows[1] = bottom[448:464].astype(F32)

    @pl.when(odd)
    def _():
        place(first, second)

    @pl.when(jnp.logical_not(odd))
    def _():
        place(second, first)

    late[0:64] = first[384:448]
    late[64:128] = second[384:448]
    for part in range(2):
        extended[part, 48:112] = secondary[0, part]

    lane = lax.broadcasted_iota(jnp.int32, (16, 128), 1)
    rows = jnp.where(
        lane < 32,
        pltpu.roll(halo_rows[0], 64, 1),
        jnp.where(lane < 96, line_rows[...], pltpu.roll(halo_rows[1], 64, 1)),
    )
    matrix = band_matrix(rows, 160)
    line = lax.broadcasted_iota(jnp.int32, matrix.shape, 0)
    low = jnp.where(has_top, 0, 48)
    high = jnp.where(has_bottom, 160, 112)
    matrix = jnp.where((line >= low) & (line < high), matrix, 0.0).astype(BF)
    values = [
        lax.dot_general(
            matrix, extended[part], (((0,), (0,)), ((), ())), preferred_element_type=F32
        )
        for part in range(2)
    ]
    values = jnp.concatenate(values, axis=0).astype(BF)
    edges[:, 0:128] = values[:, 0:128]
    edges[:, 128:256] = values[:, 384:512]
    tiles = tiles_of(values)
    for j in range(1, 8):
        resampled[j - 1] = dot(shifted(tiles, 64 * j - 48).astype(BF), bands[j - 1])


def by_date(pieces, store):
    date = lax.axis_index("date")
    for value in range(4):

        @pl.when(date == value)
        def _():
            for offset in range(4):
                place = (value ^ offset) * 128
                store(pieces[offset], slice(place, place + 128))


def root(values):
    return values * lax.rsqrt(jnp.maximum(values, np.float32(1e-36)))


def sample_columns(real, imag, master_real, master_imag, forward):
    product = jnp.concatenate(
        [master_real * real + master_imag * imag, master_imag * real - master_real * imag], axis=1
    )
    columns = dot(columns_triple(product), forward)
    return columns[:, :128], columns[:, 128:]


def response_of(spectrum):
    real, imag = spectrum[:64], spectrum[64:]
    smooth = root(real * real + imag * imag)
    smooth = smooth + pltpu.roll(smooth, 2, 1) + pltpu.roll(smooth, 126, 1)
    smooth = smooth + pltpu.roll(smooth, 1, 0) + pltpu.roll(smooth, 63, 0)
    return root(smooth)


def window_scales(responses):
    sums = jnp.concatenate(
        [jnp.sum(values.reshape(8, 8, 128), axis=0) for values in responses], axis=0
    )
    high, low = split(sums)
    row = lax.broadcasted_iota(jnp.int32, (256, 128), 0)
    lane = lax.broadcasted_iota(jnp.int32, (256, 128), 1)
    same = jnp.where((row - lane) % 2 == 0, 1.0, 0.0).astype(BF)
    totals = dot(jnp.concatenate([high, low], axis=1), same)
    scales = []
    for at in range(len(responses)):
        total = jnp.sum(totals[8 * at : 8 * at + 8], axis=0, keepdims=True)
        scales.append(1.0 / (total * np.float32(1 / 4096) + np.float32(3e-06)))
    return scales


def filter_band(highs, lows, lines, inverse):
    stacked = [jnp.concatenate([high, low, high], axis=0) for high, low in zip(highs, lows)]
    spectrum = dot(lines, jnp.concatenate(stacked, axis=1))
    spectra = [spectrum[:, at * 128 : at * 128 + 128] for at in range(len(highs))]
    responses = [response_of(values) for values in spectra]
    gained = [
        rows_triple(values * jnp.concatenate([response, response], axis=0))
        for values, response in zip(spectra, responses)
    ]
    back = dot(inverse, jnp.concatenate(gained, axis=1))
    scales = window_scales(responses)
    return [
        back[:, at * 128 : at * 128 + 128] * scales[at] for at in range(len(highs))
    ]


def pair_rows(top, bottom):
    real = jnp.concatenate([top[:32], bottom[:32]], axis=0)
    imag = jnp.concatenate([top[32:], bottom[32:]], axis=0)
    return columns_triple(jnp.concatenate([real, imag], axis=1))


def early_body(own, peer1, peer2, peer3, resampled, forward, lines, inverse,
               master, column_high, column_low, back):
    def store(piece, lanes):
        master[0:64, lanes] = piece[0]
        master[64:128, lanes] = piece[1]

    by_date((own, peer1, peer2, peer3), store)
    tiles = tiles_of(master)
    highs, lows = [], []
    for j in range(1, 8):
        around = shifted(tiles, 64 * j - 32)
        real, imag = sample_columns(
            resampled[j - 1, 32:96], resampled[j - 1, 160:224], around[:64], around[64:], forward[...]
        )
        high, low = split(jnp.concatenate([real, imag], axis=0))
        column_high[j - 1] = high
        column_low[j - 1] = low
        highs.append(high)
        lows.append(low)
    middle = filter_band(highs, lows, lines[...], inverse[...])
    for j in range(1, 8):
        back[j - 1] = middle[j - 1]


def reference_body(halo, halo1, halo2, halo3, master, edges, sample_rows,
                   around, send_first, send_second):
    az = lax.axis_index("az")
    odd = az % 2 == 1

    def store(piece, lanes):
        @pl.when(odd)
        def _():
            for part in range(2):
                around[part * 64 : part * 64 + 32, lanes] = piece[part * 32 : part * 32 + 32]
                around[part * 64 + 32 : part * 64 + 64, lanes] = piece[64 + part * 32 : 96 + part * 32]

        @pl.when(jnp.logical_not(odd))
        def _():
            for part in range(2):
                around[part * 64 : part * 64 + 32, lanes] = piece[64 + part * 32 : 96 + part * 32]
                around[part * 64 + 32 : part * 64 + 64, lanes] = piece[part * 32 : part * 32 + 32]

    by_date((halo, halo1, halo2, halo3), store)

    @pl.when(az == 0)
    def _():
        for part in range(2):
            around[part * 64 : part * 64 + 32] = jnp.zeros((32, 512), BF)

    @pl.when(az == lax.axis_size("az") - 1)
    def _():
        for part in range(2):
            around[part * 64 + 32 : part * 64 + 64] = jnp.zeros((32, 512), BF)

    lane = lax.broadcasted_iota(jnp.int32, (128, 128), 1)
    narrow = lax.broadcasted_iota(jnp.int32, (32, 128), 1)

    def message(tile, edge, turn):
        lanes = slice(tile * 128, tile * 128 + 128)
        rows = edges[:, edge * 128 : edge * 128 + 128].astype(F32)
        own, far = master[:, lanes].astype(F32), around[:, lanes].astype(F32)
        real = jnp.concatenate([far[:32], own[:64], far[32:64]], axis=0)
        imag = jnp.concatenate([far[64:96], own[64:], far[96:]], axis=0)
        wide = jnp.where(
            lane < 48,
            pltpu.roll(rows[:128], turn[0], 1) if turn[0] else rows[:128],
            jnp.where(
                lane < 96,
                pltpu.roll(rows[128:], turn[1], 1),
                pltpu.roll(real, turn[2], 1) if turn[2] else real,
            ),
        )
        tail = pltpu.roll(imag[:32], (turn[2] + 32) % 128, 1)
        for group in range(1, 4):
            step = (turn[2] + 32 + 32 * group) % 128
            part = imag[32 * group : 32 * group + 32]
            tail = jnp.where(
                narrow < 32 * group, tail, pltpu.roll(part, step, 1) if step else part
            )
        return wide.astype(BF), tail.astype(BF), sample_rows[:, lanes].astype(BF)

    to_right = message(3, 1, (48, 96, 0))
    to_left = message(0, 0, (0, 48, 96))
    rg_odd = lax.axis_index("rg") % 2 == 1

    def send(target, parts):
        target[0:128], target[128:160], target[160:176] = parts

    @pl.when(rg_odd)
    def _():
        send(send_first, to_left)
        send(send_second, to_right)

    @pl.when(jnp.logical_not(rg_odd))
    def _():
        send(send_first, to_right)
        send(send_second, to_left)


def interior_body(resampled, master, column_high, column_low, middle, forward, lines, inverse,
                  samples, out):
    tiles = tiles_of(master)
    upper_high, upper_low, lower_high, lower_low = [], [], [], []
    for j in range(1, 8):
        around = shifted(tiles, 64 * j - 32)
        values = resampled.at[j - 1]
        real, imag = sample_columns(
            jnp.concatenate([values[0:32], values[96:128]], axis=0),
            jnp.concatenate([values[128:160], values[224:256]], axis=0),
            around[:64], around[64:], forward[...],
        )
        real, imag = split(real), split(imag)
        for which, own, upper, lower in (
            (0, column_high, upper_high, lower_high), (1, column_low, upper_low, lower_low)
        ):
            held = own.at[j - 1]
            upper.append(jnp.concatenate(
                [real[which][:32], held[0:32], imag[which][:32], held[64:96]], axis=0))
            lower.append(jnp.concatenate(
                [held[32:64], real[which][32:], held[96:128], imag[which][32:]], axis=0))
    upper = filter_band(upper_high, upper_low, lines[...], inverse[64:128])
    lower = filter_band(lower_high, lower_low, lines[...], inverse[0:64])
    parts = []
    for j in range(1, 8):
        tops = middle[j - 1, 0:64] + upper[j - 1]
        bottoms = middle[j - 1, 64:128] + lower[j - 1]
        if j == 7:
            lane = lax.broadcasted_iota(jnp.int32, tops.shape, 1)
            tops = jnp.where(lane % 2 == 0, tops, 0.0)
            bottoms = jnp.where(lane % 2 == 0, bottoms, 0.0)
        parts.append(pair_rows(tops, bottoms))
    for block in range(4):
        used = [j for j in (2 * block, 2 * block + 1, 2 * block + 2) if 1 <= j <= 7]
        start = (used[0] - 2 * block) * 768
        values = dot(
            jnp.concatenate([parts[j - 1] for j in used], axis=1),
            samples[start : start + 768 * len(used)],
        )
        out[0, 0, :, block * 128 : block * 128 + 128] = values[:, :128]
        out[0, 1, :, block * 128 : block * 128 + 128] = values[:, 128:]


def edge_body(part, edges, master, around, sample_rows, first, second, forward, lines, inverse,
              samples, out, sides, sems):
    centre = pltpu.make_async_copy(
        part.at[:, :, :, 128:384], out.at[:, :, :, 128:384], sems.at[0]
    )
    centre.start()
    rg = lax.axis_index("rg")
    odd = rg % 2 == 1
    first_f = first[...].astype(F32)
    second_f = second[...].astype(F32)
    has_left = jnp.where(rg > 0, 1.0, 0.0).astype(F32)
    has_right = jnp.where(rg < lax.axis_size("rg") - 1, 1.0, 0.0).astype(F32)
    from_left = jnp.where(odd, first_f, second_f) * has_left
    from_right = jnp.where(odd, second_f, first_f) * has_right

    def turned(values, step):
        return pltpu.roll(values, step % 128, 1) if step % 128 else values

    def block(message, tile, edge, cuts, reverse):
        lanes = slice(tile * 128, tile * 128 + 128)

        def mixed(cut, halo, own):
            lane = lax.broadcasted_iota(jnp.int32, own.shape, 1)
            return jnp.where(lane >= cut if reverse else lane < cut, halo, own)

        row_turn, cell_turn = (80, 64) if reverse else (0, 0)
        own_row, own_cell = (80, 64) if reverse else (48, 32)
        rows = edges[:, edge * 128 : edge * 128 + 128].astype(F32)
        window = [
            mixed(cuts[0], turned(message[:128], row_turn - 48 * which),
                  turned(rows[which * 128 : which * 128 + 128], own_row))
            for which in range(2)
        ]
        own, far = master[:, lanes].astype(F32), around[:, lanes].astype(F32)
        real = jnp.concatenate([far[:32], own[:64], far[32:64]], axis=0)
        imag = jnp.concatenate([far[64:96], own[64:], far[96:]], axis=0)
        real = mixed(cuts[1], turned(message[:128], cell_turn - 96), turned(real, own_cell))
        tail = [turned(message[128:160], cell_turn - 32 * group) for group in range(4)]
        imag = mixed(cuts[1], jnp.concatenate(tail, axis=0), turned(imag, own_cell))
        sample = mixed(
            cuts[1], turned(message[160:176], 64 if reverse else 32),
            turned(sample_rows[:, lanes], own_cell),
        )
        matrix = band_matrix(sample, 128).astype(BF)
        values = dot(jnp.concatenate(window, axis=0).astype(BF), matrix)
        return sample_columns(values[:128], values[128:], real, imag, forward[...])

    columns = [
        block(from_left, 0, 0, (48, 32), False), block(from_right, 3, 1, (80, 64), True)
    ]
    bands = []
    for band, rows in ((0, slice(64, 128)), (1, slice(0, 128)), (2, slice(0, 64))):
        highs, lows = [], []
        for real, imag in columns:
            picked = slice(band * 32, band * 32 + 64)
            high, low = split(jnp.concatenate([real[picked], imag[picked]], axis=0))
            highs.append(high)
            lows.append(low)
        bands.append(filter_band(highs, lows, lines[...], inverse[rows]))
    for at, target in ((0, 0), (1, 3)):
        tops = bands[1][at][:64] + bands[0][at]
        bottoms = bands[1][at][64:] + bands[2][at]
        values = dot(pair_rows(tops, bottoms), samples[target * 768 : target * 768 + 768])
        lanes = slice(target * 128, target * 128 + 128)
        side = slice(at * 128, at * 128 + 128)
        sides[0, 0, :, side] = part[0, 0, :, lanes] + values[:, :128]
        sides[0, 1, :, side] = part[0, 1, :, lanes] + values[:, 128:]
    copies = [
        pltpu.make_async_copy(
            sides.at[:, :, :, at * 128 : at * 128 + 128],
            out.at[:, :, :, target * 128 : target * 128 + 128],
            sems.at[at + 1],
        )
        for at, target in ((0, 0), (1, 3))
    ]
    for copy in copies:
        copy.start()
    centre.wait()
    for copy in copies:
        copy.wait()


def call(name, body, outputs, scratch=(), hbm=0, cost=0, far_out=False):
    vmem = pl.BlockSpec(memory_space=pltpu.VMEM)
    far = pl.BlockSpec(memory_space=pltpu.HBM)
    return lambda *args: pl.pallas_call(
        body,
        name=name,
        out_shape=[jax.ShapeDtypeStruct(shape, kind) for shape, kind in outputs],
        in_specs=[far] * hbm + [vmem] * (len(args) - hbm),
        out_specs=[far if far_out else vmem] * len(outputs),
        scratch_shapes=list(scratch),
        compiler_params=pltpu.CompilerParams(vmem_limit_bytes=VMEM_LIMIT),
        cost_estimate=pl.CostEstimate(flops=cost, bytes_accessed=cost // 100, transcendentals=0),
    )(*args)


def exchange(first, second, axis):
    size = lax.axis_size(axis)
    dates = lax.axis_size("date")
    pairs = []
    for date in range(dates):
        for i in range(size):
            partner = (date, i + 1 if i % 2 == 1 else i - 1)
            if i in (0, size - 1):
                partner = (date ^ 1, i)
            pairs.append((date * size + i, partner[0] * size + partner[1]))
    received_first = lax.ppermute(first, axis, [(i, i ^ 1) for i in range(size)])
    received_second = lax.ppermute(second, ("date", axis), pairs)
    return received_first, received_second


def date_swap(values, k):
    return lax.ppermute(values, "date", [(i, i ^ k) for i in range(4)])


def on_device(reference_slab, secondary, az_shift, az_fraction, rg_shift, rg_fraction):
    own = reference_slab.reshape(2, LINES_DEV, 128)
    message = ((464, 128), BF)
    lead = call("lead", lead_body, [((16, 128), F32)], cost=2 * 10**9)()[0]
    first, second, line_rows = call(
        "pack", pack_body, [message, message, ((16, 128), F32)],
        cost=10**9,
    )(secondary, own, az_shift, az_fraction, lead)
    tables = [jnp.asarray(table) for table in filter_tables()]
    prepared = call(
        "prepare", prepare_body,
        [((1, 2, LINES_DEV, 512), BF), ((2, LINES_DEV, 128), BF), ((16, 512), F32), ((7, 128, 128), BF)]
        + [(table.shape, BF) for table in tables],
        [pltpu.VMEM((1, 512), jnp.int32), pltpu.VMEM((1, 512), F32), pltpu.SemaphoreType.DMA((8,))],
        hbm=8, cost=2 * 10**9,
    )(secondary, own, rg_shift, rg_fraction, *tables)
    secondary_v, own_v, sample_rows, bands = prepared[:4]
    tables_v = prepared[4:]
    first, second = exchange(first, second, "az")
    peers = [date_swap(own_v, k) for k in (1, 2, 3)]
    halo = jnp.concatenate([first[384:448], second[384:448]], axis=0)
    halo2, halo3 = [date_swap(halo, k) for k in (2, 3)]
    edges, resampled, late = call(
        "lines", lines_body, [((256, 256), BF), ((7, 256, 128), F32), ((128, 128), BF)],
        [pltpu.VMEM((2, 160, 512), BF), pltpu.VMEM((2, 16, 128), F32)],
        cost=10**9,
    )(secondary_v, line_rows, first, second, bands)
    halo1 = date_swap(late, 1)
    columns = ((7, 128, 128), BF)
    master, column_high, column_low, middle = call(
        "early", early_body, [((128, 512), BF), columns, columns, ((7, 128, 128), F32)],
        cost=2 * 10**9,
    )(own_v, *peers, resampled, *tables_v[:3])
    message = ((176, 128), BF)
    around, first, second = call(
        "reference", reference_body, [((128, 512), BF), message, message], cost=10**8
    )(halo, halo1, halo2, halo3, master, edges, sample_rows)
    first, second = exchange(first, second, "rg")
    whole = ((1, 2, LINES_DEV, SAMPLES_DEV), F32)
    part = call("interior", interior_body, [whole], cost=4 * 10**9)(
        resampled, around, column_high, column_low, middle, *tables_v
    )[0]
    return call(
        "edge", edge_body, [whole],
        [pltpu.VMEM((1, 2, LINES_DEV, 256), F32), pltpu.SemaphoreType.DMA((3,))],
        cost=10**9, far_out=True,
    )(part, edges, master, around, sample_rows, first, second, *tables_v)[0]


def solution(mesh):
    in_specs = (
        P(None, "az", "rg", "date"),
        P("date", None, "az", "rg"),
        P("date", "az"),
        P("date", "az"),
        P("date", "rg"),
        P("date", "rg"),
    )
    out_specs = P("date", None, "az", "rg")
    return jax.shard_map(
        on_device, mesh=mesh, in_specs=in_specs, out_specs=out_specs, check_vma=False
    )
```

```python
import functools

import jax
import jax.numpy as jnp
import ml_dtypes
import numpy as np
from jax import lax
from jax.experimental import pallas as pl
from jax.experimental.pallas import tpu as pltpu
from jax.sharding import PartitionSpec as P

PATCH = 64
HALF = 32
TAPS = 8
MARGIN = 48
LINES_DEV = 64
SAMPLES_DEV = 512
BF = jnp.bfloat16
F32 = jnp.float32
VMEM_LIMIT = 32 * 1024 * 1024


def split_table(table):
    high = table.astype(ml_dtypes.bfloat16)
    low = (table - high.astype(np.float64)).astype(ml_dtypes.bfloat16)
    return high, low


def hann(position):
    return np.minimum(position + 0.5, PATCH - 0.5 - position) / HALF


def sample_forward():
    table = np.zeros((2, 128, 2, 64, 2))
    v = np.arange(64)
    for p in range(2):
        for m in range(64):
            angle = 2 * np.pi * ((v * m) % 64) / 64
            n = m + 32 * p
            table[0, n, 0, :, p] = np.cos(angle)
            table[1, n, 0, :, p] = np.sin(angle)
            table[0, n, 1, :, p] = -np.sin(angle)
            table[1, n, 1, :, p] = np.cos(angle)
    return table.reshape(256, 256)


def line_forward():
    table = np.zeros((2, 64, 2, 64))
    u = np.arange(64)
    for m in range(64):
        angle = 2 * np.pi * ((u * m) % 64) / 64
        table[0, :, 0, m] = np.cos(angle)
        table[0, :, 1, m] = np.sin(angle)
        table[1, :, 0, m] = -np.sin(angle)
        table[1, :, 1, m] = np.cos(angle)
    return table.reshape(128, 128)


def line_bands():
    small = line_forward().reshape(2, 64, 2, 64)
    table = np.zeros((3, 2, 64, 2, 128))
    for band in range(3):
        table[band, :, :, :, 32 * band : 32 * band + 64] = small
    return table.reshape(384, 256)


def line_inverse():
    table = np.zeros((2, 2, 32, 2, 64))
    u = np.arange(64)
    for m in range(64):
        angle = 2 * np.pi * ((u * m) % 64) / 64
        weight = hann(m) / 64
        table[m // 32, 0, m % 32, 0, :] = weight * np.cos(angle)
        table[m // 32, 0, m % 32, 1, :] = -weight * np.sin(angle)
        table[m // 32, 1, m % 32, 0, :] = weight * np.sin(angle)
        table[m // 32, 1, m % 32, 1, :] = weight * np.cos(angle)
    return table.reshape(128, 128)


def sample_inverse(start):
    table = np.zeros((2, 64, 2, 2, 128))
    v = np.arange(64)
    for p in range(2):
        for y in range(128):
            n = 32 + y - start - 32 * p
            if 0 <= n < 64:
                angle = 2 * np.pi * ((v * n) % 64) / 64
                weight = hann(n) / 64
                table[0, :, p, 0, y] = weight * np.cos(angle)
                table[1, :, p, 0, y] = -weight * np.sin(angle)
                table[0, :, p, 1, y] = weight * np.sin(angle)
                table[1, :, p, 1, y] = weight * np.cos(angle)
    return table.reshape(256, 256)


def triple(table, axis):
    high, low = split_table(table)
    return np.concatenate([high, high, low], axis=axis)


def filter_tables():
    inverse = [sample_inverse(start) for start in (0, 64, 128)]
    inverse.append(inverse[0] + sample_inverse(96))
    return [
        triple(sample_forward(), 0),
        triple(line_bands(), 1),
        triple(line_inverse(), 1),
        np.concatenate([triple(table, 0) for table in inverse], axis=0),
    ]


def sinc_rows(fraction):
    tap = lax.broadcasted_iota(jnp.int32, (TAPS, fraction.shape[1]), 0)
    distance = fraction - (tap - (TAPS // 2 - 1)).astype(F32)
    centre = distance == 0.0
    sign = jnp.where(tap % 2 == 1, 1.0, -1.0)
    wave = sign * jnp.sin(np.float32(np.pi) * fraction)
    sinc = wave / jnp.where(centre, 1.0, np.float32(np.pi) * distance)
    sinc = jnp.where(centre, 1.0, sinc)
    taper = 0.5 + 0.5 * jnp.cos(np.float32(np.pi) * distance / (TAPS // 2))
    return (sinc * taper).astype(BF).astype(F32)


def kernel_rows(shift, fraction):
    weights = sinc_rows(fraction)
    row = lax.broadcasted_iota(jnp.int32, weights.shape, 0)
    shifts = jnp.where(row == 0, shift.astype(F32), 0.0)
    return jnp.concatenate([weights, shifts], axis=0)


def band_matrix(rows, depth):
    width = rows.shape[1]
    shift = rows[TAPS : TAPS + 1].astype(jnp.int32)
    source = lax.broadcasted_iota(jnp.int32, (depth, width), 0)
    target = lax.broadcasted_iota(jnp.int32, (depth, width), 1)
    step = source - (target + 13 + shift)
    matrix = jnp.zeros((depth, width), F32)
    for k in range(TAPS):
        matrix = jnp.where(step == k, rows[k : k + 1], matrix)
    return matrix


def split(values):
    high = values.astype(BF)
    return high, (values - high.astype(F32)).astype(BF)


def dot(left, right):
    return jnp.dot(left, right, preferred_element_type=F32)


def columns_triple(values):
    high, low = split(values)
    return jnp.concatenate([high, low, high], axis=1)


def rows_triple(values):
    high, low = split(values)
    return jnp.concatenate([high, low, high], axis=0)


def shifted(tiles, start):
    index, offset = start // 128, start % 128
    here = pltpu.roll(tiles[index], 128 - offset, 1)
    after = pltpu.roll(tiles[min(index + 1, 3)], 128 - offset, 1)
    lane = lax.broadcasted_iota(jnp.int32, here.shape, 1)
    return jnp.where(lane < 128 - offset, here, after)


def tiles_of(values):
    return [values[:, t * 128 : t * 128 + 128].astype(F32) for t in range(4)]


def lead_body(out):
    out[...] = jnp.zeros_like(out)


def pack_body(secondary, own, shift, fraction, lead, first, second, line_rows):
    odd = lax.axis_index("az") % 2 == 1

    def fill(message, line, half):
        for part in range(2):
            for tile in range(4):
                rows = slice((2 * tile + part) * 48, (2 * tile + part) * 48 + 48)
                message[rows] = secondary[0, part, line : line + 48, tile * 128 : tile * 128 + 128]
            message[384 + part * 32 : 416 + part * 32] = own[part, half : half + 32]

    @pl.when(odd)
    def _():
        fill(first, 0, 0)
        fill(second, 16, 32)

    @pl.when(jnp.logical_not(odd))
    def _():
        fill(first, 16, 32)
        fill(second, 0, 0)

    row_shift = jnp.concatenate([shift[...], shift[...]], axis=1)
    row_fraction = jnp.concatenate([fraction[...], fraction[...]], axis=1)
    rows = kernel_rows(pltpu.roll(row_shift, 32, 1), pltpu.roll(row_fraction, 32, 1)) + lead[...]
    line_rows[...] = rows
    first[448:464] = rows.astype(BF)
    second[448:464] = rows.astype(BF)


def cross_pack_body(first, second, own, cross_first, cross_second, own_v):
    own_v[...] = own[...]
    cross_first[...] = first[384:448]
    cross_second[...] = second[384:448]


def core_pack_body(own, piece, first, second, cross_first, cross_second, after, message):
    del after
    for part in range(2):
        message[part * 64 : part * 64 + 64] = own[part]
        message[256 + part * 64 : 320 + part * 64] = piece[part]
    message[128:192] = first[384:448]
    message[192:256] = second[384:448]
    message[384:448] = cross_first[...]
    message[448:512] = cross_second[...]


def prepare_body(secondary, shift, fraction, after, secondary_v, sample_rows, bands,
                 shift_v, fraction_v, sems):
    del after
    pairs = [(shift, shift_v), (fraction, fraction_v), (secondary, secondary_v)]
    copies = [
        pltpu.make_async_copy(source, target, sems.at[at]) for at, (source, target) in enumerate(pairs)
    ]
    for copy in copies:
        copy.start()
    for copy in copies[:2]:
        copy.wait()
    samples = kernel_rows(shift_v[...], fraction_v[...])
    sample_rows[...] = samples
    tiles = tiles_of(samples)
    for j in range(1, 8):
        bands[j - 1] = band_matrix(shifted(tiles, 64 * j - 32), 128).astype(BF)
    for copy in copies[2:]:
        copy.wait()


def lines_body(secondary, line_rows, first, second, bands, edges, resampled, extended, halo_rows):
    odd = lax.axis_index("az") % 2 == 1
    has_top = lax.axis_index("az") > 0
    has_bottom = lax.axis_index("az") < lax.axis_size("az") - 1

    def place(top, bottom):
        for part in range(2):
            for tile in range(4):
                rows = slice((2 * tile + part) * 48, (2 * tile + part) * 48 + 48)
                lanes = slice(tile * 128, tile * 128 + 128)
                extended[part, 0:48, lanes] = top[rows]
                extended[part, 112:160, lanes] = bottom[rows]
        halo_rows[0] = top[448:464].astype(F32)
        halo_rows[1] = bottom[448:464].astype(F32)

    @pl.when(odd)
    def _():
        place(first, second)

    @pl.when(jnp.logical_not(odd))
    def _():
        place(second, first)

    for part in range(2):
        extended[part, 48:112] = secondary[0, part]

    lane = lax.broadcasted_iota(jnp.int32, (16, 128), 1)
    rows = jnp.where(
        lane < 32,
        pltpu.roll(halo_rows[0], 64, 1),
        jnp.where(lane < 96, line_rows[...], pltpu.roll(halo_rows[1], 64, 1)),
    )
    matrix = band_matrix(rows, 160)
    line = lax.broadcasted_iota(jnp.int32, matrix.shape, 0)
    low = jnp.where(has_top, 0, 48)
    high = jnp.where(has_bottom, 160, 112)
    matrix = jnp.where((line >= low) & (line < high), matrix, 0.0).astype(BF)
    values = [
        lax.dot_general(
            matrix, extended[part], (((0,), (0,)), ((), ())), preferred_element_type=F32
        )
        for part in range(2)
    ]
    values = jnp.concatenate(values, axis=0).astype(BF)
    edges[:, 0:128] = values[:, 0:128]
    edges[:, 128:256] = values[:, 384:512]
    tiles = tiles_of(values)
    for j in range(1, 8):
        resampled[j - 1] = dot(shifted(tiles, 64 * j - 48).astype(BF), bands[j - 1])


def by_date(pieces, store):
    date = lax.axis_index("date")
    for value in range(4):

        @pl.when(date == value)
        def _():
            for offset in range(4):
                place = (value ^ offset) * 128
                store(pieces[offset], slice(place, place + 128))


def root(values):
    return values * lax.rsqrt(jnp.maximum(values, np.float32(1e-36)))


def cross_product(real, imag, master_real, master_imag):
    return jnp.concatenate(
        [master_real * real + master_imag * imag, master_imag * real - master_real * imag], axis=1
    )


def sample_columns(products, forward):
    result = []
    for product in products:
        columns = dot(columns_triple(product), forward)
        result.append((split(columns[:, :128]), split(columns[:, 128:])))
    return result


def response_of(spectrum):
    real, imag = spectrum[:64], spectrum[64:]
    smooth = root(real * real + imag * imag)
    smooth = smooth + pltpu.roll(smooth, 2, 1) + pltpu.roll(smooth, 126, 1)
    smooth = smooth + pltpu.roll(smooth, 1, 0) + pltpu.roll(smooth, 63, 0)
    return root(smooth)


def window_scales(responses):
    sums = jnp.concatenate(
        [jnp.sum(values.reshape(8, 8, 128), axis=0) for values in responses], axis=0
    )
    high, low = split(sums)
    row = lax.broadcasted_iota(jnp.int32, (256, 128), 0)
    lane = lax.broadcasted_iota(jnp.int32, (256, 128), 1)
    same = jnp.where((row - lane) % 2 == 0, 1.0, 0.0).astype(BF)
    totals = dot(jnp.concatenate([high, low], axis=1), same)
    scales = []
    for at in range(len(responses)):
        total = jnp.sum(totals[8 * at : 8 * at + 8], axis=0, keepdims=True)
        scales.append(1.0 / (total * np.float32(1 / 4096) + np.float32(3e-06)))
    return scales


def filter_band(spectra, inverse):
    responses = [response_of(values) for values in spectra]
    gained = [
        rows_triple(values * jnp.concatenate([response, response], axis=0))
        for values, response in zip(spectra, responses)
    ]
    back = dot(inverse, jnp.concatenate(gained, axis=1))
    scales = window_scales(responses)
    return [
        back[:, at * 128 : at * 128 + 128] * scales[at] for at in range(len(spectra))
    ]


def pair_rows(top, bottom):
    real = jnp.concatenate([top[:32], bottom[:32]], axis=0)
    imag = jnp.concatenate([top[32:], bottom[32:]], axis=0)
    return columns_triple(jnp.concatenate([real, imag], axis=1))


def reference_body(own, peer2, core, first, second, cross_first, cross_second, edges,
                   sample_rows, master, send_first, send_second):
    az = lax.axis_index("az")
    odd = az % 2 == 1
    pieces = (
        (own.at[0], own.at[1]), (core.at[0:64], core.at[64:128]),
        (peer2.at[0], peer2.at[1]), (core.at[256:320], core.at[320:384]),
    )
    halos = (
        (first.at[384:448], second.at[384:448]),
        (core.at[128:192], core.at[192:256]),
        (cross_first, cross_second),
        (core.at[384:448], core.at[448:512]),
    )

    def store(piece, lanes):
        middle, halo = piece
        for part in range(2):
            master[part * 128 + 32 : part * 128 + 96, lanes] = middle[part][...]

        def place(top, bottom):
            for part in range(2):
                rows = slice(part * 32, part * 32 + 32)
                master[part * 128 : part * 128 + 32, lanes] = top[rows]
                master[part * 128 + 96 : part * 128 + 128, lanes] = bottom[rows]

        @pl.when(odd)
        def _():
            place(*halo)

        @pl.when(jnp.logical_not(odd))
        def _():
            place(*halo[::-1])

    by_date(list(zip(pieces, halos)), store)

    @pl.when(az == 0)
    def _():
        for part in range(2):
            master[part * 128 : part * 128 + 32] = jnp.zeros((32, 512), BF)

    @pl.when(az == lax.axis_size("az") - 1)
    def _():
        for part in range(2):
            master[part * 128 + 96 : part * 128 + 128] = jnp.zeros((32, 512), BF)

    lane = lax.broadcasted_iota(jnp.int32, (128, 128), 1)
    narrow = lax.broadcasted_iota(jnp.int32, (32, 128), 1)

    def message(tile, edge, turn):
        lanes = slice(tile * 128, tile * 128 + 128)
        rows = edges[:, edge * 128 : edge * 128 + 128].astype(F32)
        cells = master[:, lanes].astype(F32)
        real, imag = cells[:128], cells[128:]
        wide = jnp.where(
            lane < 48,
            pltpu.roll(rows[:128], turn[0], 1) if turn[0] else rows[:128],
            jnp.where(
                lane < 96,
                pltpu.roll(rows[128:], turn[1], 1),
                pltpu.roll(real, turn[2], 1) if turn[2] else real,
            ),
        )
        tail = pltpu.roll(imag[:32], (turn[2] + 32) % 128, 1)
        for group in range(1, 4):
            step = (turn[2] + 32 + 32 * group) % 128
            part = imag[32 * group : 32 * group + 32]
            tail = jnp.where(
                narrow < 32 * group, tail, pltpu.roll(part, step, 1) if step else part
            )
        return wide.astype(BF), tail.astype(BF), sample_rows[:, lanes].astype(BF)

    to_right = message(3, 1, (48, 96, 0))
    to_left = message(0, 0, (0, 48, 96))
    rg_odd = lax.axis_index("rg") % 2 == 1

    def send(target, parts):
        target[0:128], target[128:160], target[160:176] = parts

    @pl.when(rg_odd)
    def _():
        send(send_first, to_left)
        send(send_second, to_right)

    @pl.when(jnp.logical_not(rg_odd))
    def _():
        send(send_first, to_right)
        send(send_second, to_left)


def filter_columns(columns, lines, inverse):
    stacked = [
        jnp.concatenate([real[0], imag[0], real[1], imag[1], real[0], imag[0]], axis=0)
        for real, imag in columns
    ]
    spectrum = dot(lines[...], jnp.concatenate(stacked, axis=1))
    bands = []
    for band, rows in ((0, slice(64, 128)), (1, slice(0, 128)), (2, slice(0, 64))):
        spectra = [
            spectrum[band * 128 : band * 128 + 128, at * 128 : at * 128 + 128]
            for at in range(len(columns))
        ]
        bands.append(filter_band(spectra, inverse[rows]))
    return [
        (middle[:64] + upper, middle[64:] + lower)
        for upper, middle, lower in zip(*bands)
    ]


def interior_body(resampled, master, forward, lines, inverse, samples, out):
    tiles = tiles_of(master)
    products = []
    for j in range(1, 8):
        around = shifted(tiles, 64 * j - 32)
        values = resampled.at[j - 1]
        products.append(cross_product(values[:128], values[128:], around[:128], around[128:]))
    columns = sample_columns(products, forward[...])
    parts = []
    for j, (tops, bottoms) in enumerate(filter_columns(columns, lines, inverse), 1):
        if j == 7:
            lane = lax.broadcasted_iota(jnp.int32, tops.shape, 1)
            tops = jnp.where(lane % 2 == 0, tops, 0.0)
            bottoms = jnp.where(lane % 2 == 0, bottoms, 0.0)
        parts.append(pair_rows(tops, bottoms))
    for block in range(4):
        used = [j for j in (2 * block, 2 * block + 1, 2 * block + 2) if 1 <= j <= 7]
        start = (used[0] - 2 * block) * 768
        values = dot(
            jnp.concatenate([parts[j - 1] for j in used], axis=1),
            samples[start : start + 768 * len(used)],
        )
        out[0, 0, :, block * 128 : block * 128 + 128] = values[:, :128]
        out[0, 1, :, block * 128 : block * 128 + 128] = values[:, 128:]


def edge_body(part, edges, master, sample_rows, first, second, forward, lines, inverse,
              samples, out, sides, sems):
    centre = pltpu.make_async_copy(
        part.at[:, :, :, 128:384], out.at[:, :, :, 128:384], sems.at[0]
    )
    centre.start()
    rg = lax.axis_index("rg")
    odd = rg % 2 == 1
    first_f = first[...].astype(F32)
    second_f = second[...].astype(F32)
    has_left = jnp.where(rg > 0, 1.0, 0.0).astype(F32)
    has_right = jnp.where(rg < lax.axis_size("rg") - 1, 1.0, 0.0).astype(F32)
    from_left = jnp.where(odd, first_f, second_f) * has_left
    from_right = jnp.where(odd, second_f, first_f) * has_right

    def turned(values, step):
        return pltpu.roll(values, step % 128, 1) if step % 128 else values

    def block(message, tile, edge, cuts, reverse):
        lanes = slice(tile * 128, tile * 128 + 128)

        def mixed(cut, halo, own):
            lane = lax.broadcasted_iota(jnp.int32, own.shape, 1)
            return jnp.where(lane >= cut if reverse else lane < cut, halo, own)

        row_turn, cell_turn = (80, 64) if reverse else (0, 0)
        own_row, own_cell = (80, 64) if reverse else (48, 32)
        rows = edges[:, edge * 128 : edge * 128 + 128].astype(F32)
        window = [
            mixed(cuts[0], turned(message[:128], row_turn - 48 * which),
                  turned(rows[which * 128 : which * 128 + 128], own_row))
            for which in range(2)
        ]
        cells = master[:, lanes].astype(F32)
        real, imag = cells[:128], cells[128:]
        real = mixed(cuts[1], turned(message[:128], cell_turn - 96), turned(real, own_cell))
        tail = [turned(message[128:160], cell_turn - 32 * group) for group in range(4)]
        imag = mixed(cuts[1], jnp.concatenate(tail, axis=0), turned(imag, own_cell))
        sample = mixed(
            cuts[1], turned(message[160:176], 64 if reverse else 32),
            turned(sample_rows[:, lanes], own_cell),
        )
        matrix = band_matrix(sample, 128).astype(BF)
        values = dot(jnp.concatenate(window, axis=0).astype(BF), matrix)
        return cross_product(values[:128], values[128:], real, imag)

    products = [
        block(from_left, 0, 0, (48, 32), False), block(from_right, 3, 1, (80, 64), True)
    ]
    results = filter_columns(sample_columns(products, forward[...]), lines, inverse)
    rows = jnp.concatenate([pair_rows(tops, bottoms) for tops, bottoms in results], axis=0)
    values = dot(rows, samples[2304:3072])
    lane = lax.broadcasted_iota(jnp.int32, (64, 128), 1)
    for at, target in ((0, 0), (1, 3)):
        lanes = slice(target * 128, target * 128 + 128)
        side = slice(at * 128, at * 128 + 128)
        kept = (lane < 64) if at == 0 else (lane >= 64)
        for which in range(2):
            found = values[at * 64 : at * 64 + 64, which * 128 : which * 128 + 128]
            sides[0, which, :, side] = part[0, which, :, lanes] + jnp.where(kept, found, 0.0)
    copies = [
        pltpu.make_async_copy(
            sides.at[:, :, :, at * 128 : at * 128 + 128],
            out.at[:, :, :, target * 128 : target * 128 + 128],
            sems.at[at + 1],
        )
        for at, target in ((0, 0), (1, 3))
    ]
    for copy in copies:
        copy.start()
    centre.wait()
    for copy in copies:
        copy.wait()


def call(name, body, outputs, scratch=(), hbm=0, cost=0, far_out=False):
    vmem = pl.BlockSpec(memory_space=pltpu.VMEM)
    far = pl.BlockSpec(memory_space=pltpu.HBM)
    return lambda *args: pl.pallas_call(
        body,
        name=name,
        out_shape=[jax.ShapeDtypeStruct(shape, kind) for shape, kind in outputs],
        in_specs=[far] * hbm + [vmem] * (len(args) - hbm),
        out_specs=[far if far_out else vmem] * len(outputs),
        scratch_shapes=list(scratch),
        compiler_params=pltpu.CompilerParams(vmem_limit_bytes=VMEM_LIMIT),
        cost_estimate=pl.CostEstimate(flops=cost, bytes_accessed=cost // 100, transcendentals=0),
    )(*args)


def exchange(first, second, axis, turn=0):
    size = lax.axis_size(axis)
    dates = lax.axis_size("date")
    pairs = []
    for date in range(dates):
        for i in range(size):
            partner = (date ^ turn, i + 1 if i % 2 == 1 else i - 1)
            if i in (0, size - 1):
                partner = (date ^ 1, i)
            pairs.append((date * size + i, partner[0] * size + partner[1]))
    near = [
        (date * size + i, (date ^ turn) * size + (i ^ 1)) for date in range(dates) for i in range(size)
    ]
    received_first = lax.ppermute(first, ("date", axis), near)
    received_second = lax.ppermute(second, ("date", axis), pairs)
    return received_first, received_second


def date_swap(values, k):
    return lax.ppermute(values, "date", [(i, i ^ k) for i in range(4)])


def on_device(reference_slab, secondary, az_shift, az_fraction, rg_shift, rg_fraction):
    own = reference_slab.reshape(2, LINES_DEV, 128)
    message = ((464, 128), BF)
    lead = call("lead", lead_body, [((16, 128), F32)], cost=2 * 10**9)()[0]
    first, second, line_rows = call(
        "pack", pack_body, [message, message, ((16, 128), F32)],
        cost=10**9,
    )(secondary, own, az_shift, az_fraction, lead)
    half = ((64, 128), BF)
    cross_first, cross_second, own_v = call(
        "cross_pack", cross_pack_body, [half, half, ((2, LINES_DEV, 128), BF)], cost=2 * 10**9
    )(first, second, own)
    first, second = exchange(first, second, "az")
    tables = [jnp.asarray(table) for table in filter_tables()]
    prepared = call(
        "prepare", prepare_body,
        [((1, 2, LINES_DEV, 512), BF), ((16, 512), F32), ((7, 128, 128), BF)],
        [pltpu.VMEM((1, 512), jnp.int32), pltpu.VMEM((1, 512), F32), pltpu.SemaphoreType.DMA((3,))],
        hbm=3, cost=2 * 10**9,
    )(secondary, rg_shift, rg_fraction, cross_first)
    secondary_v, sample_rows, bands = prepared
    cross_first, cross_second = exchange(cross_first, cross_second, "az", 2)
    peer2 = date_swap(own_v, 2)
    edges, resampled = call(
        "lines", lines_body, [((256, 256), BF), ((7, 256, 128), F32)],
        [pltpu.VMEM((2, 160, 512), BF), pltpu.VMEM((2, 16, 128), F32)],
        cost=10**9,
    )(secondary_v, line_rows, first, second, bands)
    core = call("core_pack", core_pack_body, [((512, 128), BF)], cost=10**7)(
        own_v, peer2, first, second, cross_first, cross_second, edges
    )[0]
    core = date_swap(core, 1)
    message = ((176, 128), BF)
    master, first, second = call(
        "reference", reference_body, [((256, 512), BF), message, message], cost=10**8
    )(own_v, peer2, core, first, second, cross_first, cross_second, edges, sample_rows)
    first, second = exchange(first, second, "rg")
    whole = ((1, 2, LINES_DEV, SAMPLES_DEV), F32)
    part = call("interior", interior_body, [whole], cost=4 * 10**9)(
        resampled, master, *tables
    )[0]
    return call(
        "edge", edge_body, [whole],
        [pltpu.VMEM((1, 2, LINES_DEV, 256), F32), pltpu.SemaphoreType.DMA((3,))],
        cost=10**9, far_out=True,
    )(part, edges, master, sample_rows, first, second, *tables)[0]


def solution(mesh):
    in_specs = (
        P(None, "az", "rg", "date"),
        P("date", None, "az", "rg"),
        P("date", "az"),
        P("date", "az"),
        P("date", "rg"),
        P("date", "rg"),
    )
    out_specs = P("date", None, "az", "rg")
    return jax.shard_map(
        on_device, mesh=mesh, in_specs=in_specs, out_specs=out_specs, check_vma=False
    )
```

```python
import functools

import jax
import jax.numpy as jnp
import ml_dtypes
import numpy as np
from jax import lax
from jax.experimental import pallas as pl
from jax.experimental.pallas import tpu as pltpu
from jax.sharding import PartitionSpec as P

PATCH = 64
HALF = 32
TAPS = 8
MARGIN = 48
LINES_DEV = 64
SAMPLES_DEV = 512
BF = jnp.bfloat16
F32 = jnp.float32
VMEM_LIMIT = 32 * 1024 * 1024


def split_table(table):
    high = table.astype(ml_dtypes.bfloat16)
    low = (table - high.astype(np.float64)).astype(ml_dtypes.bfloat16)
    return high, low


def hann(position):
    return np.minimum(position + 0.5, PATCH - 0.5 - position) / HALF


def sample_forward():
    table = np.zeros((2, 128, 2, 64, 2))
    v = np.arange(64)
    for p in range(2):
        for m in range(64):
            angle = 2 * np.pi * ((v * m) % 64) / 64
            n = m + 32 * p
            table[0, n, 0, :, p] = np.cos(angle)
            table[1, n, 0, :, p] = np.sin(angle)
            table[0, n, 1, :, p] = -np.sin(angle)
            table[1, n, 1, :, p] = np.cos(angle)
    return table.reshape(256, 256)


def line_forward():
    table = np.zeros((2, 64, 2, 64))
    u = np.arange(64)
    for m in range(64):
        angle = 2 * np.pi * ((u * m) % 64) / 64
        table[0, :, 0, m] = np.cos(angle)
        table[0, :, 1, m] = np.sin(angle)
        table[1, :, 0, m] = -np.sin(angle)
        table[1, :, 1, m] = np.cos(angle)
    return table.reshape(128, 128)


def line_bands():
    small = line_forward().reshape(2, 64, 2, 64)
    table = np.zeros((3, 2, 64, 2, 128))
    for band in range(3):
        table[band, :, :, :, 32 * band : 32 * band + 64] = small
    return table.reshape(384, 256)


def line_inverse():
    table = np.zeros((2, 2, 32, 2, 64))
    u = np.arange(64)
    for m in range(64):
        angle = 2 * np.pi * ((u * m) % 64) / 64
        weight = hann(m) / 64
        table[m // 32, 0, m % 32, 0, :] = weight * np.cos(angle)
        table[m // 32, 0, m % 32, 1, :] = -weight * np.sin(angle)
        table[m // 32, 1, m % 32, 0, :] = weight * np.sin(angle)
        table[m // 32, 1, m % 32, 1, :] = weight * np.cos(angle)
    return table.reshape(128, 128)


def sample_inverse(start):
    table = np.zeros((2, 64, 2, 2, 128))
    v = np.arange(64)
    for p in range(2):
        for y in range(128):
            n = 32 + y - start - 32 * p
            if 0 <= n < 64:
                angle = 2 * np.pi * ((v * n) % 64) / 64
                weight = hann(n) / 64
                table[0, :, p, 0, y] = weight * np.cos(angle)
                table[1, :, p, 0, y] = -weight * np.sin(angle)
                table[0, :, p, 1, y] = weight * np.sin(angle)
                table[1, :, p, 1, y] = weight * np.cos(angle)
    return table.reshape(256, 256)


def triple(table, axis):
    high, low = split_table(table)
    return np.concatenate([high, high, low], axis=axis)


def filter_tables():
    inverse = [sample_inverse(start) for start in (0, 64, 128)]
    inverse.append(inverse[0] + sample_inverse(96))
    return [
        triple(sample_forward(), 0),
        triple(line_bands(), 1),
        triple(line_inverse(), 1),
        np.concatenate([triple(table, 0) for table in inverse], axis=0),
    ]


def sinc_rows(fraction):
    tap = lax.broadcasted_iota(jnp.int32, (TAPS, fraction.shape[1]), 0)
    distance = fraction - (tap - (TAPS // 2 - 1)).astype(F32)
    centre = distance == 0.0
    sign = jnp.where(tap % 2 == 1, 1.0, -1.0)
    wave = sign * jnp.sin(np.float32(np.pi) * fraction)
    sinc = wave / jnp.where(centre, 1.0, np.float32(np.pi) * distance)
    sinc = jnp.where(centre, 1.0, sinc)
    taper = 0.5 + 0.5 * jnp.cos(np.float32(np.pi) * distance / (TAPS // 2))
    return (sinc * taper).astype(BF).astype(F32)


def kernel_rows(shift, fraction):
    weights = sinc_rows(fraction)
    row = lax.broadcasted_iota(jnp.int32, weights.shape, 0)
    shifts = jnp.where(row == 0, shift.astype(F32), 0.0)
    return jnp.concatenate([weights, shifts], axis=0)


def band_matrix(rows, depth):
    width = rows.shape[1]
    shift = rows[TAPS : TAPS + 1].astype(jnp.int32)
    source = lax.broadcasted_iota(jnp.int32, (depth, width), 0)
    target = lax.broadcasted_iota(jnp.int32, (depth, width), 1)
    step = source - (target + 13 + shift)
    matrix = jnp.zeros((depth, width), F32)
    for k in range(TAPS):
        matrix = jnp.where(step == k, rows[k : k + 1], matrix)
    return matrix


def split(values):
    high = values.astype(BF)
    return high, (values - high.astype(F32)).astype(BF)


def dot(left, right):
    return jnp.dot(left, right, preferred_element_type=F32)


def columns_triple(values):
    high, low = split(values)
    return jnp.concatenate([high, low, high], axis=1)


def rows_triple(values):
    high, low = split(values)
    return jnp.concatenate([high, low, high], axis=0)


def shifted(tiles, start):
    index, offset = start // 128, start % 128
    here = pltpu.roll(tiles[index], 128 - offset, 1)
    after = pltpu.roll(tiles[min(index + 1, 3)], 128 - offset, 1)
    lane = lax.broadcasted_iota(jnp.int32, here.shape, 1)
    return jnp.where(lane < 128 - offset, here, after)


def tiles_of(values):
    return [values[:, t * 128 : t * 128 + 128].astype(F32) for t in range(4)]


def lead_body(out):
    out[...] = jnp.zeros_like(out)


def pack_body(secondary, own, shift, fraction, lead, first, second, line_rows):
    odd = lax.axis_index("az") % 2 == 1

    def fill(message, line, half):
        for part in range(2):
            for tile in range(4):
                rows = slice((2 * tile + part) * 48, (2 * tile + part) * 48 + 48)
                message[rows] = secondary[0, part, line : line + 48, tile * 128 : tile * 128 + 128]
            message[384 + part * 32 : 416 + part * 32] = own[part, half : half + 32]

    @pl.when(odd)
    def _():
        fill(first, 0, 0)
        fill(second, 16, 32)

    @pl.when(jnp.logical_not(odd))
    def _():
        fill(first, 16, 32)
        fill(second, 0, 0)

    row_shift = jnp.concatenate([shift[...], shift[...]], axis=1)
    row_fraction = jnp.concatenate([fraction[...], fraction[...]], axis=1)
    rows = kernel_rows(pltpu.roll(row_shift, 32, 1), pltpu.roll(row_fraction, 32, 1)) + lead[...]
    line_rows[...] = rows
    first[448:464] = rows.astype(BF)
    second[448:464] = rows.astype(BF)


def cross_pack_body(first, second, own, mate, message, own_v):
    own_v[...] = own[...]
    odd = lax.axis_index("az") % 2
    side = lax.axis_index("date") % 2

    @pl.when(side == 0)
    def _():
        message[0:64] = first[384:448]

    @pl.when(side == 1)
    def _():
        message[0:64] = second[384:448]

    def fill(half):
        for part in range(2):
            message[64 + part * 32 : 96 + part * 32] = mate[part, half : half + 32]

    @pl.when(odd != side)
    def _():
        fill(0)

    @pl.when(odd == side)
    def _():
        fill(32)


def core_pack_body(piece, cross, message):
    for part in range(2):
        message[part * 64 : part * 64 + 64] = piece[part]
    message[128:256] = cross[...]


def prepare_body(secondary, shift, fraction, after, secondary_v, sample_rows, bands,
                 shift_v, fraction_v, sems):
    del after
    pairs = [(shift, shift_v), (fraction, fraction_v), (secondary, secondary_v)]
    copies = [
        pltpu.make_async_copy(source, target, sems.at[at]) for at, (source, target) in enumerate(pairs)
    ]
    for copy in copies:
        copy.start()
    for copy in copies[:2]:
        copy.wait()
    samples = kernel_rows(shift_v[...], fraction_v[...])
    sample_rows[...] = samples
    tiles = tiles_of(samples)
    for j in range(1, 8):
        bands[j - 1] = band_matrix(shifted(tiles, 64 * j - 32), 128).astype(BF)
    for copy in copies[2:]:
        copy.wait()


def lines_body(secondary, line_rows, first, second, bands, edges, resampled, extended, halo_rows):
    odd = lax.axis_index("az") % 2 == 1
    has_top = lax.axis_index("az") > 0
    has_bottom = lax.axis_index("az") < lax.axis_size("az") - 1

    def place(top, bottom):
        for part in range(2):
            for tile in range(4):
                rows = slice((2 * tile + part) * 48, (2 * tile + part) * 48 + 48)
                lanes = slice(tile * 128, tile * 128 + 128)
                extended[part, 0:48, lanes] = top[rows]
                extended[part, 112:160, lanes] = bottom[rows]
        halo_rows[0] = top[448:464].astype(F32)
        halo_rows[1] = bottom[448:464].astype(F32)

    @pl.when(odd)
    def _():
        place(first, second)

    @pl.when(jnp.logical_not(odd))
    def _():
        place(second, first)

    for part in range(2):
        extended[part, 48:112] = secondary[0, part]

    lane = lax.broadcasted_iota(jnp.int32, (16, 128), 1)
    rows = jnp.where(
        lane < 32,
        pltpu.roll(halo_rows[0], 64, 1),
        jnp.where(lane < 96, line_rows[...], pltpu.roll(halo_rows[1], 64, 1)),
    )
    matrix = band_matrix(rows, 160)
    line = lax.broadcasted_iota(jnp.int32, matrix.shape, 0)
    low = jnp.where(has_top, 0, 48)
    high = jnp.where(has_bottom, 160, 112)
    matrix = jnp.where((line >= low) & (line < high), matrix, 0.0).astype(BF)
    values = [
        lax.dot_general(
            matrix, extended[part], (((0,), (0,)), ((), ())), preferred_element_type=F32
        )
        for part in range(2)
    ]
    values = jnp.concatenate(values, axis=0).astype(BF)
    edges[:, 0:128] = values[:, 0:128]
    edges[:, 128:256] = values[:, 384:512]
    tiles = tiles_of(values)
    for j in range(1, 8):
        resampled[j - 1] = dot(shifted(tiles, 64 * j - 48).astype(BF), bands[j - 1])


def by_date(pieces, store):
    date = lax.axis_index("date")
    for value in range(4):

        @pl.when(date == value)
        def _():
            for offset in range(4):
                place = (value ^ offset) * 128
                store(pieces[offset], slice(place, place + 128), value)


def root(values):
    return values * lax.rsqrt(jnp.maximum(values, np.float32(1e-36)))


def cross_product(real, imag, master_real, master_imag):
    return jnp.concatenate(
        [master_real * real + master_imag * imag, master_imag * real - master_real * imag], axis=1
    )


def sample_columns(products, forward):
    result = []
    for product in products:
        columns = dot(columns_triple(product), forward)
        result.append((split(columns[:, :128]), split(columns[:, 128:])))
    return result


def response_of(spectrum):
    real, imag = spectrum[:64], spectrum[64:]
    smooth = root(real * real + imag * imag)
    smooth = smooth + pltpu.roll(smooth, 2, 1) + pltpu.roll(smooth, 126, 1)
    smooth = smooth + pltpu.roll(smooth, 1, 0) + pltpu.roll(smooth, 63, 0)
    return root(smooth)


def window_scales(responses):
    sums = jnp.concatenate(
        [jnp.sum(values.reshape(8, 8, 128), axis=0) for values in responses], axis=0
    )
    high, low = split(sums)
    row = lax.broadcasted_iota(jnp.int32, (256, 128), 0)
    lane = lax.broadcasted_iota(jnp.int32, (256, 128), 1)
    same = jnp.where((row - lane) % 2 == 0, 1.0, 0.0).astype(BF)
    totals = dot(jnp.concatenate([high, low], axis=1), same)
    scales = []
    for at in range(len(responses)):
        total = jnp.sum(totals[8 * at : 8 * at + 8], axis=0, keepdims=True)
        scales.append(1.0 / (total * np.float32(1 / 4096) + np.float32(3e-06)))
    return scales


def filter_band(spectra, inverse):
    responses = [response_of(values) for values in spectra]
    gained = [
        rows_triple(values * jnp.concatenate([response, response], axis=0))
        for values, response in zip(spectra, responses)
    ]
    back = dot(inverse, jnp.concatenate(gained, axis=1))
    scales = window_scales(responses)
    return [
        back[:, at * 128 : at * 128 + 128] * scales[at] for at in range(len(spectra))
    ]


def pair_rows(top, bottom):
    real = jnp.concatenate([top[:32], bottom[:32]], axis=0)
    imag = jnp.concatenate([top[32:], bottom[32:]], axis=0)
    return columns_triple(jnp.concatenate([real, imag], axis=1))


def reference_body(own, peer1, peer2, core, first, second, near, cross, edges, sample_rows,
                   master, send_first, send_second):
    az = lax.axis_index("az")
    odd = az % 2 == 1
    pieces = (
        (own.at[0], own.at[1]), (peer1.at[0], peer1.at[1]),
        (peer2.at[0], peer2.at[1]), (core.at[0:64], core.at[64:128]),
    )
    held, lent = (cross.at[0:64], cross.at[64:128]), (core.at[192:256], core.at[128:192])
    halos = (
        (first.at[384:448], second.at[384:448]), (near.at[0:64], near.at[64:128]),
        (held[0], lent[0]), (held[1], lent[1]),
    )

    def store(piece, lanes, date):
        middle, halo, shared = piece
        if shared and date % 2 == 1:
            halo = halo[::-1]
        for part in range(2):
            master[part * 128 + 32 : part * 128 + 96, lanes] = middle[part][...]

        def place(top, bottom):
            for part in range(2):
                rows = slice(part * 32, part * 32 + 32)
                master[part * 128 : part * 128 + 32, lanes] = top[rows]
                master[part * 128 + 96 : part * 128 + 128, lanes] = bottom[rows]

        @pl.when(odd)
        def _():
            place(*halo)

        @pl.when(jnp.logical_not(odd))
        def _():
            place(*halo[::-1])

    by_date(list(zip(pieces, halos, (False, False, True, True))), store)

    @pl.when(az == 0)
    def _():
        for part in range(2):
            master[part * 128 : part * 128 + 32] = jnp.zeros((32, 512), BF)

    @pl.when(az == lax.axis_size("az") - 1)
    def _():
        for part in range(2):
            master[part * 128 + 96 : part * 128 + 128] = jnp.zeros((32, 512), BF)

    lane = lax.broadcasted_iota(jnp.int32, (128, 128), 1)
    narrow = lax.broadcasted_iota(jnp.int32, (32, 128), 1)

    def message(tile, edge, turn):
        lanes = slice(tile * 128, tile * 128 + 128)
        rows = edges[:, edge * 128 : edge * 128 + 128].astype(F32)
        cells = master[:, lanes].astype(F32)
        real, imag = cells[:128], cells[128:]
        wide = jnp.where(
            lane < 48,
            pltpu.roll(rows[:128], turn[0], 1) if turn[0] else rows[:128],
            jnp.where(
                lane < 96,
                pltpu.roll(rows[128:], turn[1], 1),
                pltpu.roll(real, turn[2], 1) if turn[2] else real,
            ),
        )
        tail = pltpu.roll(imag[:32], (turn[2] + 32) % 128, 1)
        for group in range(1, 4):
            step = (turn[2] + 32 + 32 * group) % 128
            part = imag[32 * group : 32 * group + 32]
            tail = jnp.where(
                narrow < 32 * group, tail, pltpu.roll(part, step, 1) if step else part
            )
        return wide.astype(BF), tail.astype(BF), sample_rows[:, lanes].astype(BF)

    to_right = message(3, 1, (48, 96, 0))
    to_left = message(0, 0, (0, 48, 96))
    rg_odd = lax.axis_index("rg") % 2 == 1

    def send(target, parts):
        target[0:128], target[128:160], target[160:176] = parts

    @pl.when(rg_odd)
    def _():
        send(send_first, to_left)
        send(send_second, to_right)

    @pl.when(jnp.logical_not(rg_odd))
    def _():
        send(send_first, to_right)
        send(send_second, to_left)


def filter_columns(columns, lines, inverse):
    stacked = [
        jnp.concatenate([real[0], imag[0], real[1], imag[1], real[0], imag[0]], axis=0)
        for real, imag in columns
    ]
    spectrum = dot(lines[...], jnp.concatenate(stacked, axis=1))
    bands = []
    for band, rows in ((0, slice(64, 128)), (1, slice(0, 128)), (2, slice(0, 64))):
        spectra = [
            spectrum[band * 128 : band * 128 + 128, at * 128 : at * 128 + 128]
            for at in range(len(columns))
        ]
        bands.append(filter_band(spectra, inverse[rows]))
    return [
        (middle[:64] + upper, middle[64:] + lower)
        for upper, middle, lower in zip(*bands)
    ]


def interior_body(resampled, master, forward, lines, inverse, samples, out):
    tiles = tiles_of(master)
    products = []
    for j in range(1, 8):
        around = shifted(tiles, 64 * j - 32)
        values = resampled.at[j - 1]
        products.append(cross_product(values[:128], values[128:], around[:128], around[128:]))
    columns = sample_columns(products, forward[...])
    parts = []
    for j, (tops, bottoms) in enumerate(filter_columns(columns, lines, inverse), 1):
        if j == 7:
            lane = lax.broadcasted_iota(jnp.int32, tops.shape, 1)
            tops = jnp.where(lane % 2 == 0, tops, 0.0)
            bottoms = jnp.where(lane % 2 == 0, bottoms, 0.0)
        parts.append(pair_rows(tops, bottoms))
    for block in range(4):
        used = [j for j in (2 * block, 2 * block + 1, 2 * block + 2) if 1 <= j <= 7]
        start = (used[0] - 2 * block) * 768
        values = dot(
            jnp.concatenate([parts[j - 1] for j in used], axis=1),
            samples[start : start + 768 * len(used)],
        )
        out[0, 0, :, block * 128 : block * 128 + 128] = values[:, :128]
        out[0, 1, :, block * 128 : block * 128 + 128] = values[:, 128:]


def edge_body(part, edges, master, sample_rows, first, second, forward, lines, inverse,
              samples, out, sides, sems):
    centre = pltpu.make_async_copy(
        part.at[:, :, :, 128:384], out.at[:, :, :, 128:384], sems.at[0]
    )
    centre.start()
    rg = lax.axis_index("rg")
    odd = rg % 2 == 1
    first_f = first[...].astype(F32)
    second_f = second[...].astype(F32)
    has_left = jnp.where(rg > 0, 1.0, 0.0).astype(F32)
    has_right = jnp.where(rg < lax.axis_size("rg") - 1, 1.0, 0.0).astype(F32)
    from_left = jnp.where(odd, first_f, second_f) * has_left
    from_right = jnp.where(odd, second_f, first_f) * has_right

    def turned(values, step):
        return pltpu.roll(values, step % 128, 1) if step % 128 else values

    def block(message, tile, edge, cuts, reverse):
        lanes = slice(tile * 128, tile * 128 + 128)

        def mixed(cut, halo, own):
            lane = lax.broadcasted_iota(jnp.int32, own.shape, 1)
            return jnp.where(lane >= cut if reverse else lane < cut, halo, own)

        row_turn, cell_turn = (80, 64) if reverse else (0, 0)
        own_row, own_cell = (80, 64) if reverse else (48, 32)
        rows = edges[:, edge * 128 : edge * 128 + 128].astype(F32)
        window = [
            mixed(cuts[0], turned(message[:128], row_turn - 48 * which),
                  turned(rows[which * 128 : which * 128 + 128], own_row))
            for which in range(2)
        ]
        cells = master[:, lanes].astype(F32)
        real, imag = cells[:128], cells[128:]
        real = mixed(cuts[1], turned(message[:128], cell_turn - 96), turned(real, own_cell))
        tail = [turned(message[128:160], cell_turn - 32 * group) for group in range(4)]
        imag = mixed(cuts[1], jnp.concatenate(tail, axis=0), turned(imag, own_cell))
        sample = mixed(
            cuts[1], turned(message[160:176], 64 if reverse else 32),
            turned(sample_rows[:, lanes], own_cell),
        )
        matrix = band_matrix(sample, 128).astype(BF)
        values = dot(jnp.concatenate(window, axis=0).astype(BF), matrix)
        return cross_product(values[:128], values[128:], real, imag)

    products = [
        block(from_left, 0, 0, (48, 32), False), block(from_right, 3, 1, (80, 64), True)
    ]
    results = filter_columns(sample_columns(products, forward[...]), lines, inverse)
    rows = jnp.concatenate([pair_rows(tops, bottoms) for tops, bottoms in results], axis=0)
    values = dot(rows, samples[2304:3072])
    lane = lax.broadcasted_iota(jnp.int32, (64, 128), 1)
    for at, target in ((0, 0), (1, 3)):
        lanes = slice(target * 128, target * 128 + 128)
        side = slice(at * 128, at * 128 + 128)
        kept = (lane < 64) if at == 0 else (lane >= 64)
        for which in range(2):
            found = values[at * 64 : at * 64 + 64, which * 128 : which * 128 + 128]
            sides[0, which, :, side] = part[0, which, :, lanes] + jnp.where(kept, found, 0.0)
    copies = [
        pltpu.make_async_copy(
            sides.at[:, :, :, at * 128 : at * 128 + 128],
            out.at[:, :, :, target * 128 : target * 128 + 128],
            sems.at[at + 1],
        )
        for at, target in ((0, 0), (1, 3))
    ]
    for copy in copies:
        copy.start()
    centre.wait()
    for copy in copies:
        copy.wait()


def call(name, body, outputs, scratch=(), hbm=0, cost=0, far_out=False):
    vmem = pl.BlockSpec(memory_space=pltpu.VMEM)
    far = pl.BlockSpec(memory_space=pltpu.HBM)
    return lambda *args: pl.pallas_call(
        body,
        name=name,
        out_shape=[jax.ShapeDtypeStruct(shape, kind) for shape, kind in outputs],
        in_specs=[far] * hbm + [vmem] * (len(args) - hbm),
        out_specs=[far if far_out else vmem] * len(outputs),
        scratch_shapes=list(scratch),
        compiler_params=pltpu.CompilerParams(vmem_limit_bytes=VMEM_LIMIT),
        cost_estimate=pl.CostEstimate(flops=cost, bytes_accessed=cost // 100, transcendentals=0),
    )(*args)


def exchange(first, second, axis):
    size = lax.axis_size(axis)
    dates = lax.axis_size("date")
    pairs = []
    for date in range(dates):
        for i in range(size):
            partner = (date, i + 1 if i % 2 == 1 else i - 1)
            if i in (0, size - 1):
                partner = (date ^ 1, i)
            pairs.append((date * size + i, partner[0] * size + partner[1]))
    received_first = lax.ppermute(first, axis, [(i, i ^ 1) for i in range(size)])
    received_second = lax.ppermute(second, ("date", axis), pairs)
    return received_first, received_second


def cross_swap(values):
    size = lax.axis_size("az")
    pairs = []
    for date in range(lax.axis_size("date")):
        for i in range(size):
            partner = i ^ 1
            if date % 2 == 1:
                partner = i if i in (0, size - 1) else i + 1 if i % 2 == 1 else i - 1
            pairs.append((date * size + i, (date ^ 2) * size + partner))
    return lax.ppermute(values, ("date", "az"), pairs)


def date_swap(values, k):
    return lax.ppermute(values, "date", [(i, i ^ k) for i in range(4)])


def on_device(reference_slab, secondary, az_shift, az_fraction, rg_shift, rg_fraction):
    own = reference_slab.reshape(2, LINES_DEV, 128)
    message = ((464, 128), BF)
    peer1 = date_swap(own, 1)
    lead = call("lead", lead_body, [((16, 128), F32)], cost=2 * 10**9)()[0]
    first, second, line_rows = call(
        "pack", pack_body, [message, message, ((16, 128), F32)],
        cost=10**9,
    )(secondary, own, az_shift, az_fraction, lead)
    cross, own_v = call(
        "cross_pack", cross_pack_body, [((128, 128), BF), ((2, LINES_DEV, 128), BF)], cost=2 * 10**9
    )(first, second, own, peer1)
    first, second = exchange(first, second, "az")
    tables = [jnp.asarray(table) for table in filter_tables()]
    prepared = call(
        "prepare", prepare_body,
        [((1, 2, LINES_DEV, 512), BF), ((16, 512), F32), ((7, 128, 128), BF)],
        [pltpu.VMEM((1, 512), jnp.int32), pltpu.VMEM((1, 512), F32), pltpu.SemaphoreType.DMA((3,))],
        hbm=3, cost=2 * 10**9,
    )(secondary, rg_shift, rg_fraction, cross)
    secondary_v, sample_rows, bands = prepared
    near = date_swap(jnp.concatenate([first[384:448], second[384:448]], axis=0), 1)
    peer2 = date_swap(own_v, 2)
    cross = cross_swap(cross)
    core = call("core_pack", core_pack_body, [((256, 128), BF)], cost=10**7)(peer2, cross)[0]
    core = date_swap(core, 1)
    edges, resampled = call(
        "lines", lines_body, [((256, 256), BF), ((7, 256, 128), F32)],
        [pltpu.VMEM((2, 160, 512), BF), pltpu.VMEM((2, 16, 128), F32)],
        cost=10**9,
    )(secondary_v, line_rows, first, second, bands)
    message = ((176, 128), BF)
    master, first, second = call(
        "reference", reference_body, [((256, 512), BF), message, message], cost=10**8
    )(own_v, peer1, peer2, core, first, second, near, cross, edges, sample_rows)
    first, second = exchange(first, second, "rg")
    whole = ((1, 2, LINES_DEV, SAMPLES_DEV), F32)
    part = call("interior", interior_body, [whole], cost=4 * 10**9)(
        resampled, master, *tables
    )[0]
    return call(
        "edge", edge_body, [whole],
        [pltpu.VMEM((1, 2, LINES_DEV, 256), F32), pltpu.SemaphoreType.DMA((3,))],
        cost=10**9, far_out=True,
    )(part, edges, master, sample_rows, first, second, *tables)[0]


def solution(mesh):
    in_specs = (
        P(None, "az", "rg", "date"),
        P("date", None, "az", "rg"),
        P("date", "az"),
        P("date", "az"),
        P("date", "rg"),
        P("date", "rg"),
    )
    out_specs = P("date", None, "az", "rg")
    return jax.shard_map(
        on_device, mesh=mesh, in_specs=in_specs, out_specs=out_specs, check_vma=False
    )
```

```python
import functools

import jax
import jax.numpy as jnp
import ml_dtypes
import numpy as np
from jax import lax
from jax.experimental import pallas as pl
from jax.experimental.pallas import tpu as pltpu
from jax.sharding import PartitionSpec as P

PATCH = 64
HALF = 32
TAPS = 8
MARGIN = 48
LINES_DEV = 64
SAMPLES_DEV = 512
BF = jnp.bfloat16
F32 = jnp.float32
VMEM_LIMIT = 32 * 1024 * 1024


def split_table(table):
    high = table.astype(ml_dtypes.bfloat16)
    low = (table - high.astype(np.float64)).astype(ml_dtypes.bfloat16)
    return high, low


def hann(position):
    return np.minimum(position + 0.5, PATCH - 0.5 - position) / HALF


def sample_forward():
    table = np.zeros((2, 128, 2, 64, 2))
    v = np.arange(64)
    for p in range(2):
        for m in range(64):
            angle = 2 * np.pi * ((v * m) % 64) / 64
            n = m + 32 * p
            table[0, n, 0, :, p] = np.cos(angle)
            table[1, n, 0, :, p] = np.sin(angle)
            table[0, n, 1, :, p] = -np.sin(angle)
            table[1, n, 1, :, p] = np.cos(angle)
    return table.reshape(256, 256)


def line_forward():
    table = np.zeros((2, 64, 2, 64))
    u = np.arange(64)
    for m in range(64):
        angle = 2 * np.pi * ((u * m) % 64) / 64
        table[0, :, 0, m] = np.cos(angle)
        table[0, :, 1, m] = np.sin(angle)
        table[1, :, 0, m] = -np.sin(angle)
        table[1, :, 1, m] = np.cos(angle)
    return table.reshape(128, 128)


def line_bands():
    small = line_forward().reshape(2, 64, 2, 64)
    table = np.zeros((3, 2, 64, 2, 128))
    for band in range(3):
        table[band, :, :, :, 32 * band : 32 * band + 64] = small
    return table.reshape(384, 256)


def line_inverse():
    table = np.zeros((2, 2, 32, 2, 64))
    u = np.arange(64)
    for m in range(64):
        angle = 2 * np.pi * ((u * m) % 64) / 64
        weight = hann(m) / 64
        table[m // 32, 0, m % 32, 0, :] = weight * np.cos(angle)
        table[m // 32, 0, m % 32, 1, :] = -weight * np.sin(angle)
        table[m // 32, 1, m % 32, 0, :] = weight * np.sin(angle)
        table[m // 32, 1, m % 32, 1, :] = weight * np.cos(angle)
    return table.reshape(128, 128)


def sample_inverse(start):
    table = np.zeros((2, 64, 2, 2, 128))
    v = np.arange(64)
    for p in range(2):
        for y in range(128):
            n = 32 + y - start - 32 * p
            if 0 <= n < 64:
                angle = 2 * np.pi * ((v * n) % 64) / 64
                weight = hann(n) / 64
                table[0, :, p, 0, y] = weight * np.cos(angle)
                table[1, :, p, 0, y] = -weight * np.sin(angle)
                table[0, :, p, 1, y] = weight * np.sin(angle)
                table[1, :, p, 1, y] = weight * np.cos(angle)
    return table.reshape(256, 256)


def triple(table, axis):
    high, low = split_table(table)
    return np.concatenate([high, high, low], axis=axis)


def filter_tables():
    inverse = [sample_inverse(start) for start in (0, 64, 128)]
    inverse.append(inverse[0] + sample_inverse(96))
    return [
        triple(sample_forward(), 0),
        triple(line_bands(), 1),
        triple(line_inverse(), 1),
        np.concatenate([triple(table, 0) for table in inverse], axis=0),
    ]


def sinc_rows(fraction):
    tap = lax.broadcasted_iota(jnp.int32, (TAPS, fraction.shape[1]), 0)
    distance = fraction - (tap - (TAPS // 2 - 1)).astype(F32)
    centre = distance == 0.0
    sign = jnp.where(tap % 2 == 1, 1.0, -1.0)
    wave = sign * jnp.sin(np.float32(np.pi) * fraction)
    sinc = wave / jnp.where(centre, 1.0, np.float32(np.pi) * distance)
    sinc = jnp.where(centre, 1.0, sinc)
    taper = 0.5 + 0.5 * jnp.cos(np.float32(np.pi) * distance / (TAPS // 2))
    return (sinc * taper).astype(BF).astype(F32)


def kernel_rows(shift, fraction):
    weights = sinc_rows(fraction)
    row = lax.broadcasted_iota(jnp.int32, weights.shape, 0)
    shifts = jnp.where(row == 0, shift.astype(F32), 0.0)
    return jnp.concatenate([weights, shifts], axis=0)


def band_matrix(rows, depth):
    width = rows.shape[1]
    shift = rows[TAPS : TAPS + 1].astype(jnp.int32)
    source = lax.broadcasted_iota(jnp.int32, (depth, width), 0)
    target = lax.broadcasted_iota(jnp.int32, (depth, width), 1)
    step = source - (target + 13 + shift)
    matrix = jnp.zeros((depth, width), F32)
    for k in range(TAPS):
        matrix = jnp.where(step == k, rows[k : k + 1], matrix)
    return matrix


def split(values):
    high = values.astype(BF)
    return high, (values - high.astype(F32)).astype(BF)


def dot(left, right):
    return jnp.dot(left, right, preferred_element_type=F32)


def columns_triple(values):
    high, low = split(values)
    return jnp.concatenate([high, low, high], axis=1)


def rows_triple(values):
    high, low = split(values)
    return jnp.concatenate([high, low, high], axis=0)


def shifted(tiles, start):
    index, offset = start // 128, start % 128
    here = pltpu.roll(tiles[index], 128 - offset, 1)
    after = pltpu.roll(tiles[min(index + 1, 3)], 128 - offset, 1)
    lane = lax.broadcasted_iota(jnp.int32, here.shape, 1)
    return jnp.where(lane < 128 - offset, here, after)


def tiles_of(values):
    return [values[:, t * 128 : t * 128 + 128].astype(F32) for t in range(4)]


def lead_body(out):
    out[...] = jnp.zeros_like(out)


def pack_body(secondary, own, shift, fraction, lead, first, second, line_rows):
    odd = lax.axis_index("az") % 2 == 1

    def fill(message, line, half):
        for part in range(2):
            for tile in range(4):
                rows = slice((2 * tile + part) * 48, (2 * tile + part) * 48 + 48)
                message[rows] = secondary[0, part, line : line + 48, tile * 128 : tile * 128 + 128]
            message[384 + part * 32 : 416 + part * 32] = own[part, half : half + 32]

    @pl.when(odd)
    def _():
        fill(first, 0, 0)
        fill(second, 16, 32)

    @pl.when(jnp.logical_not(odd))
    def _():
        fill(first, 16, 32)
        fill(second, 0, 0)

    row_shift = jnp.concatenate([shift[...], shift[...]], axis=1)
    row_fraction = jnp.concatenate([fraction[...], fraction[...]], axis=1)
    rows = kernel_rows(pltpu.roll(row_shift, 32, 1), pltpu.roll(row_fraction, 32, 1)) + lead[...]
    line_rows[...] = rows
    first[448:464] = rows.astype(BF)
    second[448:464] = rows.astype(BF)


def cross_pack_body(first, second, own, mate, message, own_v):
    own_v[...] = own[...]
    odd = lax.axis_index("az") % 2
    side = lax.axis_index("date") % 2

    @pl.when(side == 0)
    def _():
        message[0:64] = first[384:448]

    @pl.when(side == 1)
    def _():
        message[0:64] = second[384:448]

    def fill(half):
        for part in range(2):
            message[64 + part * 32 : 96 + part * 32] = mate[part, half : half + 32]

    @pl.when(odd != side)
    def _():
        fill(0)

    @pl.when(odd == side)
    def _():
        fill(32)


def core_pack_body(piece, cross, first, second, after, message):
    del after
    message[256:320] = first[384:448]
    message[320:384] = second[384:448]
    for part in range(2):
        message[part * 64 : part * 64 + 64] = piece[part]
    message[128:256] = cross[...]


def prepare_body(secondary, shift, fraction, after, secondary_v, sample_rows, bands,
                 shift_v, fraction_v, sems):
    del after
    pairs = [(shift, shift_v), (fraction, fraction_v), (secondary, secondary_v)]
    copies = [
        pltpu.make_async_copy(source, target, sems.at[at]) for at, (source, target) in enumerate(pairs)
    ]
    for copy in copies:
        copy.start()
    for copy in copies[:2]:
        copy.wait()
    samples = kernel_rows(shift_v[...], fraction_v[...])
    sample_rows[...] = samples
    tiles = tiles_of(samples)
    for j in range(1, 8):
        bands[j - 1] = band_matrix(shifted(tiles, 64 * j - 32), 128).astype(BF)
    for copy in copies[2:]:
        copy.wait()


def lines_body(secondary, line_rows, first, second, bands, edges, resampled, extended, halo_rows):
    odd = lax.axis_index("az") % 2 == 1
    has_top = lax.axis_index("az") > 0
    has_bottom = lax.axis_index("az") < lax.axis_size("az") - 1

    def place(top, bottom):
        for part in range(2):
            for tile in range(4):
                rows = slice((2 * tile + part) * 48, (2 * tile + part) * 48 + 48)
                lanes = slice(tile * 128, tile * 128 + 128)
                extended[part, 0:48, lanes] = top[rows]
                extended[part, 112:160, lanes] = bottom[rows]
        halo_rows[0] = top[448:464].astype(F32)
        halo_rows[1] = bottom[448:464].astype(F32)

    @pl.when(odd)
    def _():
        place(first, second)

    @pl.when(jnp.logical_not(odd))
    def _():
        place(second, first)

    for part in range(2):
        extended[part, 48:112] = secondary[0, part]

    lane = lax.broadcasted_iota(jnp.int32, (16, 128), 1)
    rows = jnp.where(
        lane < 32,
        pltpu.roll(halo_rows[0], 64, 1),
        jnp.where(lane < 96, line_rows[...], pltpu.roll(halo_rows[1], 64, 1)),
    )
    matrix = band_matrix(rows, 160)
    line = lax.broadcasted_iota(jnp.int32, matrix.shape, 0)
    low = jnp.where(has_top, 0, 48)
    high = jnp.where(has_bottom, 160, 112)
    matrix = jnp.where((line >= low) & (line < high), matrix, 0.0).astype(BF)
    values = [
        lax.dot_general(
            matrix, extended[part], (((0,), (0,)), ((), ())), preferred_element_type=F32
        )
        for part in range(2)
    ]
    values = jnp.concatenate(values, axis=0).astype(BF)
    edges[:, 0:128] = values[:, 0:128]
    edges[:, 128:256] = values[:, 384:512]
    tiles = tiles_of(values)
    for j in range(1, 8):
        resampled[j - 1] = dot(shifted(tiles, 64 * j - 48).astype(BF), bands[j - 1])


def by_date(pieces, store):
    date = lax.axis_index("date")
    for value in range(4):

        @pl.when(date == value)
        def _():
            for offset in range(4):
                place = (value ^ offset) * 128
                store(pieces[offset], slice(place, place + 128), value)


def root(values):
    return values * lax.rsqrt(jnp.maximum(values, np.float32(1e-36)))


def cross_product(real, imag, master_real, master_imag):
    return jnp.concatenate(
        [master_real * real + master_imag * imag, master_imag * real - master_real * imag], axis=1
    )


def sample_columns(products, forward):
    result = []
    for product in products:
        columns = dot(columns_triple(product), forward)
        result.append((split(columns[:, :128]), split(columns[:, 128:])))
    return result


def response_of(spectrum):
    real, imag = spectrum[:64], spectrum[64:]
    smooth = root(real * real + imag * imag)
    smooth = smooth + pltpu.roll(smooth, 2, 1) + pltpu.roll(smooth, 126, 1)
    smooth = smooth + pltpu.roll(smooth, 1, 0) + pltpu.roll(smooth, 63, 0)
    return root(smooth)


def window_scales(responses):
    sums = jnp.concatenate(
        [jnp.sum(values.reshape(8, 8, 128), axis=0) for values in responses], axis=0
    )
    high, low = split(sums)
    row = lax.broadcasted_iota(jnp.int32, (256, 128), 0)
    lane = lax.broadcasted_iota(jnp.int32, (256, 128), 1)
    same = jnp.where((row - lane) % 2 == 0, 1.0, 0.0).astype(BF)
    totals = dot(jnp.concatenate([high, low], axis=1), same)
    scales = []
    for at in range(len(responses)):
        total = jnp.sum(totals[8 * at : 8 * at + 8], axis=0, keepdims=True)
        scales.append(1.0 / (total * np.float32(1 / 4096) + np.float32(3e-06)))
    return scales


def filter_band(spectra, inverse):
    responses = [response_of(values) for values in spectra]
    gained = [
        rows_triple(values * jnp.concatenate([response, response], axis=0))
        for values, response in zip(spectra, responses)
    ]
    back = dot(inverse, jnp.concatenate(gained, axis=1))
    scales = window_scales(responses)
    return [
        back[:, at * 128 : at * 128 + 128] * scales[at] for at in range(len(spectra))
    ]


def pair_rows(top, bottom):
    real = jnp.concatenate([top[:32], bottom[:32]], axis=0)
    imag = jnp.concatenate([top[32:], bottom[32:]], axis=0)
    return columns_triple(jnp.concatenate([real, imag], axis=1))


def reference_body(own, peer1, peer2, core, first, second, cross, edges, sample_rows,
                   master, send_first, send_second):
    az = lax.axis_index("az")
    odd = az % 2 == 1
    pieces = (
        (own.at[0], own.at[1]), (peer1.at[0], peer1.at[1]),
        (peer2.at[0], peer2.at[1]), (core.at[0:64], core.at[64:128]),
    )
    held, lent = (cross.at[0:64], cross.at[64:128]), (core.at[192:256], core.at[128:192])
    halos = (
        (first.at[384:448], second.at[384:448]), (core.at[256:320], core.at[320:384]),
        (held[0], lent[0]), (held[1], lent[1]),
    )

    def store(piece, lanes, date):
        middle, halo, shared = piece
        if shared and date % 2 == 1:
            halo = halo[::-1]
        for part in range(2):
            master[part * 128 + 32 : part * 128 + 96, lanes] = middle[part][...]

        def place(top, bottom):
            for part in range(2):
                rows = slice(part * 32, part * 32 + 32)
                master[part * 128 : part * 128 + 32, lanes] = top[rows]
                master[part * 128 + 96 : part * 128 + 128, lanes] = bottom[rows]

        @pl.when(odd)
        def _():
            place(*halo)

        @pl.when(jnp.logical_not(odd))
        def _():
            place(*halo[::-1])

    by_date(list(zip(pieces, halos, (False, False, True, True))), store)

    @pl.when(az == 0)
    def _():
        for part in range(2):
            master[part * 128 : part * 128 + 32] = jnp.zeros((32, 512), BF)

    @pl.when(az == lax.axis_size("az") - 1)
    def _():
        for part in range(2):
            master[part * 128 + 96 : part * 128 + 128] = jnp.zeros((32, 512), BF)

    lane = lax.broadcasted_iota(jnp.int32, (128, 128), 1)
    narrow = lax.broadcasted_iota(jnp.int32, (32, 128), 1)

    def message(tile, edge, turn):
        lanes = slice(tile * 128, tile * 128 + 128)
        rows = edges[:, edge * 128 : edge * 128 + 128].astype(F32)
        cells = master[:, lanes].astype(F32)
        real, imag = cells[:128], cells[128:]
        wide = jnp.where(
            lane < 48,
            pltpu.roll(rows[:128], turn[0], 1) if turn[0] else rows[:128],
            jnp.where(
                lane < 96,
                pltpu.roll(rows[128:], turn[1], 1),
                pltpu.roll(real, turn[2], 1) if turn[2] else real,
            ),
        )
        tail = pltpu.roll(imag[:32], (turn[2] + 32) % 128, 1)
        for group in range(1, 4):
            step = (turn[2] + 32 + 32 * group) % 128
            part = imag[32 * group : 32 * group + 32]
            tail = jnp.where(
                narrow < 32 * group, tail, pltpu.roll(part, step, 1) if step else part
            )
        return wide.astype(BF), tail.astype(BF), sample_rows[:, lanes].astype(BF)

    to_right = message(3, 1, (48, 96, 0))
    to_left = message(0, 0, (0, 48, 96))
    rg_odd = lax.axis_index("rg") % 2 == 1

    def send(target, parts):
        target[0:128], target[128:160], target[160:176] = parts

    @pl.when(rg_odd)
    def _():
        send(send_first, to_left)
        send(send_second, to_right)

    @pl.when(jnp.logical_not(rg_odd))
    def _():
        send(send_first, to_right)
        send(send_second, to_left)


def filter_columns(columns, lines, inverse):
    stacked = [
        jnp.concatenate([real[0], imag[0], real[1], imag[1], real[0], imag[0]], axis=0)
        for real, imag in columns
    ]
    spectrum = dot(lines[...], jnp.concatenate(stacked, axis=1))
    bands = []
    for band, rows in ((0, slice(64, 128)), (1, slice(0, 128)), (2, slice(0, 64))):
        spectra = [
            spectrum[band * 128 : band * 128 + 128, at * 128 : at * 128 + 128]
            for at in range(len(columns))
        ]
        bands.append(filter_band(spectra, inverse[rows]))
    return [
        (middle[:64] + upper, middle[64:] + lower)
        for upper, middle, lower in zip(*bands)
    ]


def interior_body(resampled, master, forward, lines, inverse, samples, out):
    tiles = tiles_of(master)
    products = []
    for j in range(1, 8):
        around = shifted(tiles, 64 * j - 32)
        values = resampled.at[j - 1]
        products.append(cross_product(values[:128], values[128:], around[:128], around[128:]))
    columns = sample_columns(products, forward[...])
    parts = []
    for j, (tops, bottoms) in enumerate(filter_columns(columns, lines, inverse), 1):
        if j == 7:
            lane = lax.broadcasted_iota(jnp.int32, tops.shape, 1)
            tops = jnp.where(lane % 2 == 0, tops, 0.0)
            bottoms = jnp.where(lane % 2 == 0, bottoms, 0.0)
        parts.append(pair_rows(tops, bottoms))
    for block in range(4):
        used = [j for j in (2 * block, 2 * block + 1, 2 * block + 2) if 1 <= j <= 7]
        start = (used[0] - 2 * block) * 768
        values = dot(
            jnp.concatenate([parts[j - 1] for j in used], axis=1),
            samples[start : start + 768 * len(used)],
        )
        out[0, 0, :, block * 128 : block * 128 + 128] = values[:, :128]
        out[0, 1, :, block * 128 : block * 128 + 128] = values[:, 128:]


def edge_body(part, edges, master, sample_rows, first, second, forward, lines, inverse,
              samples, out, sides, sems):
    centre = pltpu.make_async_copy(
        part.at[:, :, :, 128:384], out.at[:, :, :, 128:384], sems.at[0]
    )
    centre.start()
    rg = lax.axis_index("rg")
    odd = rg % 2 == 1
    first_f = first[...].astype(F32)
    second_f = second[...].astype(F32)
    has_left = jnp.where(rg > 0, 1.0, 0.0).astype(F32)
    has_right = jnp.where(rg < lax.axis_size("rg") - 1, 1.0, 0.0).astype(F32)
    from_left = jnp.where(odd, first_f, second_f) * has_left
    from_right = jnp.where(odd, second_f, first_f) * has_right

    def turned(values, step):
        return pltpu.roll(values, step % 128, 1) if step % 128 else values

    def block(message, tile, edge, cuts, reverse):
        lanes = slice(tile * 128, tile * 128 + 128)

        def mixed(cut, halo, own):
            lane = lax.broadcasted_iota(jnp.int32, own.shape, 1)
            return jnp.where(lane >= cut if reverse else lane < cut, halo, own)

        row_turn, cell_turn = (80, 64) if reverse else (0, 0)
        own_row, own_cell = (80, 64) if reverse else (48, 32)
        rows = edges[:, edge * 128 : edge * 128 + 128].astype(F32)
        window = [
            mixed(cuts[0], turned(message[:128], row_turn - 48 * which),
                  turned(rows[which * 128 : which * 128 + 128], own_row))
            for which in range(2)
        ]
        cells = master[:, lanes].astype(F32)
        real, imag = cells[:128], cells[128:]
        real = mixed(cuts[1], turned(message[:128], cell_turn - 96), turned(real, own_cell))
        tail = [turned(message[128:160], cell_turn - 32 * group) for group in range(4)]
        imag = mixed(cuts[1], jnp.concatenate(tail, axis=0), turned(imag, own_cell))
        sample = mixed(
            cuts[1], turned(message[160:176], 64 if reverse else 32),
            turned(sample_rows[:, lanes], own_cell),
        )
        matrix = band_matrix(sample, 128).astype(BF)
        values = dot(jnp.concatenate(window, axis=0).astype(BF), matrix)
        return cross_product(values[:128], values[128:], real, imag)

    products = [
        block(from_left, 0, 0, (48, 32), False), block(from_right, 3, 1, (80, 64), True)
    ]
    results = filter_columns(sample_columns(products, forward[...]), lines, inverse)
    rows = jnp.concatenate([pair_rows(tops, bottoms) for tops, bottoms in results], axis=0)
    values = dot(rows, samples[2304:3072])
    lane = lax.broadcasted_iota(jnp.int32, (64, 128), 1)
    for at, target in ((0, 0), (1, 3)):
        lanes = slice(target * 128, target * 128 + 128)
        side = slice(at * 128, at * 128 + 128)
        kept = (lane < 64) if at == 0 else (lane >= 64)
        for which in range(2):
            found = values[at * 64 : at * 64 + 64, which * 128 : which * 128 + 128]
            sides[0, which, :, side] = part[0, which, :, lanes] + jnp.where(kept, found, 0.0)
    copies = [
        pltpu.make_async_copy(
            sides.at[:, :, :, at * 128 : at * 128 + 128],
            out.at[:, :, :, target * 128 : target * 128 + 128],
            sems.at[at + 1],
        )
        for at, target in ((0, 0), (1, 3))
    ]
    for copy in copies:
        copy.start()
    centre.wait()
    for copy in copies:
        copy.wait()


def call(name, body, outputs, scratch=(), hbm=0, cost=0, far_out=False):
    vmem = pl.BlockSpec(memory_space=pltpu.VMEM)
    far = pl.BlockSpec(memory_space=pltpu.HBM)
    return lambda *args: pl.pallas_call(
        body,
        name=name,
        out_shape=[jax.ShapeDtypeStruct(shape, kind) for shape, kind in outputs],
        in_specs=[far] * hbm + [vmem] * (len(args) - hbm),
        out_specs=[far if far_out else vmem] * len(outputs),
        scratch_shapes=list(scratch),
        compiler_params=pltpu.CompilerParams(vmem_limit_bytes=VMEM_LIMIT),
        cost_estimate=pl.CostEstimate(flops=cost, bytes_accessed=cost // 100, transcendentals=0),
    )(*args)


def exchange(first, second, axis):
    size = lax.axis_size(axis)
    dates = lax.axis_size("date")
    pairs = []
    for date in range(dates):
        for i in range(size):
            partner = (date, i + 1 if i % 2 == 1 else i - 1)
            if i in (0, size - 1):
                partner = (date ^ 1, i)
            pairs.append((date * size + i, partner[0] * size + partner[1]))
    received_first = lax.ppermute(first, axis, [(i, i ^ 1) for i in range(size)])
    received_second = lax.ppermute(second, ("date", axis), pairs)
    return received_first, received_second


def cross_swap(values):
    size = lax.axis_size("az")
    pairs = []
    for date in range(lax.axis_size("date")):
        for i in range(size):
            partner = i ^ 1
            if date % 2 == 1:
                partner = i if i in (0, size - 1) else i + 1 if i % 2 == 1 else i - 1
            pairs.append((date * size + i, (date ^ 2) * size + partner))
    return lax.ppermute(values, ("date", "az"), pairs)


def date_swap(values, k):
    return lax.ppermute(values, "date", [(i, i ^ k) for i in range(4)])


def on_device(reference_slab, secondary, az_shift, az_fraction, rg_shift, rg_fraction):
    own = reference_slab.reshape(2, LINES_DEV, 128)
    message = ((464, 128), BF)
    peer1 = date_swap(own, 1)
    lead = call("lead", lead_body, [((16, 128), F32)], cost=2 * 10**9)()[0]
    first, second, line_rows = call(
        "pack", pack_body, [message, message, ((16, 128), F32)],
        cost=10**9,
    )(secondary, own, az_shift, az_fraction, lead)
    cross, own_v = call(
        "cross_pack", cross_pack_body, [((128, 128), BF), ((2, LINES_DEV, 128), BF)], cost=2 * 10**9
    )(first, second, own, peer1)
    first, second = exchange(first, second, "az")
    tables = [jnp.asarray(table) for table in filter_tables()]
    prepared = call(
        "prepare", prepare_body,
        [((1, 2, LINES_DEV, 512), BF), ((16, 512), F32), ((7, 128, 128), BF)],
        [pltpu.VMEM((1, 512), jnp.int32), pltpu.VMEM((1, 512), F32), pltpu.SemaphoreType.DMA((3,))],
        hbm=3, cost=2 * 10**9,
    )(secondary, rg_shift, rg_fraction, cross)
    secondary_v, sample_rows, bands = prepared
    peer2 = date_swap(own_v, 2)
    cross = cross_swap(cross)
    core = call("core_pack", core_pack_body, [((384, 128), BF)], cost=10**7)(
        peer2, cross, first, second, sample_rows
    )[0]
    core = date_swap(core, 1)
    edges, resampled = call(
        "lines", lines_body, [((256, 256), BF), ((7, 256, 128), F32)],
        [pltpu.VMEM((2, 160, 512), BF), pltpu.VMEM((2, 16, 128), F32)],
        cost=10**9,
    )(secondary_v, line_rows, first, second, bands)
    message = ((176, 128), BF)
    master, first, second = call(
        "reference", reference_body, [((256, 512), BF), message, message], cost=10**8
    )(own_v, peer1, peer2, core, first, second, cross, edges, sample_rows)
    first, second = exchange(first, second, "rg")
    whole = ((1, 2, LINES_DEV, SAMPLES_DEV), F32)
    part = call("interior", interior_body, [whole], cost=4 * 10**9)(
        resampled, master, *tables
    )[0]
    return call(
        "edge", edge_body, [whole],
        [pltpu.VMEM((1, 2, LINES_DEV, 256), F32), pltpu.SemaphoreType.DMA((3,))],
        cost=10**9, far_out=True,
    )(part, edges, master, sample_rows, first, second, *tables)[0]


def solution(mesh):
    in_specs = (
        P(None, "az", "rg", "date"),
        P("date", None, "az", "rg"),
        P("date", "az"),
        P("date", "az"),
        P("date", "rg"),
        P("date", "rg"),
    )
    out_specs = P("date", None, "az", "rg")
    return jax.shard_map(
        on_device, mesh=mesh, in_specs=in_specs, out_specs=out_specs, check_vma=False
    )
```

```python
import functools

import jax
import jax.numpy as jnp
import ml_dtypes
import numpy as np
from jax import lax
from jax.experimental import pallas as pl
from jax.experimental.pallas import tpu as pltpu
from jax.sharding import PartitionSpec as P

PATCH = 64
HALF = 32
TAPS = 8
MARGIN = 48
LINES_DEV = 64
SAMPLES_DEV = 512
BF = jnp.bfloat16
F32 = jnp.float32
VMEM_LIMIT = 32 * 1024 * 1024


def split_table(table):
    high = table.astype(ml_dtypes.bfloat16)
    low = (table - high.astype(np.float64)).astype(ml_dtypes.bfloat16)
    return high, low


def hann(position):
    return np.minimum(position + 0.5, PATCH - 0.5 - position) / HALF


def sample_forward():
    table = np.zeros((2, 128, 2, 64, 2))
    v = np.arange(64)
    for p in range(2):
        for m in range(64):
            angle = 2 * np.pi * ((v * m) % 64) / 64
            n = m + 32 * p
            table[0, n, 0, :, p] = np.cos(angle)
            table[1, n, 0, :, p] = np.sin(angle)
            table[0, n, 1, :, p] = -np.sin(angle)
            table[1, n, 1, :, p] = np.cos(angle)
    return table.reshape(256, 256)


def line_forward():
    table = np.zeros((2, 64, 2, 64))
    u = np.arange(64)
    for m in range(64):
        angle = 2 * np.pi * ((u * m) % 64) / 64
        table[0, :, 0, m] = np.cos(angle)
        table[0, :, 1, m] = np.sin(angle)
        table[1, :, 0, m] = -np.sin(angle)
        table[1, :, 1, m] = np.cos(angle)
    return table.reshape(128, 128)


def line_bands():
    small = line_forward().reshape(2, 64, 2, 64)
    table = np.zeros((3, 2, 64, 2, 128))
    for band in range(3):
        table[band, :, :, :, 32 * band : 32 * band + 64] = small
    return table.reshape(384, 256)


def line_inverse():
    table = np.zeros((2, 2, 32, 2, 64))
    u = np.arange(64)
    for m in range(64):
        angle = 2 * np.pi * ((u * m) % 64) / 64
        weight = hann(m) / 64
        table[m // 32, 0, m % 32, 0, :] = weight * np.cos(angle)
        table[m // 32, 0, m % 32, 1, :] = -weight * np.sin(angle)
        table[m // 32, 1, m % 32, 0, :] = weight * np.sin(angle)
        table[m // 32, 1, m % 32, 1, :] = weight * np.cos(angle)
    return table.reshape(128, 128)


def sample_inverse(start):
    table = np.zeros((2, 64, 2, 2, 128))
    v = np.arange(64)
    for p in range(2):
        for y in range(128):
            n = 32 + y - start - 32 * p
            if 0 <= n < 64:
                angle = 2 * np.pi * ((v * n) % 64) / 64
                weight = hann(n) / 64
                table[0, :, p, 0, y] = weight * np.cos(angle)
                table[1, :, p, 0, y] = -weight * np.sin(angle)
                table[0, :, p, 1, y] = weight * np.sin(angle)
                table[1, :, p, 1, y] = weight * np.cos(angle)
    return table.reshape(256, 256)


def triple(table, axis):
    high, low = split_table(table)
    return np.concatenate([high, high, low], axis=axis)


def filter_tables():
    inverse = [sample_inverse(start) for start in (0, 64, 128)]
    inverse.append(inverse[0] + sample_inverse(96))
    return [
        triple(sample_forward(), 0),
        triple(line_bands(), 1),
        triple(line_inverse(), 1),
        np.concatenate([triple(table, 0) for table in inverse], axis=0),
    ]


def sinc_rows(fraction):
    tap = lax.broadcasted_iota(jnp.int32, (TAPS, fraction.shape[1]), 0)
    distance = fraction - (tap - (TAPS // 2 - 1)).astype(F32)
    centre = distance == 0.0
    sign = jnp.where(tap % 2 == 1, 1.0, -1.0)
    wave = sign * jnp.sin(np.float32(np.pi) * fraction)
    sinc = wave / jnp.where(centre, 1.0, np.float32(np.pi) * distance)
    sinc = jnp.where(centre, 1.0, sinc)
    taper = 0.5 + 0.5 * jnp.cos(np.float32(np.pi) * distance / (TAPS // 2))
    return (sinc * taper).astype(BF).astype(F32)


def kernel_rows(shift, fraction):
    weights = sinc_rows(fraction)
    row = lax.broadcasted_iota(jnp.int32, weights.shape, 0)
    shifts = jnp.where(row == 0, shift.astype(F32), 0.0)
    return jnp.concatenate([weights, shifts], axis=0)


def band_matrix(rows, depth):
    width = rows.shape[1]
    shift = rows[TAPS : TAPS + 1].astype(jnp.int32)
    source = lax.broadcasted_iota(jnp.int32, (depth, width), 0)
    target = lax.broadcasted_iota(jnp.int32, (depth, width), 1)
    step = source - (target + 13 + shift)
    matrix = jnp.zeros((depth, width), F32)
    for k in range(TAPS):
        matrix = jnp.where(step == k, rows[k : k + 1], matrix)
    return matrix


def split(values):
    high = values.astype(BF)
    return high, (values - high.astype(F32)).astype(BF)


def dot(left, right):
    return jnp.dot(left, right, preferred_element_type=F32)


def columns_triple(values):
    high, low = split(values)
    return jnp.concatenate([high, low, high], axis=1)


def rows_triple(values):
    high, low = split(values)
    return jnp.concatenate([high, low, high], axis=0)


def shifted(tiles, start):
    index, offset = start // 128, start % 128
    here = pltpu.roll(tiles[index], 128 - offset, 1)
    after = pltpu.roll(tiles[min(index + 1, 3)], 128 - offset, 1)
    lane = lax.broadcasted_iota(jnp.int32, here.shape, 1)
    return jnp.where(lane < 128 - offset, here, after)


def tiles_of(values):
    return [values[:, t * 128 : t * 128 + 128].astype(F32) for t in range(4)]


def lead_body(out):
    out[...] = jnp.zeros_like(out)


def pack_body(secondary, own, shift, fraction, lead, first, second, line_rows):
    odd = lax.axis_index("az") % 2 == 1

    def fill(message, line, half):
        for part in range(2):
            for tile in range(4):
                rows = slice((2 * tile + part) * 48, (2 * tile + part) * 48 + 48)
                message[rows] = secondary[0, part, line : line + 48, tile * 128 : tile * 128 + 128]
            message[384 + part * 32 : 416 + part * 32] = own[part, half : half + 32]

    @pl.when(odd)
    def _():
        fill(first, 0, 0)
        fill(second, 16, 32)

    @pl.when(jnp.logical_not(odd))
    def _():
        fill(first, 16, 32)
        fill(second, 0, 0)

    row_shift = jnp.concatenate([shift[...], shift[...]], axis=1)
    row_fraction = jnp.concatenate([fraction[...], fraction[...]], axis=1)
    rows = kernel_rows(pltpu.roll(row_shift, 32, 1), pltpu.roll(row_fraction, 32, 1)) + lead[...]
    line_rows[...] = rows
    first[448:464] = rows.astype(BF)
    second[448:464] = rows.astype(BF)


def cross_pack_body(first, second, own, mate, message, own_v):
    own_v[...] = own[...]
    odd = lax.axis_index("az") % 2
    side = lax.axis_index("date") % 2

    @pl.when(side == 0)
    def _():
        message[0:64] = first[384:448]

    @pl.when(side == 1)
    def _():
        message[0:64] = second[384:448]

    def fill(half):
        for part in range(2):
            message[64 + part * 32 : 96 + part * 32] = mate[part, half : half + 32]

    @pl.when(odd != side)
    def _():
        fill(0)

    @pl.when(odd == side)
    def _():
        fill(32)


def core_pack_body(piece, cross, first, second, after, message):
    del after
    message[256:320] = first[384:448]
    message[320:384] = second[384:448]
    for part in range(2):
        message[part * 64 : part * 64 + 64] = piece[part]
    message[128:256] = cross[...]


def prepare_body(secondary, shift, fraction, after, secondary_v, sample_rows, bands,
                 shift_v, fraction_v, sems):
    del after
    pairs = [(shift, shift_v), (fraction, fraction_v), (secondary, secondary_v)]
    copies = [
        pltpu.make_async_copy(source, target, sems.at[at]) for at, (source, target) in enumerate(pairs)
    ]
    for copy in copies:
        copy.start()
    for copy in copies[:2]:
        copy.wait()
    samples = kernel_rows(shift_v[...], fraction_v[...])
    sample_rows[...] = samples
    tiles = tiles_of(samples)
    for j in range(1, 8):
        bands[j - 1] = band_matrix(shifted(tiles, 64 * j - 32), 128).astype(BF)
    for copy in copies[2:]:
        copy.wait()


def lines_body(secondary, line_rows, first, second, bands, edges, resampled, extended, halo_rows):
    odd = lax.axis_index("az") % 2 == 1
    has_top = lax.axis_index("az") > 0
    has_bottom = lax.axis_index("az") < lax.axis_size("az") - 1

    def place(top, bottom):
        for part in range(2):
            for tile in range(4):
                rows = slice((2 * tile + part) * 48, (2 * tile + part) * 48 + 48)
                lanes = slice(tile * 128, tile * 128 + 128)
                extended[part, 0:48, lanes] = top[rows]
                extended[part, 112:160, lanes] = bottom[rows]
        halo_rows[0] = top[448:464].astype(F32)
        halo_rows[1] = bottom[448:464].astype(F32)

    @pl.when(odd)
    def _():
        place(first, second)

    @pl.when(jnp.logical_not(odd))
    def _():
        place(second, first)

    for part in range(2):
        extended[part, 48:112] = secondary[0, part]

    lane = lax.broadcasted_iota(jnp.int32, (16, 128), 1)
    rows = jnp.where(
        lane < 32,
        pltpu.roll(halo_rows[0], 64, 1),
        jnp.where(lane < 96, line_rows[...], pltpu.roll(halo_rows[1], 64, 1)),
    )
    matrix = band_matrix(rows, 160)
    line = lax.broadcasted_iota(jnp.int32, matrix.shape, 0)
    low = jnp.where(has_top, 0, 48)
    high = jnp.where(has_bottom, 160, 112)
    matrix = jnp.where((line >= low) & (line < high), matrix, 0.0).astype(BF)
    values = [
        lax.dot_general(
            matrix, extended[part], (((0,), (0,)), ((), ())), preferred_element_type=F32
        )
        for part in range(2)
    ]
    values = jnp.concatenate(values, axis=0).astype(BF)
    edges[:, 0:128] = values[:, 0:128]
    edges[:, 128:256] = values[:, 384:512]
    tiles = tiles_of(values)
    for j in range(1, 8):
        resampled[j - 1] = dot(shifted(tiles, 64 * j - 48).astype(BF), bands[j - 1])


def by_date(pieces, store):
    date = lax.axis_index("date")
    for value in range(4):

        @pl.when(date == value)
        def _():
            for offset in range(4):
                place = (value ^ offset) * 128
                store(pieces[offset], slice(place, place + 128), value)


def root(values):
    return values * lax.rsqrt(jnp.maximum(values, np.float32(1e-36)))


def cross_product(real, imag, master_real, master_imag):
    return jnp.concatenate(
        [master_real * real + master_imag * imag, master_imag * real - master_real * imag], axis=1
    )


def sample_columns(products, forward):
    result = []
    for product in products:
        columns = dot(columns_triple(product), forward)
        result.append((split(columns[:, :128]), split(columns[:, 128:])))
    return result


def response_of(spectrum):
    real, imag = spectrum[:64], spectrum[64:]
    smooth = root(real * real + imag * imag)
    smooth = smooth + pltpu.roll(smooth, 2, 1) + pltpu.roll(smooth, 126, 1)
    smooth = smooth + pltpu.roll(smooth, 1, 0) + pltpu.roll(smooth, 63, 0)
    return root(smooth)


def window_scales(responses):
    sums = jnp.concatenate(
        [jnp.sum(values.reshape(8, 8, 128), axis=0) for values in responses], axis=0
    )
    high, low = split(sums)
    row = lax.broadcasted_iota(jnp.int32, (256, 128), 0)
    lane = lax.broadcasted_iota(jnp.int32, (256, 128), 1)
    same = jnp.where((row - lane) % 2 == 0, 1.0, 0.0).astype(BF)
    totals = dot(jnp.concatenate([high, low], axis=1), same)
    scales = []
    for at in range(len(responses)):
        total = jnp.sum(totals[8 * at : 8 * at + 8], axis=0, keepdims=True)
        scales.append(1.0 / (total * np.float32(1 / 4096) + np.float32(3e-06)))
    return scales


def filter_band(spectra, inverse):
    responses = [response_of(values) for values in spectra]
    gained = [
        rows_triple(values * jnp.concatenate([response, response], axis=0))
        for values, response in zip(spectra, responses)
    ]
    back = dot(inverse, jnp.concatenate(gained, axis=1))
    scales = window_scales(responses)
    return [
        back[:, at * 128 : at * 128 + 128] * scales[at] for at in range(len(spectra))
    ]


def pair_rows(top, bottom):
    real = jnp.concatenate([top[:32], bottom[:32]], axis=0)
    imag = jnp.concatenate([top[32:], bottom[32:]], axis=0)
    return columns_triple(jnp.concatenate([real, imag], axis=1))


def reference_body(own, peer1, peer2, core, first, second, cross, edges, sample_rows,
                   master, send_first, send_second):
    az = lax.axis_index("az")
    odd = az % 2 == 1
    pieces = (
        (own.at[0], own.at[1]), (peer1.at[0], peer1.at[1]),
        (peer2.at[0], peer2.at[1]), (core.at[0:64], core.at[64:128]),
    )
    held, lent = (cross.at[0:64], cross.at[64:128]), (core.at[192:256], core.at[128:192])
    halos = (
        (first.at[384:448], second.at[384:448]), (core.at[256:320], core.at[320:384]),
        (held[0], lent[0]), (held[1], lent[1]),
    )

    def store(piece, lanes, date):
        middle, halo, shared = piece
        if shared and date % 2 == 1:
            halo = halo[::-1]
        for part in range(2):
            master[part * 128 + 32 : part * 128 + 96, lanes] = middle[part][...]

        def place(top, bottom):
            for part in range(2):
                rows = slice(part * 32, part * 32 + 32)
                master[part * 128 : part * 128 + 32, lanes] = top[rows]
                master[part * 128 + 96 : part * 128 + 128, lanes] = bottom[rows]

        @pl.when(odd)
        def _():
            place(*halo)

        @pl.when(jnp.logical_not(odd))
        def _():
            place(*halo[::-1])

    by_date(list(zip(pieces, halos, (False, False, True, True))), store)

    @pl.when(az == 0)
    def _():
        for part in range(2):
            master[part * 128 : part * 128 + 32] = jnp.zeros((32, 512), BF)

    @pl.when(az == lax.axis_size("az") - 1)
    def _():
        for part in range(2):
            master[part * 128 + 96 : part * 128 + 128] = jnp.zeros((32, 512), BF)

    lane = lax.broadcasted_iota(jnp.int32, (128, 128), 1)
    narrow = lax.broadcasted_iota(jnp.int32, (32, 128), 1)

    def message(tile, edge, turn):
        lanes = slice(tile * 128, tile * 128 + 128)
        rows = edges[:, edge * 128 : edge * 128 + 128].astype(F32)
        cells = master[:, lanes].astype(F32)
        real, imag = cells[:128], cells[128:]
        wide = jnp.where(
            lane < 48,
            pltpu.roll(rows[:128], turn[0], 1) if turn[0] else rows[:128],
            jnp.where(
                lane < 96,
                pltpu.roll(rows[128:], turn[1], 1),
                pltpu.roll(real, turn[2], 1) if turn[2] else real,
            ),
        )
        tail = pltpu.roll(imag[:32], (turn[2] + 32) % 128, 1)
        for group in range(1, 4):
            step = (turn[2] + 32 + 32 * group) % 128
            part = imag[32 * group : 32 * group + 32]
            tail = jnp.where(
                narrow < 32 * group, tail, pltpu.roll(part, step, 1) if step else part
            )
        return wide.astype(BF), tail.astype(BF), sample_rows[:, lanes].astype(BF)

    to_right = message(3, 1, (48, 96, 0))
    to_left = message(0, 0, (0, 48, 96))
    rg_odd = lax.axis_index("rg") % 2 == 1

    def send(target, parts):
        target[0:128], target[128:160], target[160:176] = parts

    @pl.when(rg_odd)
    def _():
        send(send_first, to_left)
        send(send_second, to_right)

    @pl.when(jnp.logical_not(rg_odd))
    def _():
        send(send_first, to_right)
        send(send_second, to_left)


def filter_columns(columns, lines, inverse):
    stacked = [
        jnp.concatenate([real[0], imag[0], real[1], imag[1], real[0], imag[0]], axis=0)
        for real, imag in columns
    ]
    spectrum = dot(lines[...], jnp.concatenate(stacked, axis=1))
    bands = []
    for band, rows in ((0, slice(64, 128)), (1, slice(0, 128)), (2, slice(0, 64))):
        spectra = [
            spectrum[band * 128 : band * 128 + 128, at * 128 : at * 128 + 128]
            for at in range(len(columns))
        ]
        bands.append(filter_band(spectra, inverse[rows]))
    return [
        (middle[:64] + upper, middle[64:] + lower)
        for upper, middle, lower in zip(*bands)
    ]


def interior_body(resampled, master, forward, lines, inverse, samples, out):
    tiles = tiles_of(master)
    products = []
    for j in range(1, 8):
        around = shifted(tiles, 64 * j - 32)
        values = resampled.at[j - 1]
        products.append(cross_product(values[:128], values[128:], around[:128], around[128:]))
    columns = sample_columns(products, forward[...])
    parts = []
    for j, (tops, bottoms) in enumerate(filter_columns(columns, lines, inverse), 1):
        if j == 7:
            lane = lax.broadcasted_iota(jnp.int32, tops.shape, 1)
            tops = jnp.where(lane % 2 == 0, tops, 0.0)
            bottoms = jnp.where(lane % 2 == 0, bottoms, 0.0)
        parts.append(pair_rows(tops, bottoms))
    for block in range(4):
        used = [j for j in (2 * block, 2 * block + 1, 2 * block + 2) if 1 <= j <= 7]
        start = (used[0] - 2 * block) * 768
        values = dot(
            jnp.concatenate([parts[j - 1] for j in used], axis=1),
            samples[start : start + 768 * len(used)],
        )
        out[0, 0, :, block * 128 : block * 128 + 128] = values[:, :128]
        out[0, 1, :, block * 128 : block * 128 + 128] = values[:, 128:]


def edge_body(part, edges, master, sample_rows, first, second, forward, lines, inverse,
              samples, out, sides, sems):
    centre = pltpu.make_async_copy(
        part.at[:, :, :, 128:384], out.at[:, :, :, 128:384], sems.at[0]
    )
    centre.start()
    rg = lax.axis_index("rg")
    odd = rg % 2 == 1
    first_f = first[...].astype(F32)
    second_f = second[...].astype(F32)
    has_left = jnp.where(rg > 0, 1.0, 0.0).astype(F32)
    has_right = jnp.where(rg < lax.axis_size("rg") - 1, 1.0, 0.0).astype(F32)
    from_left = jnp.where(odd, first_f, second_f) * has_left
    from_right = jnp.where(odd, second_f, first_f) * has_right

    def turned(values, step):
        return pltpu.roll(values, step % 128, 1) if step % 128 else values

    def block(message, tile, edge, cuts, reverse):
        lanes = slice(tile * 128, tile * 128 + 128)

        def mixed(cut, halo, own):
            lane = lax.broadcasted_iota(jnp.int32, own.shape, 1)
            return jnp.where(lane >= cut if reverse else lane < cut, halo, own)

        row_turn, cell_turn = (80, 64) if reverse else (0, 0)
        own_row, own_cell = (80, 64) if reverse else (48, 32)
        rows = edges[:, edge * 128 : edge * 128 + 128].astype(F32)
        window = [
            mixed(cuts[0], turned(message[:128], row_turn - 48 * which),
                  turned(rows[which * 128 : which * 128 + 128], own_row))
            for which in range(2)
        ]
        cells = master[:, lanes].astype(F32)
        real, imag = cells[:128], cells[128:]
        real = mixed(cuts[1], turned(message[:128], cell_turn - 96), turned(real, own_cell))
        tail = [turned(message[128:160], cell_turn - 32 * group) for group in range(4)]
        imag = mixed(cuts[1], jnp.concatenate(tail, axis=0), turned(imag, own_cell))
        sample = mixed(
            cuts[1], turned(message[160:176], 64 if reverse else 32),
            turned(sample_rows[:, lanes], own_cell),
        )
        matrix = band_matrix(sample, 128).astype(BF)
        return jnp.concatenate(window, axis=0).astype(BF), matrix, real, imag

    sides_in = [
        block(from_left, 0, 0, (48, 32), False), block(from_right, 3, 1, (80, 64), True)
    ]
    empty = jnp.zeros((128, 128), BF)
    (left, left_matrix, *_), (right, right_matrix, *_) = sides_in
    both = jnp.concatenate(
        [
            jnp.concatenate([left_matrix, empty], axis=1),
            jnp.concatenate([empty, right_matrix], axis=1),
        ],
        axis=0,
    )
    values = dot(jnp.concatenate([left, right], axis=1), both)
    products = [
        cross_product(
            values[:128, at * 128 : at * 128 + 128], values[128:, at * 128 : at * 128 + 128], *side[2:]
        )
        for at, side in enumerate(sides_in)
    ]
    results = filter_columns(sample_columns(products, forward[...]), lines, inverse)
    rows = jnp.concatenate([pair_rows(tops, bottoms) for tops, bottoms in results], axis=0)
    values = dot(rows, samples[2304:3072])
    lane = lax.broadcasted_iota(jnp.int32, (64, 128), 1)
    for at, target in ((0, 0), (1, 3)):
        lanes = slice(target * 128, target * 128 + 128)
        side = slice(at * 128, at * 128 + 128)
        kept = (lane < 64) if at == 0 else (lane >= 64)
        for which in range(2):
            found = values[at * 64 : at * 64 + 64, which * 128 : which * 128 + 128]
            sides[0, which, :, side] = part[0, which, :, lanes] + jnp.where(kept, found, 0.0)
    copies = [
        pltpu.make_async_copy(
            sides.at[:, :, :, at * 128 : at * 128 + 128],
            out.at[:, :, :, target * 128 : target * 128 + 128],
            sems.at[at + 1],
        )
        for at, target in ((0, 0), (1, 3))
    ]
    for copy in copies:
        copy.start()
    centre.wait()
    for copy in copies:
        copy.wait()


def call(name, body, outputs, scratch=(), hbm=0, cost=0, far_out=False):
    vmem = pl.BlockSpec(memory_space=pltpu.VMEM)
    far = pl.BlockSpec(memory_space=pltpu.HBM)
    return lambda *args: pl.pallas_call(
        body,
        name=name,
        out_shape=[jax.ShapeDtypeStruct(shape, kind) for shape, kind in outputs],
        in_specs=[far] * hbm + [vmem] * (len(args) - hbm),
        out_specs=[far if far_out else vmem] * len(outputs),
        scratch_shapes=list(scratch),
        compiler_params=pltpu.CompilerParams(vmem_limit_bytes=VMEM_LIMIT),
        cost_estimate=pl.CostEstimate(flops=cost, bytes_accessed=cost // 100, transcendentals=0),
    )(*args)


def exchange(first, second, axis):
    size = lax.axis_size(axis)
    dates = lax.axis_size("date")
    pairs = []
    for date in range(dates):
        for i in range(size):
            partner = (date, i + 1 if i % 2 == 1 else i - 1)
            if i in (0, size - 1):
                partner = (date ^ 1, i)
            pairs.append((date * size + i, partner[0] * size + partner[1]))
    received_first = lax.ppermute(first, axis, [(i, i ^ 1) for i in range(size)])
    received_second = lax.ppermute(second, ("date", axis), pairs)
    return received_first, received_second


def cross_swap(values):
    size = lax.axis_size("az")
    pairs = []
    for date in range(lax.axis_size("date")):
        for i in range(size):
            partner = i ^ 1
            if date % 2 == 1:
                partner = i if i in (0, size - 1) else i + 1 if i % 2 == 1 else i - 1
            pairs.append((date * size + i, (date ^ 2) * size + partner))
    return lax.ppermute(values, ("date", "az"), pairs)


def date_swap(values, k):
    return lax.ppermute(values, "date", [(i, i ^ k) for i in range(4)])


def on_device(reference_slab, secondary, az_shift, az_fraction, rg_shift, rg_fraction):
    own = reference_slab.reshape(2, LINES_DEV, 128)
    message = ((464, 128), BF)
    peer1 = date_swap(own, 1)
    lead = call("lead", lead_body, [((16, 128), F32)], cost=2 * 10**9)()[0]
    first, second, line_rows = call(
        "pack", pack_body, [message, message, ((16, 128), F32)],
        cost=10**9,
    )(secondary, own, az_shift, az_fraction, lead)
    cross, own_v = call(
        "cross_pack", cross_pack_body, [((128, 128), BF), ((2, LINES_DEV, 128), BF)], cost=2 * 10**9
    )(first, second, own, peer1)
    first, second = exchange(first, second, "az")
    tables = [jnp.asarray(table) for table in filter_tables()]
    prepared = call(
        "prepare", prepare_body,
        [((1, 2, LINES_DEV, 512), BF), ((16, 512), F32), ((7, 128, 128), BF)],
        [pltpu.VMEM((1, 512), jnp.int32), pltpu.VMEM((1, 512), F32), pltpu.SemaphoreType.DMA((3,))],
        hbm=3, cost=2 * 10**9,
    )(secondary, rg_shift, rg_fraction, cross)
    secondary_v, sample_rows, bands = prepared
    peer2 = date_swap(own_v, 2)
    cross = cross_swap(cross)
    core = call("core_pack", core_pack_body, [((384, 128), BF)], cost=10**7)(
        peer2, cross, first, second, sample_rows
    )[0]
    core = date_swap(core, 1)
    edges, resampled = call(
        "lines", lines_body, [((256, 256), BF), ((7, 256, 128), F32)],
        [pltpu.VMEM((2, 160, 512), BF), pltpu.VMEM((2, 16, 128), F32)],
        cost=10**9,
    )(secondary_v, line_rows, first, second, bands)
    message = ((176, 128), BF)
    master, first, second = call(
        "reference", reference_body, [((256, 512), BF), message, message], cost=10**8
    )(own_v, peer1, peer2, core, first, second, cross, edges, sample_rows)
    first, second = exchange(first, second, "rg")
    whole = ((1, 2, LINES_DEV, SAMPLES_DEV), F32)
    part = call("interior", interior_body, [whole], cost=4 * 10**9)(
        resampled, master, *tables
    )[0]
    return call(
        "edge", edge_body, [whole],
        [pltpu.VMEM((1, 2, LINES_DEV, 256), F32), pltpu.SemaphoreType.DMA((3,))],
        cost=10**9, far_out=True,
    )(part, edges, master, sample_rows, first, second, *tables)[0]


def solution(mesh):
    in_specs = (
        P(None, "az", "rg", "date"),
        P("date", None, "az", "rg"),
        P("date", "az"),
        P("date", "az"),
        P("date", "rg"),
        P("date", "rg"),
    )
    out_specs = P("date", None, "az", "rg")
    return jax.shard_map(
        on_device, mesh=mesh, in_specs=in_specs, out_specs=out_specs, check_vma=False
    )
```
